32 devices in a mesh: gx: 8 (over y, x, core), gy: 4 (over z).
Axes of the slice: x: 2, y: 2, z: 4, core: 2. Of those that a mesh axis runs over, the one named last changes fastest.
Arguments:
- offsets: float32 [3, 32, 32, 256], P(None, 'gx', 'gy'), may hold values from -0.5 to 0.5
- strengths: float32 [3, 32, 32, 256], P(None, 'gx', 'gy'), may hold values from -6 to 6
- counts: int32 [32, 32, 2], P('gx', 'gy'), may hold values from 64 to 128, as said below
- check_inverse: float32 [121, 121], replicated, may hold values from -1 to 1
Outputs:
- field: float32 [12, 32, 32, 256], P(None, 'gx', 'gy')
The draws below stay inside these ranges and needn't reach their ends.
Inputs may be any that keep to these rules, and one draw needn't show every extreme that they name: `counts`: A leaf's live particles fill its first slots; in each block of 4 x 8 x 2 leaves that one device holds, one leaf is full.
All inputs are finite; a program needn't handle non-finite values.
Results may differ from the reference program's by a relative error of at most 0.0003.
Values sent between devices are 32-bit elements; how exact they have to be, the bound alone decides.
No kernel may reach another device: no remote copies, remote signals or barrier semaphores. Data moves between devices by JAX's collectives and lax.ppermute only.
A program may use at most 192 MiB of HBM per device.

```python
import math
import jax
import jax.numpy as jnp
from jax import lax

NEQ = 121
PER_LEAF = 128
BX = 4
BY = 8
BZ = 2
G_X = 32
G_Y = 32
TX = 16
TY = 16
TOPS = 256


def draw_counts(key, part):
    key = jax.random.fold_in(key, 5)
    count_key, pick_key = jax.random.split(key)
    filled = jax.random.randint(count_key, (G_X, G_Y, BZ), PER_LEAF // 2, PER_LEAF + 1)
    chosen = jax.random.randint(pick_key, (G_X // BX, G_Y // BY), 0, BX * BY * BZ)
    chosen = jnp.repeat(jnp.repeat(chosen, BX, axis=0), BY, axis=1)[:, :, None]
    x_index = jnp.arange(G_X)[:, None, None]
    y_index = jnp.arange(G_Y)[None, :, None]
    z_index = jnp.arange(BZ)[None, None, :]
    local_index = x_index % BX * (BY * BZ) + y_index % BY * BZ + z_index
    return jnp.where(local_index == chosen, PER_LEAF, filled).astype(jnp.int32)


def draw_check_inverse(key, part):
    key = jax.random.fold_in(key, 11)
    spread = 0.4 * jax.random.normal(key, (NEQ, NEQ), jnp.float32) / math.sqrt(NEQ)
    return (jnp.eye(NEQ, dtype=jnp.float32) + spread) * (3.0 / NEQ)


def shard_levels(key, shape, cuts, low, largest):
    level = 1.0
    for position, shards_of in cuts:
        draws = jax.random.uniform(jax.random.fold_in(jax.random.fold_in(key, 6), position), (shards_of,), jnp.float32, low / len(cuts), largest / len(cuts))
        level = level * jnp.repeat(jnp.exp(draws), shape[position] // shards_of).reshape((-1,) + (1,) * (len(shape) - 1 - position))
    return level


def scatter_about(own_key, shape, scale, limit, cuts=(), kind=jnp.bfloat16):
    drawn = jax.random.normal(own_key, shape, jnp.float32) * scale
    if len(cuts) > 0:
        drawn = shard_levels(own_key, shape, cuts, -0.22, 0.18) * drawn
    return jnp.clip(drawn, min=-limit, max=limit).astype(kind)


def setup_inputs(seed: int = 0) -> dict:
    arg_keys = jax.random.split(jax.random.key(seed), 5)
    return {
        "offsets": jnp.clip(jax.random.uniform(arg_keys[0], (3, G_X, G_Y, BZ * PER_LEAF), jnp.float32, -0.5, 0.5) * shard_levels(arg_keys[0], (3, G_X, G_Y, BZ * PER_LEAF), ((1, 8), (2, 4)), -0.4, 0.0), -0.5, 0.5),
        "strengths": scatter_about(arg_keys[1], (3, G_X, G_Y, BZ * PER_LEAF), 1.0, 6.0, ((1, 8), (2, 4)), jnp.float32),
        "counts": draw_counts(jax.random.fold_in(arg_keys[4], 71), 0),
        "check_inverse": draw_check_inverse(jax.random.fold_in(arg_keys[4], 71), 0),
    }


SMOOTH2 = 0.01
STRENGTH_SCALE = 0.03
GOLDEN = math.pi * (3.0 - math.sqrt(5.0))
HIGHEST = lax.Precision.HIGHEST

def sphere_points(amount):
    counter = jnp.arange(amount).astype(jnp.float32)
    height = 1.0 - (2.0 * counter + 1.0) / amount
    radius = jnp.sqrt(jnp.maximum(1.0 - height * height, 0.0))
    azimuth = counter * GOLDEN
    return jnp.stack([radius * jnp.cos(azimuth), radius * jnp.sin(azimuth), height])

def kernel_of(vector):
    return lax.rsqrt(lax.optimization_barrier(jnp.sum(vector * vector, axis=0)) + SMOOTH2)

def translation(displacement, target_radius, source_radius, points):
    offset = jnp.array(displacement, dtype=jnp.float32)
    vector = offset[:, None, None] + target_radius * points[:, :, None] - source_radius * points[:, None, :]
    return kernel_of(vector)

def child_tables(points, target_radius, source_radius, direction):
    tables = []
    for corner_x in range(2):
        for corner_y in range(2):
            for corner_z in range(2):
                displacement = [direction * (corner_x - 0.5), direction * (corner_y - 0.5), direction * (corner_z - 0.5)]
                tables.append(translation(displacement, target_radius, source_radius, points))
    return jnp.stack(tables)

def parent_near(counter, displacement):
    return (jnp.abs((counter + displacement) // 2 - counter // 2) <= 1).astype(jnp.float32)

def apply_inverse(matrix, operand):
    return jnp.dot(matrix, operand.reshape(operand.shape[0], -1), precision=HIGHEST).reshape(operand.shape)

def top_block(charges, source_x, source_y, target_x, target_y, within):
    gap_x = target_x[:, None] - source_x[None, :]
    gap_y = target_y[:, None] - source_y[None, :]
    distant_mask = ((jnp.abs(gap_x) >= 2) | (jnp.abs(gap_y) >= 2)).astype(jnp.float32)
    along_x = 1.8 * within[0][:, None, :, None] + 2.0 * gap_x.astype(jnp.float32)[None, :, None, :]
    along_y = 1.8 * within[1][:, None, :, None] + 2.0 * gap_y.astype(jnp.float32)[None, :, None, :]
    along_z = 1.8 * within[2][:, None, :, None]
    weight = lax.rsqrt(along_x * along_x + along_y * along_y + along_z * along_z + SMOOTH2) * distant_mask[None, :, None, :]
    return jnp.einsum('ktmb,mcb->kct', weight, charges, precision=HIGHEST)

def evaluate(target, local_eq, source_places, source_charge, points):
    size_x, size_y, depth = (target.shape[1], target.shape[2], target.shape[3])
    potential = jnp.zeros((3,) + target.shape[1:], jnp.float32)
    gradient = jnp.zeros((3, 3) + target.shape[1:], jnp.float32)
    for shift_x in range(-1, 2):
        for shift_y in range(-1, 2):
            for shift_z in range(-1, 2):
                source = source_places[:, 1 + shift_x:1 + shift_x + size_x, 1 + shift_y:1 + shift_y + size_y, 1 + shift_z:1 + shift_z + depth]
                weight = source_charge[:, 1 + shift_x:1 + shift_x + size_x, 1 + shift_y:1 + shift_y + size_y, 1 + shift_z:1 + shift_z + depth]
                offset = jnp.array([shift_x, shift_y, shift_z], dtype=jnp.float32)
                vector = target[..., :, None] - source[..., None, :] - offset[:, None, None, None, None, None]
                inverse = kernel_of(vector)
                weighted = inverse[None] * weight[..., None, :]
                potential = potential + lax.optimization_barrier(jnp.sum(weighted, axis=-1))
                gradient = gradient - lax.optimization_barrier(jnp.sum(vector[None] * (weighted * inverse[None] * inverse[None])[:, None], axis=-1))
    vector = target[..., None] - 1.5 * points[:, None, None, None, None, :]
    inverse = kernel_of(vector)
    weighted = inverse[None] * jnp.moveaxis(local_eq, 0, -1)[..., None, :]
    potential = potential + lax.optimization_barrier(jnp.sum(weighted, axis=-1))
    gradient = gradient - lax.optimization_barrier(jnp.sum(vector[None] * (weighted * inverse[None] * inverse[None])[:, None], axis=-1))
    return jnp.concatenate([potential, gradient.reshape((9,) + target.shape[1:])], axis=0)

def reference(offsets, strengths, counts, check_inverse):
    points = sphere_points(NEQ)
    within = points[:, :, None] - points[:, None, :]
    slot_index = jnp.arange(PER_LEAF).astype(jnp.int32)
    living = (slot_index[None, None, None, :] < counts[:, :, :, None]).astype(jnp.float32)
    places = offsets.reshape(3, G_X, G_Y, BZ, PER_LEAF)
    charge = STRENGTH_SCALE * strengths.reshape(3, G_X, G_Y, BZ, PER_LEAF) * living[None]

    def upward_row(element):
        row_places, row_charge = element
        vector = 1.5 * points[:, :, None, None, None] - row_places[:, None]
        return jnp.einsum('kyzp,cyzp->kcyz', kernel_of(vector), row_charge, precision=HIGHEST)
    upward = lax.map(upward_row, (jnp.moveaxis(places, 1, 0), jnp.moveaxis(charge, 1, 0)))
    upward = jnp.moveaxis(upward, 0, 2)
    leaf_charges = 0.5 * apply_inverse(check_inverse, upward)
    grouped = leaf_charges.reshape(NEQ, 3, TX, 2, TY, 2, 2).transpose(3, 5, 6, 0, 1, 2, 4).reshape(8, NEQ, 3 * TOPS)
    top_check = jnp.einsum('ckm,cmt->kt', child_tables(points, 3.0, 0.9, -1.0), grouped, precision=HIGHEST)
    top_charges = apply_inverse(check_inverse, top_check.reshape(NEQ, 3, TOPS))
    top_x = jnp.arange(TOPS).astype(jnp.int32) // TY
    top_y = jnp.arange(TOPS).astype(jnp.int32) % TY

    def top_target(target_index):
        single_x = lax.dynamic_slice_in_dim(top_x, target_index, 1)
        single_y = lax.dynamic_slice_in_dim(top_y, target_index, 1)
        return top_block(top_charges, top_x, top_y, single_x, single_y, within)[:, :, 0]
    top_down = jnp.moveaxis(lax.map(top_target, jnp.arange(TOPS).astype(jnp.int32)), 0, 2)
    top_local = apply_inverse(check_inverse, top_down)
    spread = jnp.einsum('ckm,mt->ckt', child_tables(points, 0.9, 3.0, 1.0), top_local.reshape(NEQ, -1), precision=HIGHEST)
    inherited = spread.reshape(2, 2, 2, NEQ, 3, TX, TY).transpose(3, 4, 5, 0, 6, 1, 2).reshape(NEQ, 3, G_X, G_Y, BZ)
    padded = jnp.pad(leaf_charges, ((0, 0), (0, 0), (3, 3), (3, 3), (1, 1)))
    grid_x = jnp.arange(G_X).astype(jnp.int32)
    grid_y = jnp.arange(G_Y).astype(jnp.int32)
    distant = jnp.zeros((NEQ, 3 * G_X * G_Y * BZ), jnp.float32)
    for shift_x in range(-3, 4):
        for shift_y in range(-3, 4):
            if abs(shift_x) < 2 and abs(shift_y) < 2:
                continue
            parent_mask = parent_near(grid_x, shift_x)[:, None, None] * parent_near(grid_y, shift_y)[None, :, None]
            for shift_z in range(-1, 2):
                operator = translation([-shift_x, -shift_y, -shift_z], 0.9, 0.9, points)
                source = padded[:, :, 3 + shift_x:3 + shift_x + G_X, 3 + shift_y:3 + shift_y + G_Y, 1 + shift_z:1 + shift_z + BZ] * parent_mask
                distant = distant + jnp.dot(operator, source.reshape(NEQ, -1), precision=HIGHEST)
    leaf_down = distant.reshape(NEQ, 3, G_X, G_Y, BZ) + inherited
    leaf_local = 0.5 * apply_inverse(check_inverse, leaf_down)
    pad_places = jnp.pad(places, ((0, 0), (1, 1), (1, 1), (1, 1), (0, 0)))
    pad_charge = jnp.pad(charge, ((0, 0), (1, 1), (1, 1), (1, 1), (0, 0)))

    def field_row(row_index):
        target = lax.dynamic_slice_in_dim(places, row_index, 1, 1)
        local_eq = lax.dynamic_slice_in_dim(leaf_local, row_index, 1, 2)
        near_places = lax.dynamic_slice_in_dim(pad_places, row_index, 3, 1)
        near_charge = lax.dynamic_slice_in_dim(pad_charge, row_index, 3, 1)
        return evaluate(target, local_eq, near_places, near_charge, points)[:, 0]
    result_field = jnp.moveaxis(lax.map(field_row, jnp.arange(G_X).astype(jnp.int32)), 0, 1)
    result_field = result_field * living[None]
    return result_field.reshape(12, G_X, G_Y, BZ * PER_LEAF)
```

```python
import functools
import math

import jax
import jax.numpy as jnp
import numpy as np
from jax import lax
from jax.experimental import pallas as pl
from jax.experimental.pallas import tpu as pltpu
from jax.sharding import PartitionSpec as P

SMOOTH2 = 0.01
STRENGTH_SCALE = 0.03
LANES = 128
F32 = jnp.float32
BF16 = jnp.bfloat16
HIGHEST = lax.Precision.HIGHEST


def sphere_points(amount):
    counter = np.arange(amount, dtype=np.float32)
    height = (1.0 - (2.0 * counter + 1.0) / np.float32(amount)).astype(np.float32)
    radius = np.sqrt(np.maximum(1.0 - height * height, 0.0)).astype(np.float32)
    azimuth = counter * np.float32(math.pi * (3.0 - math.sqrt(5.0)))
    points = np.zeros((3, LANES), np.float32)
    points[:, :amount] = np.stack([radius * np.cos(azimuth), radius * np.sin(azimuth), height])
    return points


def split(value):
    high = value.astype(BF16)
    return high, (value - high.astype(F32)).astype(BF16)


def bdot(left, right):
    return jnp.dot(left, right, preferred_element_type=F32)


def dot_nt(left, right):
    return lax.dot_general(
        left, right, (((1,), (1,)), ((), ())), precision=HIGHEST, preferred_element_type=F32
    )


def two_terms(high, low):
    return jnp.concatenate(
        [
            jnp.concatenate([high, high], axis=1),
            jnp.concatenate([low, jnp.zeros_like(low)], axis=1),
        ],
        axis=0,
    )


def cubes(dx, dy, dz):
    inverse = lax.rsqrt(dx * dx + dy * dy + dz * dz + SMOOTH2)
    return inverse * inverse * inverse


def up_kernel(size_x, size_y, pack_ref, rows_ref, cols_ref, inverse_ref, leaf_ref, top_ref, check):
    point = [rows_ref[j : j + 1, :] for j in range(3)]

    def column(index, carry):
        i = index // size_y
        j = index % size_y
        row = [pack_ref[c, i, pl.ds(j, 1), :] for c in range(6)]
        for half in range(2):
            lanes = slice(half * LANES, (half + 1) * LANES)
            delta = []
            for axis in range(3):
                source = jnp.broadcast_to(row[axis][:, lanes], (LANES, LANES)).T
                delta.append(1.5 * point[axis] - source)
            kernel = lax.rsqrt(
                delta[0] * delta[0] + delta[1] * delta[1] + delta[2] * delta[2] + SMOOTH2
            )
            charge = jnp.concatenate(
                [row[3 + c][:, lanes] for c in range(3)] + [jnp.zeros((5, LANES), F32)], axis=0
            )
            c_high, c_low = split(charge)
            k_high, k_low = split(kernel)
            total = bdot(
                two_terms(
                    jnp.concatenate([c_high, c_low], axis=0),
                    jnp.zeros((16, LANES), BF16),
                )[:16],
                jnp.concatenate([k_high, k_low], axis=0),
            )
            total = total[:8] + total[8:]
            for c in range(3):
                check[half, c, i, pl.ds(j, 1), :] = total[c : c + 1]
        return carry

    lax.fori_loop(0, size_x * size_y, column, 0)
    matrix = inverse_ref[...]
    rows = 6 * size_x * size_y
    charges = 0.5 * dot_nt(check[...].reshape(rows, LANES), matrix)
    leaf_ref[...] = charges.reshape(2, 3, size_x, size_y, LANES)
    half_x = size_x // 2
    half_y = size_y // 2
    total = jnp.zeros((3 * half_x * half_y, LANES), F32)
    for a in range(2):
        for b in range(2):
            for e in range(2):
                shift = (a - 0.5, b - 0.5, e - 0.5)
                delta = [
                    3.0 * point[axis] - shift[axis] - 0.9 * cols_ref[axis] for axis in range(3)
                ]
                table = lax.rsqrt(
                    delta[0] * delta[0] + delta[1] * delta[1] + delta[2] * delta[2] + SMOOTH2
                )
                pieces = [
                    leaf_ref[e, c, 2 * x + a, pl.ds(b, half_y, stride=2), :]
                    for c in range(3)
                    for x in range(half_x)
                ]
                total = total + jnp.dot(
                    jnp.concatenate(pieces, axis=0),
                    table,
                    precision=HIGHEST,
                    preferred_element_type=F32,
                )
    top_ref[...] = dot_nt(total, matrix)


def near_kernel(size_x, size_y, ext_ref, out_ref, spread, moments):
    ext_y = size_y + 2
    lane = lax.broadcasted_iota(jnp.int32, (1, 2 * LANES), 1)
    lift = jnp.where(lane < LANES, -0.5, 0.5).astype(F32)

    def prepare(index, carry):
        i = index // ext_y
        j = index % ext_y
        row = [ext_ref[c, i, pl.ds(j, 1), :] for c in range(6)]
        x, y, z = row[0], row[1], row[2] + lift
        for axis, value in enumerate((x, y, z)):
            for half in range(2):
                lanes = slice(half * LANES, (half + 1) * LANES)
                spread[index, axis, lanes, :] = jnp.broadcast_to(
                    value[:, lanes], (LANES, LANES)
                ).T
        zero = jnp.zeros_like(x)
        one = jnp.ones_like(x)

        def weighted(factors):
            return jnp.concatenate(
                [factor * row[3 + c] for factor in factors for c in range(3)] + [zero], axis=0
            )

        moments[index, 0] = weighted([one, x, y, z, x * x + y * y + z * z])
        moments[index, 1] = weighted([zero, one, zero, zero, 2.0 * x])
        moments[index, 2] = weighted([zero, zero, one, zero, 2.0 * y])
        moments[index, 3] = weighted([zero, zero, zero, zero, one])
        return carry

    lax.fori_loop(0, (size_x + 2) * ext_y, prepare, 0)

    def target(index, carry):
        i = index // size_y
        j = index % size_y
        row = [ext_ref[c, i + 1, pl.ds(j + 1, 1), :] for c in range(3)]
        total = jnp.zeros((32, 2 * LANES), F32)
        for shift_x in (-1, 0, 1):
            for shift_y in (-1, 0, 1):
                source = (i + 1 + shift_x) * ext_y + j + 1 + shift_y
                weight = moments[source, 0]
                if shift_x:
                    weight = weight + float(shift_x) * moments[source, 1]
                if shift_y:
                    weight = weight + float(shift_y) * moments[source, 2]
                if shift_x or shift_y:
                    weight = weight + float(shift_x**2 + shift_y**2) * moments[source, 3]
                w_high, w_low = split(weight)
                place = [row[0] - float(shift_x), row[1] - float(shift_y), row[2] + lift]
                for half in range(2):
                    part = slice(half * LANES, (half + 1) * LANES)
                    highs = []
                    lows = []
                    for side in range(2):
                        lanes = slice(side * LANES, (side + 1) * LANES)
                        delta = [
                            place[axis][:, lanes] - spread[source, axis, part, :]
                            for axis in range(3)
                        ]
                        high, low = split(cubes(*delta))
                        highs.append(high)
                        lows.append(low)
                    total = total + bdot(
                        two_terms(w_high[:, part], w_low[:, part]),
                        jnp.concatenate(
                            [jnp.concatenate(highs, axis=1), jnp.concatenate(lows, axis=1)],
                            axis=0,
                        ),
                    )
        out_ref[index] = total[:16] + total[16:]
        return carry

    lax.fori_loop(0, size_x * size_y, target, 0)


def far_kernel(
    size_x,
    size_y,
    tops_x,
    tops_y,
    scalar_ref,
    shift_ref,
    counts_ref,
    leaf_ref,
    tops_ref,
    near_ref,
    pack_ref,
    rows_ref,
    cols_ref,
    pattern_ref,
    inverse_ref,
    out_ref,
    base,
    windows,
    down,
    top_down,
    local,
):
    half_x = size_x // 2
    half_y = size_y // 2
    group = half_x * 4
    across = tops_x + half_x - 1
    along = tops_y + half_y - 1
    point = [rows_ref[j : j + 1, :] for j in range(3)]
    for axis in range(3):
        base[axis] = point[axis] - cols_ref[axis]

    windows[...] = jnp.zeros_like(windows)

    def place(index, carry):
        i = index // tops_y
        j = index % tops_y
        device = (i // half_x) * (tops_y // half_y) + j // half_y
        inside = (i % half_x) * half_y + j % half_y
        for c in range(3):
            row = tops_ref[device, pl.ds(c * half_x * half_y + inside, 1), :]
            for x in range(half_x):
                windows[
                    i + half_x - 1 - x, pl.ds((j + half_y - 1) * group + x * 4 + c, 1), :
                ] = row
        return carry

    lax.fori_loop(0, tops_x * tops_y, place, 0)
    first_x = scalar_ref[0]
    first_y = scalar_ref[1]
    top_down[...] = jnp.zeros_like(top_down)

    def top_row(wx, carry):
        gap_x = first_x - (wx - (half_x - 1))
        dx = 1.8 * base[0] + 2.0 * gap_x.astype(F32)
        dz = 1.8 * base[2]
        squares = dx * dx + dz * dz + SMOOTH2

        def top_step(wy, inner):
            gap_y = first_y - (wy - (half_y - 1))
            distant = (jnp.abs(gap_x) >= 2) | (jnp.abs(gap_y) >= 2)
            dy = 1.8 * base[1] + 2.0 * gap_y.astype(F32)
            table = lax.rsqrt(squares + dy * dy)
            t_high, t_low = split(table)
            rows = windows[wx, pl.ds(wy * group, half_y * group), :]
            rows = jnp.where(distant, rows, 0.0)
            r_high, r_low = split(rows)
            both = bdot(jnp.concatenate([r_high, r_low], axis=0), t_high)
            top_down[...] += both[: half_y * group] + both[half_y * group :] + bdot(r_high, t_low)
            return inner

        return lax.fori_loop(0, along, top_step, carry)

    lax.fori_loop(0, across, top_row, 0)
    matrix = inverse_ref[...]
    top_local = dot_nt(top_down[...], matrix)

    down[...] = jnp.zeros_like(down)
    odd_y = lax.broadcasted_iota(jnp.int32, (size_y, LANES), 0) % 2

    def leaf_step(step, carry):
        shift_x = shift_ref[2 * step]
        shift_y = shift_ref[2 * step + 1]
        dx = 0.9 * base[0] - shift_x.astype(F32)
        dy = 0.9 * base[1] - shift_y.astype(F32)
        flat = dx * dx + dy * dy + SMOOTH2
        tables = []
        for shift_z in (-1, 0, 1):
            dz = 0.9 * base[2] - float(shift_z)
            tables.append(split(lax.rsqrt(flat + dz * dz)))
        wide = [
            jnp.concatenate(
                [
                    jnp.concatenate([tables[1][t], tables[0][t]], axis=1),
                    jnp.concatenate([tables[2][t], tables[1][t]], axis=1),
                ],
                axis=0,
            )
            for t in range(2)
        ]
        near_y = jnp.where(
            ((shift_y > -3) | (odd_y == 1)) & ((shift_y < 3) | (odd_y == 0)), 1.0, 0.0
        )
        highs = []
        lows = []
        for depth in range(2):
            pieces = []
            for c in range(3):
                for x in range(size_x):
                    near_x = (shift_x > -3) if x % 2 == 0 else (shift_x < 3)
                    pieces.append(
                        leaf_ref[depth, c, x + 3 + shift_x, pl.ds(3 + shift_y, size_y), :]
                        * jnp.where(near_x, near_y, 0.0)
                    )
            high, low = split(jnp.concatenate(pieces, axis=0))
            highs.append(high)
            lows.append(low)
        high = jnp.concatenate(highs, axis=1)
        low = jnp.concatenate(lows, axis=1)
        down[...] += bdot(high, wide[0]) + bdot(low, wide[0]) + bdot(high, wide[1])
        return carry

    lax.fori_loop(0, shift_ref.shape[0] // 2, leaf_step, 0)

    for a in range(2):
        for b in range(2):
            for e in range(2):
                offset = (a - 0.5, b - 0.5, e - 0.5)
                delta = [
                    offset[axis] + 0.9 * point[axis] - 3.0 * cols_ref[axis] for axis in range(3)
                ]
                table = lax.rsqrt(
                    delta[0] * delta[0] + delta[1] * delta[1] + delta[2] * delta[2] + SMOOTH2
                )
                inherited = jnp.dot(
                    top_local, table, precision=HIGHEST, preferred_element_type=F32
                )
                for y in range(half_y):
                    for x in range(half_x):
                        for c in range(3):
                            row = (c * size_x + 2 * x + a) * size_y + 2 * y + b
                            down[row : row + 1, e * LANES : (e + 1) * LANES] += inherited[
                                y * group + x * 4 + c : y * group + x * 4 + c + 1
                            ]
    for e in range(2):
        part = 0.5 * dot_nt(down[:, e * LANES : (e + 1) * LANES], matrix)
        local[e] = part.reshape(3, size_x, size_y, LANES)

    lane = lax.broadcasted_iota(jnp.int32, (1, LANES), 1)

    def column(index, carry):
        i = index // size_y
        j = index % size_y
        row = [pack_ref[c, i, pl.ds(j, 1), :] for c in range(3)]
        results = []
        for half in range(2):
            lanes = slice(half * LANES, (half + 1) * LANES)
            place = [row[axis][:, lanes] for axis in range(3)]
            delta = [place[axis] - 1.5 * cols_ref[axis] for axis in range(3)]
            high, low = split(cubes(*delta))
            charge = jnp.concatenate(
                [local[half, c, i, pl.ds(j, 1), :] for c in range(3)], axis=0
            )
            weight = pattern_ref[half] * jnp.concatenate(
                [charge] * 5 + [jnp.zeros((1, LANES), F32)], axis=0
            )
            total = bdot(two_terms(*split(weight)), jnp.concatenate([high, low], axis=0))
            total = total[:16] + total[16:] + near_ref[index, :, lanes]
            place[2] = place[2] + (half - 0.5)
            living = jnp.where(lane < counts_ref[2 * index + half], 1.0, 0.0)
            square = (
                place[0] * place[0] + place[1] * place[1] + place[2] * place[2] + SMOOTH2
            )
            potential = (
                square * total[0:3]
                - 2.0
                * (place[0] * total[3:6] + place[1] * total[6:9] + place[2] * total[9:12])
                + total[12:15]
            ) * living
            slopes = [
                (total[3 + 3 * axis : 6 + 3 * axis] - place[axis] * total[0:3]) * living
                for axis in range(3)
            ]
            results.append((potential, slopes))
        potential = jnp.concatenate([results[0][0], results[1][0]], axis=1)
        slopes = [
            jnp.concatenate([results[0][1][axis], results[1][1][axis]], axis=1)
            for axis in range(3)
        ]
        for c in range(3):
            out_ref[c, i, pl.ds(j, 1), :] = potential[c : c + 1]
            for axis in range(3):
                out_ref[3 + 3 * c + axis, i, pl.ds(j, 1), :] = slopes[axis][c : c + 1]
        return carry

    lax.fori_loop(0, size_x * size_y, column, 0)


def extended(cells, sides):
    for axis, dim, width in sides:
        count = lax.axis_size(axis)
        head = lax.slice_in_dim(cells, 0, width, axis=dim)
        tail = lax.slice_in_dim(cells, cells.shape[dim] - width, cells.shape[dim], axis=dim)
        cells = jnp.concatenate(
            [
                lax.ppermute(tail, axis, [(i, i + 1) for i in range(count - 1)]),
                cells,
                lax.ppermute(head, axis, [(i + 1, i) for i in range(count - 1)]),
            ],
            axis=dim,
        )
    return cells


def body(offsets, strengths, counts, check_inverse):
    size_x, size_y, depth = counts.shape
    expansion = check_inverse.shape[0]
    half_x = size_x // 2
    half_y = size_y // 2
    lanes_x = lax.axis_size("gx")
    lanes_y = lax.axis_size("gy")
    tops_x = lanes_x * half_x
    tops_y = lanes_y * half_y
    points = sphere_points(expansion)
    rows = jnp.asarray(np.concatenate([points, np.zeros((5, LANES), np.float32)], axis=0))
    cols = jnp.asarray(np.repeat(points[:, :, None], LANES, axis=2))
    patterns = np.zeros((2, 16, LANES), np.float32)
    for half in range(2):
        lifted = (1.5 * points).astype(np.float32)
        lifted[2] += half - 0.5
        factors = [np.ones(LANES), *lifted, np.sum(lifted.astype(np.float64) ** 2, axis=0)]
        for k in range(5):
            patterns[half, 3 * k : 3 * k + 3, :] = factors[k]
    patterns = jnp.asarray(patterns)
    pad = LANES - expansion
    matrix = jnp.pad(check_inverse, ((0, pad), (0, pad)))
    slot = jnp.arange(LANES)
    living = (slot < counts[:, :, :, None]).astype(F32).reshape(1, size_x, size_y, depth * LANES)
    pack = jnp.concatenate([offsets, STRENGTH_SCALE * strengths * living], axis=0)

    params = pltpu.CompilerParams(vmem_limit_bytes=58 * 2**20)
    leaf_charges, top_charges = pl.pallas_call(
        functools.partial(up_kernel, size_x, size_y),
        out_shape=(
            jax.ShapeDtypeStruct((2, 3, size_x, size_y, LANES), F32),
            jax.ShapeDtypeStruct((3 * half_x * half_y, LANES), F32),
        ),
        scratch_shapes=[pltpu.VMEM((2, 3, size_x, size_y, LANES), F32)],
        compiler_params=params,
        cost_estimate=pl.CostEstimate(flops=10**9, bytes_accessed=10**6, transcendentals=0),
        name="up",
    )(pack, rows, cols, matrix)

    neighbours = extended(pack, (("gx", 1, 1), ("gy", 2, 1)))
    border = extended(leaf_charges, (("gx", 2, 3), ("gy", 3, 3)))
    gathered = lax.all_gather(top_charges, ("gx", "gy"), axis=0)

    near = pl.pallas_call(
        functools.partial(near_kernel, size_x, size_y),
        out_shape=jax.ShapeDtypeStruct((size_x * size_y, 16, 2 * LANES), F32),
        scratch_shapes=[
            pltpu.VMEM(((size_x + 2) * (size_y + 2), 3, 2 * LANES, LANES), F32),
            pltpu.VMEM(((size_x + 2) * (size_y + 2), 4, 16, 2 * LANES), F32),
        ],
        compiler_params=params,
        cost_estimate=pl.CostEstimate(flops=4 * 10**10, bytes_accessed=10**6, transcendentals=0),
        name="near",
    )(neighbours)

    shifts = np.array(
        [
            (x, y)
            for x in range(-3, 4)
            for y in range(-3, 4)
            if abs(x) >= 2 or abs(y) >= 2
        ],
        np.int32,
    ).reshape(-1)
    first = jnp.stack([lax.axis_index("gx") * half_x, lax.axis_index("gy") * half_y])
    across = tops_x + half_x - 1
    along = tops_y + 2 * half_y - 2
    smem = pl.BlockSpec(memory_space=pltpu.SMEM)
    vmem = pl.BlockSpec(memory_space=pltpu.VMEM)
    return pl.pallas_call(
        functools.partial(far_kernel, size_x, size_y, tops_x, tops_y),
        out_shape=jax.ShapeDtypeStruct((12, size_x, size_y, depth * LANES), F32),
        in_specs=[smem] * 3 + [vmem] * 8,
        out_specs=vmem,
        scratch_shapes=[
            pltpu.VMEM((3, LANES, LANES), F32),
            pltpu.VMEM((across, along * half_x * 4, LANES), F32),
            pltpu.VMEM((3 * size_x * size_y, 2 * LANES), F32),
            pltpu.VMEM((half_y * half_x * 4, LANES), F32),
            pltpu.VMEM((2, 3, size_x, size_y, LANES), F32),
        ],
        compiler_params=params,
        cost_estimate=pl.CostEstimate(flops=10**10, bytes_accessed=10**6, transcendentals=0),
        name="far",
    )(
        first.astype(jnp.int32),
        jnp.asarray(shifts),
        counts.reshape(-1),
        border,
        gathered,
        near,
        pack,
        rows,
        cols,
        patterns,
        matrix,
    )


def solution(mesh):
    return jax.shard_map(
        body,
        mesh=mesh,
        in_specs=(P(None, "gx", "gy", None), P(None, "gx", "gy", None), P("gx", "gy", None), P()),
        out_specs=P(None, "gx", "gy", None),
        check_vma=False,
    )
```

```python
import functools
import math

import jax
import jax.numpy as jnp
import numpy as np
from jax import lax
from jax.experimental import pallas as pl
from jax.experimental.pallas import tpu as pltpu
from jax.sharding import PartitionSpec as P

SMOOTH2 = 0.01
STRENGTH_SCALE = 0.03
LANES = 128
F32 = jnp.float32
BF16 = jnp.bfloat16
HIGHEST = lax.Precision.HIGHEST


def sphere_points(amount):
    counter = np.arange(amount, dtype=np.float32)
    height = (1.0 - (2.0 * counter + 1.0) / np.float32(amount)).astype(np.float32)
    radius = np.sqrt(np.maximum(1.0 - height * height, 0.0)).astype(np.float32)
    azimuth = counter * np.float32(math.pi * (3.0 - math.sqrt(5.0)))
    points = np.zeros((3, LANES), np.float32)
    points[:, :amount] = np.stack([radius * np.cos(azimuth), radius * np.sin(azimuth), height])
    return points


def split(value):
    high = value.astype(BF16)
    return high, (value - high.astype(F32)).astype(BF16)


def bdot(left, right):
    return jnp.dot(left, right, preferred_element_type=F32)


def dot_nt(left, right):
    return lax.dot_general(
        left, right, (((1,), (1,)), ((), ())), precision=HIGHEST, preferred_element_type=F32
    )


def two_terms(high, low):
    return jnp.concatenate(
        [
            jnp.concatenate([high, high], axis=1),
            jnp.concatenate([low, jnp.zeros_like(low)], axis=1),
        ],
        axis=0,
    )


def cubes(dx, dy, dz):
    inverse = lax.rsqrt(dx * dx + dy * dy + dz * dz + SMOOTH2)
    return inverse * inverse * inverse


def up_kernel(size_x, size_y, pack_ref, rows_ref, cols_ref, inverse_ref, leaf_ref, top_ref, check):
    point = [rows_ref[j : j + 1, :] for j in range(3)]

    def one_column(i, j):
        row = [pack_ref[c, i, pl.ds(j, 1), :] for c in range(6)]
        charge = jnp.concatenate(row[3:] + [jnp.zeros((5, 2 * LANES), F32)], axis=0)
        for half in range(2):
            lanes = slice(half * LANES, (half + 1) * LANES)
            delta = [1.5 * cols_ref[axis] - row[axis][:, lanes] for axis in range(3)]
            kernel = lax.rsqrt(
                delta[0] * delta[0] + delta[1] * delta[1] + delta[2] * delta[2] + SMOOTH2
            )
            high, low = split(charge[:, lanes])
            both = jnp.concatenate([high, low], axis=0)
            first = jnp.concatenate([both, both], axis=1)
            total = lax.dot_general(
                first,
                jnp.concatenate(split(kernel), axis=1),
                (((1,), (1,)), ((), ())),
                preferred_element_type=F32,
            )
            total = total[:8] + total[8:]
            for c in range(3):
                check[half, c, i, pl.ds(j, 1), :] = total[c : c + 1]

    def columns(index, carry):
        for k in range(4):
            step = index * 4 + k
            one_column(step // size_y, step % size_y)
        return carry

    lax.fori_loop(0, size_x * size_y // 4, columns, 0)
    matrix = inverse_ref[...]
    rows = 6 * size_x * size_y
    charges = 0.5 * dot_nt(check[...].reshape(rows, LANES), matrix)
    leaf_ref[...] = charges.reshape(2, 3, size_x, size_y, LANES)
    half_x = size_x // 2
    half_y = size_y // 2
    total = jnp.zeros((3 * half_x * half_y, LANES), F32)
    for a in range(2):
        for b in range(2):
            for e in range(2):
                shift = (a - 0.5, b - 0.5, e - 0.5)
                delta = [
                    3.0 * point[axis] - shift[axis] - 0.9 * cols_ref[axis] for axis in range(3)
                ]
                table = lax.rsqrt(
                    delta[0] * delta[0] + delta[1] * delta[1] + delta[2] * delta[2] + SMOOTH2
                )
                pieces = [
                    leaf_ref[e, c, 2 * x + a, pl.ds(b, half_y, stride=2), :]
                    for c in range(3)
                    for x in range(half_x)
                ]
                total = total + jnp.dot(
                    jnp.concatenate(pieces, axis=0),
                    table,
                    precision=HIGHEST,
                    preferred_element_type=F32,
                )
    top_ref[...] = dot_nt(total, matrix)


def near_kernel(size_x, size_y, ext_ref, out_ref, spread, moments):
    ext_y = size_y + 2
    lane = lax.broadcasted_iota(jnp.int32, (1, 2 * LANES), 1)
    lift = jnp.where(lane < LANES, -0.5, 0.5).astype(F32)
    wide_row = lax.broadcasted_iota(jnp.int32, (16, 2 * LANES), 0)
    level = wide_row // 3
    kind = wide_row % 3

    def prepare(index, carry):
        i = index // ext_y
        j = index % ext_y
        row = [ext_ref[c, i, pl.ds(j, 1), :] for c in range(6)]
        x, y, z = row[0], row[1], row[2] + lift
        for axis, value in enumerate((x, y, z)):
            for half in range(2):
                lanes = slice(half * LANES, (half + 1) * LANES)
                spread[index, axis, lanes, :] = jnp.broadcast_to(
                    value[:, lanes], (LANES, LANES)
                ).T
        wide = (16, 2 * LANES)
        charge = jnp.where(
            kind == 0,
            jnp.broadcast_to(row[3], wide),
            jnp.where(kind == 1, jnp.broadcast_to(row[4], wide), jnp.broadcast_to(row[5], wide)),
        )
        charge = jnp.where(level < 5, charge, 0.0)
        square = x * x + y * y + z * z
        factor = jnp.where(
            level == 0,
            1.0,
            jnp.where(
                level == 1,
                jnp.broadcast_to(x, wide),
                jnp.where(
                    level == 2,
                    jnp.broadcast_to(y, wide),
                    jnp.where(
                        level == 3, jnp.broadcast_to(z, wide), jnp.broadcast_to(square, wide)
                    ),
                ),
            ),
        )
        moments[index, 0] = charge * factor
        moments[index, 1] = charge * jnp.where(
            level == 1, 1.0, jnp.where(level == 4, jnp.broadcast_to(2.0 * x, wide), 0.0)
        )
        moments[index, 2] = charge * jnp.where(
            level == 2, 1.0, jnp.where(level == 4, jnp.broadcast_to(2.0 * y, wide), 0.0)
        )
        moments[index, 3] = jnp.where(level == 4, charge, 0.0)
        return carry

    lax.fori_loop(0, (size_x + 2) * ext_y, prepare, 0, unroll=2)

    def target(index, carry):
        i = index // size_y
        j = index % size_y
        row = [ext_ref[c, i + 1, pl.ds(j + 1, 1), :] for c in range(3)]
        total = jnp.zeros((32, 2 * LANES), F32)
        for shift_x in (-1, 0, 1):
            for shift_y in (-1, 0, 1):
                source = (i + 1 + shift_x) * ext_y + j + 1 + shift_y
                weight = moments[source, 0]
                if shift_x:
                    weight = weight + float(shift_x) * moments[source, 1]
                if shift_y:
                    weight = weight + float(shift_y) * moments[source, 2]
                if shift_x or shift_y:
                    weight = weight + float(shift_x**2 + shift_y**2) * moments[source, 3]
                w_high, w_low = split(weight)
                place = [row[0] - float(shift_x), row[1] - float(shift_y), row[2] + lift]
                for half in range(2):
                    part = slice(half * LANES, (half + 1) * LANES)
                    highs = []
                    lows = []
                    for side in range(2):
                        lanes = slice(side * LANES, (side + 1) * LANES)
                        delta = [
                            place[axis][:, lanes] - spread[source, axis, part, :]
                            for axis in range(3)
                        ]
                        high, low = split(cubes(*delta))
                        highs.append(high)
                        lows.append(low)
                    total = total + bdot(
                        two_terms(w_high[:, part], w_low[:, part]),
                        jnp.concatenate(
                            [jnp.concatenate(highs, axis=1), jnp.concatenate(lows, axis=1)],
                            axis=0,
                        ),
                    )
        out_ref[index] = total[:16] + total[16:]
        return carry

    lax.fori_loop(0, size_x * size_y, target, 0)


def leaf_kernel(size_x, size_y, leaf_ref, rows_ref, cols_ref, down_ref, base):
    for axis in range(3):
        base[axis] = 0.9 * rows_ref[axis : axis + 1, :] - 0.9 * cols_ref[axis]
    down_ref[...] = jnp.zeros_like(down_ref)
    odd_y = lax.broadcasted_iota(jnp.int32, (size_y, LANES), 0) % 2
    near_y = {-3: jnp.where(odd_y == 1, 1.0, 0.0), 3: jnp.where(odd_y == 0, 1.0, 0.0)}

    def one_row(shift_x, shifts_y):
        dx = base[0] - shift_x.astype(F32)
        tables = []
        highs = []
        lows = []
        for shift_y in shifts_y:
            dy = base[1] - float(shift_y)
            flat = dx * dx + dy * dy + SMOOTH2
            table = []
            for shift_z in (-1, 0, 1):
                dz = base[2] - float(shift_z)
                table.append(lax.rsqrt(flat + dz * dz).astype(BF16))
            tables.append(jnp.concatenate([table[1], table[0]], axis=1))
            tables.append(jnp.concatenate([table[2], table[1]], axis=1))
            for depth in range(2):
                pieces = []
                for c in range(3):
                    for x in range(size_x):
                        near_x = (shift_x > -3) if x % 2 == 0 else (shift_x < 3)
                        piece = jnp.where(
                            near_x,
                            leaf_ref[depth, c, x + 3 + shift_x, 3 + shift_y : 3 + shift_y + size_y],
                            0.0,
                        )
                        if abs(shift_y) == 3:
                            piece = piece * near_y[shift_y]
                        pieces.append(piece)
                high, low = split(jnp.concatenate(pieces, axis=0))
                highs.append(high)
                lows.append(low)
        rows = 3 * size_x * size_y
        both = bdot(
            jnp.concatenate(
                [jnp.concatenate(highs, axis=1), jnp.concatenate(lows, axis=1)], axis=0
            ),
            jnp.concatenate(tables, axis=0),
        )
        down_ref[...] += both[:rows] + both[rows:]

    def outer(step, carry):
        one_row(jnp.where(step < 2, step - 3, step), (-3, -2, -1, 0, 1, 2, 3))
        return carry

    def inner(step, carry):
        one_row(step - 1, (-3, -2, 2, 3))
        return carry

    lax.fori_loop(0, 4, outer, 0)
    lax.fori_loop(0, 3, inner, 0)


def far_kernel(
    size_x,
    size_y,
    tops_x,
    tops_y,
    chunk,
    scalar_ref,
    counts_ref,
    down_ref,
    tops_ref,
    near_ref,
    pack_ref,
    rows_ref,
    cols_ref,
    pattern_ref,
    inverse_ref,
    out_ref,
    base,
    windows,
    down,
    top_down,
    local,
):
    half_x = size_x // 2
    half_y = size_y // 2
    group = half_x * 4
    across = tops_x + half_x - 1
    along = tops_y + half_y - 1
    point = [rows_ref[j : j + 1, :] for j in range(3)]
    for axis in range(3):
        base[axis] = 1.8 * point[axis] - 1.8 * cols_ref[axis]

    windows[...] = jnp.zeros_like(windows)
    mine = scalar_ref[2]
    lanes_y = tops_y // half_y

    def place(device, carry):
        slot = jnp.bitwise_xor(device, mine)
        i = (device // lanes_y) * half_x
        j = (device % lanes_y) * half_y
        for c in range(3):
            for p in range(half_x):
                for q in range(half_y):
                    row = tops_ref[slot, (c * half_x + p) * half_y + q, :][None]
                    for x in range(half_x):
                        windows[
                            i + p + half_x - 1 - x,
                            pl.ds((j + q + half_y - 1) * group + x * 4 + c, 1),
                            :,
                        ] = row
        return carry

    lax.fori_loop(0, tops_ref.shape[0], place, 0)
    first_x = scalar_ref[0]
    first_y = scalar_ref[1]
    top_down[...] = jnp.zeros_like(top_down)
    parts = -(-along // chunk)

    def top_row(step, carry):
        wx = step // parts
        start = (step % parts) * chunk
        gap_x = first_x - (wx - (half_x - 1))
        dx = base[0] + 2.0 * gap_x.astype(F32)
        squares = dx * dx + base[2] * base[2] + SMOOTH2
        tables = []
        pieces = []
        for k in range(chunk):
            wy = start + k
            gap_y = first_y - (wy - (half_y - 1))
            distant = (jnp.abs(gap_x) >= 2) | (jnp.abs(gap_y) >= 2)
            dy = base[1] + 2.0 * gap_y.astype(F32)
            tables.append(lax.rsqrt(squares + dy * dy).astype(BF16))
            rows = windows[wx, pl.ds(wy * group, half_y * group), :]
            pieces.append(jnp.where(distant, rows, 0.0))
        high, low = split(jnp.concatenate(pieces, axis=1))
        top_down[...] += bdot(
            jnp.concatenate([high, low], axis=0), jnp.concatenate(tables, axis=0)
        )
        return carry

    lax.fori_loop(0, across * parts, top_row, 0)
    matrix = inverse_ref[...]
    rows = half_y * group
    top_local = dot_nt(top_down[:rows] + top_down[rows:], matrix)
    down[...] = down_ref[...]
    for a in range(2):
        for b in range(2):
            for e in range(2):
                offset = (a - 0.5, b - 0.5, e - 0.5)
                delta = [
                    offset[axis] + 0.9 * point[axis] - 3.0 * cols_ref[axis] for axis in range(3)
                ]
                table = lax.rsqrt(
                    delta[0] * delta[0] + delta[1] * delta[1] + delta[2] * delta[2] + SMOOTH2
                )
                inherited = jnp.dot(
                    top_local, table, precision=HIGHEST, preferred_element_type=F32
                )
                for y in range(half_y):
                    for x in range(half_x):
                        for c in range(3):
                            row = (c * size_x + 2 * x + a) * size_y + 2 * y + b
                            down[row : row + 1, e * LANES : (e + 1) * LANES] += inherited[
                                y * group + x * 4 + c : y * group + x * 4 + c + 1
                            ]
    for e in range(2):
        part = 0.5 * dot_nt(down[:, e * LANES : (e + 1) * LANES], matrix)
        local[e] = part.reshape(3, size_x, size_y, LANES)

    lane = lax.broadcasted_iota(jnp.int32, (1, LANES), 1)

    def one_column(index):
        i = index // size_y
        j = index % size_y
        row = [pack_ref[c, i, pl.ds(j, 1), :] for c in range(3)]
        results = []
        for half in range(2):
            lanes = slice(half * LANES, (half + 1) * LANES)
            place = [row[axis][:, lanes] for axis in range(3)]
            delta = [place[axis] - 1.5 * cols_ref[axis] for axis in range(3)]
            high, low = split(cubes(*delta))
            charge = jnp.concatenate(
                [local[half, c, i, pl.ds(j, 1), :] for c in range(3)], axis=0
            )
            weight = pattern_ref[half] * jnp.concatenate(
                [charge] * 5 + [jnp.zeros((1, LANES), F32)], axis=0
            )
            total = bdot(two_terms(*split(weight)), jnp.concatenate([high, low], axis=0))
            total = total[:16] + total[16:] + near_ref[index, :, lanes]
            place[2] = place[2] + (half - 0.5)
            living = jnp.where(lane < counts_ref[2 * index + half], 1.0, 0.0)
            square = (
                place[0] * place[0] + place[1] * place[1] + place[2] * place[2] + SMOOTH2
            )
            potential = (
                square * total[0:3]
                - 2.0
                * (place[0] * total[3:6] + place[1] * total[6:9] + place[2] * total[9:12])
                + total[12:15]
            ) * living
            slopes = [
                (total[3 + 3 * axis : 6 + 3 * axis] - place[axis] * total[0:3]) * living
                for axis in range(3)
            ]
            results.append((potential, slopes))
        potential = jnp.concatenate([results[0][0], results[1][0]], axis=1)
        slopes = [
            jnp.concatenate([results[0][1][axis], results[1][1][axis]], axis=1)
            for axis in range(3)
        ]
        for c in range(3):
            out_ref[c, i, pl.ds(j, 1), :] = potential[c : c + 1]
            for axis in range(3):
                out_ref[3 + 3 * c + axis, i, pl.ds(j, 1), :] = slopes[axis][c : c + 1]

    def columns(index, carry):
        for k in range(4):
            one_column(index * 4 + k)
        return carry

    lax.fori_loop(0, size_x * size_y // 4, columns, 0)


def gathered(block):
    held = block[None]
    for axis in ("gy", "gx"):
        count = lax.axis_size(axis)
        bit = 1
        while bit < count:
            radix = 4 if bit * 4 <= count else 2
            received = [
                lax.ppermute(held, axis, [(i, i ^ (k * bit)) for i in range(count)])
                for k in range(1, radix)
            ]
            held = jnp.concatenate([held] + received, axis=0)
            bit *= radix
    return held


def extended(cells, sides):
    for axis, dim, width in sides:
        count = lax.axis_size(axis)
        head = lax.slice_in_dim(cells, 0, width, axis=dim)
        tail = lax.slice_in_dim(cells, cells.shape[dim] - width, cells.shape[dim], axis=dim)
        cells = jnp.concatenate(
            [
                lax.ppermute(tail, axis, [(i, i + 1) for i in range(count - 1)]),
                cells,
                lax.ppermute(head, axis, [(i + 1, i) for i in range(count - 1)]),
            ],
            axis=dim,
        )
    return cells


def body(offsets, strengths, counts, check_inverse):
    size_x, size_y, depth = counts.shape
    expansion = check_inverse.shape[0]
    half_x = size_x // 2
    half_y = size_y // 2
    lanes_x = lax.axis_size("gx")
    lanes_y = lax.axis_size("gy")
    tops_x = lanes_x * half_x
    tops_y = lanes_y * half_y
    points = sphere_points(expansion)
    rows = jnp.asarray(np.concatenate([points, np.zeros((5, LANES), np.float32)], axis=0))
    cols = jnp.asarray(np.repeat(points[:, :, None], LANES, axis=2))
    patterns = np.zeros((2, 16, LANES), np.float32)
    for half in range(2):
        lifted = (1.5 * points).astype(np.float32)
        lifted[2] += half - 0.5
        factors = [np.ones(LANES), *lifted, np.sum(lifted.astype(np.float64) ** 2, axis=0)]
        for k in range(5):
            patterns[half, 3 * k : 3 * k + 3, :] = factors[k]
    patterns = jnp.asarray(patterns)
    pad = LANES - expansion
    matrix = jnp.pad(check_inverse, ((0, pad), (0, pad)))
    slot = jnp.arange(LANES)
    living = (slot < counts[:, :, :, None]).astype(F32).reshape(1, size_x, size_y, depth * LANES)
    pack = jnp.concatenate([offsets, STRENGTH_SCALE * strengths * living], axis=0)

    params = pltpu.CompilerParams(vmem_limit_bytes=58 * 2**20)
    leaf_charges, top_charges = pl.pallas_call(
        functools.partial(up_kernel, size_x, size_y),
        out_shape=(
            jax.ShapeDtypeStruct((2, 3, size_x, size_y, LANES), F32),
            jax.ShapeDtypeStruct((3 * half_x * half_y, LANES), F32),
        ),
        scratch_shapes=[pltpu.VMEM((2, 3, size_x, size_y, LANES), F32)],
        compiler_params=params,
        cost_estimate=pl.CostEstimate(flops=10**9, bytes_accessed=10**6, transcendentals=0),
        name="up",
    )(pack, rows, cols, matrix)

    neighbours = extended(pack, (("gx", 1, 1), ("gy", 2, 1)))
    border = extended(leaf_charges, (("gx", 2, 3), ("gy", 3, 3)))
    tops = gathered(top_charges)

    near = pl.pallas_call(
        functools.partial(near_kernel, size_x, size_y),
        out_shape=jax.ShapeDtypeStruct((size_x * size_y, 16, 2 * LANES), F32),
        scratch_shapes=[
            pltpu.VMEM(((size_x + 2) * (size_y + 2), 3, 2 * LANES, LANES), F32),
            pltpu.VMEM(((size_x + 2) * (size_y + 2), 4, 16, 2 * LANES), F32),
        ],
        compiler_params=params,
        cost_estimate=pl.CostEstimate(flops=4 * 10**10, bytes_accessed=10**6, transcendentals=0),
        name="near",
    )(neighbours)

    down = pl.pallas_call(
        functools.partial(leaf_kernel, size_x, size_y),
        out_shape=jax.ShapeDtypeStruct((3 * size_x * size_y, 2 * LANES), F32),
        scratch_shapes=[pltpu.VMEM((3, LANES, LANES), F32)],
        compiler_params=params,
        cost_estimate=pl.CostEstimate(flops=6 * 10**9, bytes_accessed=10**6, transcendentals=0),
        name="leaf",
    )(border, rows, cols)

    gx = lax.axis_index("gx")
    gy = lax.axis_index("gy")
    scalars = jnp.stack([gx * half_x, gy * half_y, gx * lanes_y + gy]).astype(jnp.int32)
    across = tops_x + half_x - 1
    along = tops_y + half_y - 1
    parts = -(-along // 20)
    chunk = -(-along // parts)
    smem = pl.BlockSpec(memory_space=pltpu.SMEM)
    vmem = pl.BlockSpec(memory_space=pltpu.VMEM)
    return pl.pallas_call(
        functools.partial(far_kernel, size_x, size_y, tops_x, tops_y, chunk),
        out_shape=jax.ShapeDtypeStruct((12, size_x, size_y, depth * LANES), F32),
        in_specs=[smem] * 2 + [vmem] * 8,
        out_specs=vmem,
        scratch_shapes=[
            pltpu.VMEM((3, LANES, LANES), F32),
            pltpu.VMEM((across, (parts * chunk + half_y - 1) * half_x * 4, LANES), F32),
            pltpu.VMEM((3 * size_x * size_y, 2 * LANES), F32),
            pltpu.VMEM((2 * half_y * half_x * 4, LANES), F32),
            pltpu.VMEM((2, 3, size_x, size_y, LANES), F32),
        ],
        compiler_params=params,
        cost_estimate=pl.CostEstimate(flops=10**10, bytes_accessed=10**6, transcendentals=0),
        name="far",
    )(scalars, counts.reshape(-1), down, tops, near, pack, rows, cols, patterns, matrix)


def solution(mesh):
    return jax.shard_map(
        body,
        mesh=mesh,
        in_specs=(P(None, "gx", "gy", None), P(None, "gx", "gy", None), P("gx", "gy", None), P()),
        out_specs=P(None, "gx", "gy", None),
        check_vma=False,
    )
```

```python
import functools
import math

import jax
import jax.numpy as jnp
import numpy as np
from jax import lax
from jax.experimental import pallas as pl
from jax.experimental.pallas import tpu as pltpu
from jax.sharding import PartitionSpec as P

SMOOTH2 = 0.01
STRENGTH_SCALE = 0.03
LANES = 128
F32 = jnp.float32
BF16 = jnp.bfloat16
HIGHEST = lax.Precision.HIGHEST


def sphere_points(amount):
    counter = np.arange(amount, dtype=np.float32)
    height = (1.0 - (2.0 * counter + 1.0) / np.float32(amount)).astype(np.float32)
    radius = np.sqrt(np.maximum(1.0 - height * height, 0.0)).astype(np.float32)
    azimuth = counter * np.float32(math.pi * (3.0 - math.sqrt(5.0)))
    points = np.zeros((3, LANES), np.float32)
    points[:, :amount] = np.stack([radius * np.cos(azimuth), radius * np.sin(azimuth), height])
    return points


def split(value):
    high = value.astype(BF16)
    return high, (value - high.astype(F32)).astype(BF16)


def bdot(left, right):
    return jnp.dot(left, right, preferred_element_type=F32)


def dot_nt(left, right):
    return lax.dot_general(
        left, right, (((1,), (1,)), ((), ())), precision=HIGHEST, preferred_element_type=F32
    )


def two_terms(high, low):
    return jnp.concatenate(
        [
            jnp.concatenate([high, high], axis=1),
            jnp.concatenate([low, jnp.zeros_like(low)], axis=1),
        ],
        axis=0,
    )


def cubes(dx, dy, dz):
    inverse = lax.rsqrt(dx * dx + dy * dy + dz * dz + SMOOTH2)
    return inverse * inverse * inverse


SIDES = (-1, 1)
WIDTH = 3


def edge(side, size, width):
    return 0 if side < 0 else size - width


def landing(side, size, width):
    return 0 if side < 0 else size + width


def parcel_rows(size_x, size_y):
    tops = 3 * (size_x // 2) * (size_y // 2)
    leaves_x = 6 * WIDTH * size_y
    leaves_y = 6 * (size_x + 2 * WIDTH) * WIDTH
    near_x = leaves_x + 12 * size_y
    near_y = leaves_y + 12 * (size_x + 2)
    return (leaves_x, near_x, near_x + tops), (leaves_y, near_y, near_y + 3 * tops)


def lies_inside(axis, side):
    place = lax.axis_index(axis) + side
    return jnp.where((place >= 0) & (place < lax.axis_size(axis)), 1.0, 0.0)


def up_kernel(
    size_x,
    size_y,
    counts_ref,
    offsets_ref,
    strengths_ref,
    rows_ref,
    cols_ref,
    inverse_ref,
    pack_ref,
    leaf_ref,
    top_ref,
    matrix_ref,
    *rest,
):
    parcels = rest[:2]
    check = rest[2]
    point = [rows_ref[j : j + 1, :] for j in range(3)]
    lane = lax.broadcasted_iota(jnp.int32, (1, 2 * LANES), 1)
    expansion = inverse_ref.shape[0]
    matrix_ref[...] = jnp.zeros_like(matrix_ref)
    matrix_ref[:expansion, :expansion] = inverse_ref[...]
    pack_ref[0:3] = offsets_ref[...]

    def one_column(i, j):
        row = [offsets_ref[c, i, pl.ds(j, 1), :] for c in range(3)]
        last = jnp.where(lane < LANES, counts_ref[i, j, 0], counts_ref[i, j, 1] + LANES)
        charges = []
        for c in range(3):
            value = jnp.where(
                lane < last, STRENGTH_SCALE * strengths_ref[c, i, pl.ds(j, 1), :], 0.0
            )
            pack_ref[3 + c, i, pl.ds(j, 1), :] = value
            charges.append(value)
        charge = jnp.concatenate(charges + [jnp.zeros((5, 2 * LANES), F32)], axis=0)
        for half in range(2):
            lanes = slice(half * LANES, (half + 1) * LANES)
            delta = [1.5 * cols_ref[axis] - row[axis][:, lanes] for axis in range(3)]
            kernel = lax.rsqrt(
                delta[0] * delta[0] + delta[1] * delta[1] + delta[2] * delta[2] + SMOOTH2
            )
            both = jnp.concatenate(split(charge[:, lanes]), axis=0)
            total = lax.dot_general(
                jnp.concatenate([both, both], axis=1),
                jnp.concatenate(split(kernel), axis=1),
                (((1,), (1,)), ((), ())),
                preferred_element_type=F32,
            )
            total = total[:8] + total[8:]
            for c in range(3):
                check[half, c, i, pl.ds(j, 1), :] = total[c : c + 1]

    def columns(index, carry):
        for k in range(4):
            step = index * 4 + k
            one_column(step // size_y, step % size_y)
        return carry

    lax.fori_loop(0, size_x * size_y // 4, columns, 0)
    matrix = matrix_ref[...]
    rows = 6 * size_x * size_y
    charges = 0.5 * dot_nt(check[...].reshape(rows, LANES), matrix)
    leaf_ref[...] = charges.reshape(2, 3, size_x, size_y, LANES)
    half_x = size_x // 2
    half_y = size_y // 2
    total = jnp.zeros((3 * half_x * half_y, LANES), F32)
    for a in range(2):
        for b in range(2):
            for e in range(2):
                shift = (a - 0.5, b - 0.5, e - 0.5)
                delta = [
                    3.0 * point[axis] - shift[axis] - 0.9 * cols_ref[axis] for axis in range(3)
                ]
                table = lax.rsqrt(
                    delta[0] * delta[0] + delta[1] * delta[1] + delta[2] * delta[2] + SMOOTH2
                )
                pieces = [
                    leaf_ref[e, c, 2 * x + a, pl.ds(b, half_y, stride=2), :]
                    for c in range(3)
                    for x in range(half_x)
                ]
                total = total + jnp.dot(
                    jnp.concatenate(pieces, axis=0),
                    table,
                    precision=HIGHEST,
                    preferred_element_type=F32,
                )
    tops = dot_nt(total, matrix)
    top_ref[...] = tops
    (_, second, end), _ = parcel_rows(size_x, size_y)
    for side, parcel in zip(SIDES, parcels):
        row = 0
        start = edge(side, size_x, WIDTH)
        for depth in range(2):
            for c in range(3):
                for x in range(start, start + WIDTH):
                    parcel[row : row + size_y] = leaf_ref[depth, c, x]
                    row += size_y
        for c in range(6):
            for half in range(2):
                lanes = slice(half * LANES, (half + 1) * LANES)
                parcel[row : row + size_y] = pack_ref[c, edge(side, size_x, 1), :, lanes]
                row += size_y
        parcel[second:end] = tops


def turn_kernel(
    size_x, size_y, leaf_ref, pack_ref, top_ref, below_ref, above_ref, low_ref, high_ref, tops_ref
):
    (_, near_x, end_x), (_, near_y, _) = parcel_rows(size_x, size_y)
    count = end_x - near_x
    for place, ref in ((0, below_ref), (2, above_ref)):
        tops_ref[place * count : (place + 1) * count] = ref[near_x:end_x]
    tops_ref[count : 2 * count] = top_ref[...]
    inside = [lies_inside("gx", side) for side in SIDES]
    for side, parcel in zip(SIDES, (low_ref, high_ref)):
        row = 0
        start = edge(side, size_y, WIDTH)
        for depth in range(2):
            for c in range(3):
                for x in range(-WIDTH, size_x + WIDTH):
                    if 0 <= x < size_x:
                        value = leaf_ref[depth, c, x, start : start + WIDTH]
                    else:
                        which = int(x >= size_x)
                        ref = (below_ref, above_ref)[which]
                        cell = x - size_x if which else x + WIDTH
                        at = ((depth * 3 + c) * WIDTH + cell) * size_y + start
                        value = ref[at : at + WIDTH] * inside[which]
                    parcel[row : row + WIDTH] = value
                    row += WIDTH
        start = edge(side, size_y, 1)
        first, _, _ = parcel_rows(size_x, size_y)[0]
        for c in range(6):
            for x in range(-1, size_x + 1):
                for half in range(2):
                    if 0 <= x < size_x:
                        lanes = slice(half * LANES, (half + 1) * LANES)
                        value = pack_ref[c, x, start : start + 1, lanes]
                    else:
                        which = int(x >= size_x)
                        ref = (below_ref, above_ref)[which]
                        at = first + (c * 2 + half) * size_y + start
                        value = ref[at : at + 1]
                        if c >= 3:
                            value = value * inside[which]
                    parcel[row : row + 1] = value
                    row += 1
        parcel[near_y : near_y + 3 * count] = tops_ref[...]


def near_masks():
    row = lax.broadcasted_iota(jnp.int32, (16, 2 * LANES), 0)
    lane = lax.broadcasted_iota(jnp.int32, (1, 2 * LANES), 1)
    return row // 3, row % 3, jnp.where(lane < LANES, -0.5, 0.5).astype(F32)


def prepare_column(row, slot, masks, spread, moments):
    level, kind, lift = masks
    x, y, z = row[0], row[1], row[2] + lift
    square = x * x + y * y + z * z
    for axis, value in enumerate((-2.0 * x, -2.0 * y, -2.0 * z, square)):
        for half in range(2):
            lanes = slice(half * LANES, (half + 1) * LANES)
            spread[slot, axis, lanes, :] = jnp.broadcast_to(value[:, lanes], (LANES, LANES)).T

    def wide(value):
        return jnp.broadcast_to(value, (16, 2 * LANES))

    charge = jnp.where(
        kind == 0, wide(row[3]), jnp.where(kind == 1, wide(row[4]), wide(row[5]))
    )
    charge = jnp.where(level < 5, charge, 0.0)
    factor = jnp.where(level == 3, wide(z), wide(square))
    factor = jnp.where(level == 2, wide(y), factor)
    factor = jnp.where(level == 1, wide(x), factor)
    moments[slot, 0] = charge * jnp.where(level == 0, 1.0, factor)
    last = jnp.where(level == 4, charge, 0.0)
    moments[slot, 1] = jnp.where(level == 1, charge, last * wide(2.0 * x))
    moments[slot, 2] = jnp.where(level == 2, charge, last * wide(2.0 * y))
    moments[slot, 3] = last


def near_sums(target, blocks, spread, moments):
    total = jnp.zeros((32, 2 * LANES), F32)
    for slot, shift_x, shift_y in blocks:
        weight = (
            moments[slot, 0]
            + shift_x * moments[slot, 1]
            + shift_y * moments[slot, 2]
            + (shift_x * shift_x + shift_y * shift_y) * moments[slot, 3]
        )
        w_high, w_low = split(weight)
        x = target[0] - shift_x
        y = target[1] - shift_y
        z = target[2]
        square = x * x + y * y + z * z + SMOOTH2
        for half in range(2):
            part = slice(half * LANES, (half + 1) * LANES)
            highs = []
            lows = []
            for side in range(2):
                lanes = slice(side * LANES, (side + 1) * LANES)
                distance = (
                    (square[:, lanes] + spread[slot, 3, part, :])
                    + x[:, lanes] * spread[slot, 0, part, :]
                    + y[:, lanes] * spread[slot, 1, part, :]
                    + z[:, lanes] * spread[slot, 2, part, :]
                )
                inverse = lax.rsqrt(distance)
                high, low = split(inverse * inverse * inverse)
                highs.append(high)
                lows.append(low)
            total = total + bdot(
                two_terms(w_high[:, part], w_low[:, part]),
                jnp.concatenate(
                    [jnp.concatenate(highs, axis=1), jnp.concatenate(lows, axis=1)], axis=0
                ),
            )
    return total[:16] + total[16:]


def run_tasks(size_y, tasks, table_ref, pack_ref, out_ref, lift, spread, moments, adds):
    for start, amount, sources in tasks:
        together = 1
        while together * sources < 6 and amount % (2 * together) == 0:
            together *= 2

        def one(index, start, sources):
            at = start + index * (2 + 3 * sources)
            i = table_ref[at]
            j = table_ref[at + 1]
            target = [pack_ref[c, i, pl.ds(j, 1), :] for c in range(3)]
            target[2] = target[2] + lift
            blocks = [
                (
                    table_ref[at + 2 + 3 * k],
                    table_ref[at + 3 + 3 * k].astype(F32),
                    table_ref[at + 4 + 3 * k].astype(F32),
                )
                for k in range(sources)
            ]
            return i * size_y + j, near_sums(target, blocks, spread, moments)

        def step(index, carry, start=start, sources=sources, together=together):
            found = [one(index * together + k, start, sources) for k in range(together)]
            for place, total in found:
                out_ref[place] = total + out_ref[place] if adds else total
            return carry

        lax.fori_loop(0, amount // together, step, 0)


def own_kernel(size_x, size_y, tasks, table_ref, pack_ref, out_ref, spread, moments):
    masks = near_masks()

    def prepare(index, carry):
        for k in range(2):
            slot = index * 2 + k
            row = [pack_ref[c, slot // size_y, pl.ds(slot % size_y, 1), :] for c in range(6)]
            prepare_column(row, slot, masks, spread, moments)
        return carry

    lax.fori_loop(0, size_x * size_y // 2, prepare, 0)
    run_tasks(size_y, tasks, table_ref, pack_ref, out_ref, masks[2], spread, moments, False)


def halo_kernel(size_x, size_y, axis, tasks, table_ref, before_ref, pack_ref, *rest):
    parcels = rest[:2]
    out_ref, spread, moments, held = rest[2:]
    masks = near_masks()
    out_ref[...] = before_ref[...]
    ends = parcel_rows(size_x, size_y)[0 if axis == "gx" else 1]
    cells = size_y if axis == "gx" else size_x + 2
    for number, (side, parcel) in enumerate(zip(SIDES, parcels)):
        row = ends[0]
        inside = lies_inside(axis, side)
        for c in range(6):
            for half in range(2):
                lanes = slice(half * LANES, (half + 1) * LANES)
                if axis == "gx":
                    value = parcel[row : row + cells]
                    row += cells
                else:
                    value = parcel[pl.ds(ends[0] + c * 2 * cells + half, cells, stride=2), :]
                held[c, number * cells : (number + 1) * cells, lanes] = (
                    value if c < 3 else value * inside
                )

    def prepare(index, carry):
        for k in range(2):
            slot = index * 2 + k
            row = [held[c, pl.ds(slot, 1), :] for c in range(6)]
            prepare_column(row, slot, masks, spread, moments)
        return carry

    lax.fori_loop(0, cells, prepare, 0)
    run_tasks(size_y, tasks, table_ref, pack_ref, out_ref, masks[2], spread, moments, True)


def near_tables(size_x, size_y):
    kinds = ({}, {}, {})
    for i in range(size_x):
        for j in range(size_y):
            found = ([], [], [])
            for x in (-1, 0, 1):
                for y in (-1, 0, 1):
                    if not 0 <= j + y < size_y:
                        found[2].extend([int(y > 0) * (size_x + 2) + i + x + 1, x, y])
                    elif not 0 <= i + x < size_x:
                        found[1].extend([int(x > 0) * size_y + j + y, x, y])
                    else:
                        found[0].extend([(i + x) * size_y + j + y, x, y])
            for groups, sources in zip(kinds, found):
                if sources:
                    groups.setdefault(len(sources) // 3, []).append([i, j] + sources)
    result = []
    for groups in kinds:
        flat = []
        tasks = []
        for sources in sorted(groups, reverse=True):
            tasks.append((len(flat), len(groups[sources]), sources))
            for entry in groups[sources]:
                flat += entry
        result.append((np.array(flat, np.int32), tasks))
    return result


def leaf_kernel(size_x, size_y, own_ref, rows_ref, cols_ref, *rest):
    parcels = rest[:4]
    down_ref, base, leaf_ref = rest[4:]
    for depth in range(2):
        for c in range(3):
            for x in range(size_x):
                leaf_ref[depth, c, WIDTH + x, WIDTH : WIDTH + size_y] = own_ref[depth, c, x]
    for side, parcel in zip(SIDES, parcels[:2]):
        inside = lies_inside("gx", side)
        start = landing(side, size_x, WIDTH)
        row = 0
        for depth in range(2):
            for c in range(3):
                for x in range(start, start + WIDTH):
                    leaf_ref[depth, c, x, WIDTH : WIDTH + size_y] = (
                        parcel[row : row + size_y] * inside
                    )
                    row += size_y
    for side, parcel in zip(SIDES, parcels[2:]):
        inside = lies_inside("gy", side)
        start = landing(side, size_y, WIDTH)
        row = 0
        for depth in range(2):
            for c in range(3):
                for x in range(size_x + 2 * WIDTH):
                    leaf_ref[depth, c, x, start : start + WIDTH] = (
                        parcel[row : row + WIDTH] * inside
                    )
                    row += WIDTH
    for axis in range(3):
        base[axis] = 0.9 * rows_ref[axis : axis + 1, :] - 0.9 * cols_ref[axis]
    down_ref[...] = jnp.zeros_like(down_ref)
    odd_y = lax.broadcasted_iota(jnp.int32, (size_y, LANES), 0) % 2
    near_y = {-3: jnp.where(odd_y == 1, 1.0, 0.0), 3: jnp.where(odd_y == 0, 1.0, 0.0)}

    def one_row(shift_x, shifts_y):
        dx = base[0] - shift_x.astype(F32)
        tables = []
        highs = []
        lows = []
        for shift_y in shifts_y:
            dy = base[1] - float(shift_y)
            flat = dx * dx + dy * dy + SMOOTH2
            table = []
            for shift_z in (-1, 0, 1):
                dz = base[2] - float(shift_z)
                table.append(lax.rsqrt(flat + dz * dz).astype(BF16))
            tables.append(jnp.concatenate([table[1], table[0]], axis=1))
            tables.append(jnp.concatenate([table[2], table[1]], axis=1))
            for depth in range(2):
                pieces = []
                for c in range(3):
                    for x in range(size_x):
                        near_x = (shift_x > -3) if x % 2 == 0 else (shift_x < 3)
                        piece = jnp.where(
                            near_x,
                            leaf_ref[depth, c, x + 3 + shift_x, 3 + shift_y : 3 + shift_y + size_y],
                            0.0,
                        )
                        if abs(shift_y) == 3:
                            piece = piece * near_y[shift_y]
                        pieces.append(piece)
                high, low = split(jnp.concatenate(pieces, axis=0))
                highs.append(high)
                lows.append(low)
        rows = 3 * size_x * size_y
        both = bdot(
            jnp.concatenate(
                [jnp.concatenate(highs, axis=1), jnp.concatenate(lows, axis=1)], axis=0
            ),
            jnp.concatenate(tables, axis=0),
        )
        down_ref[...] += both[:rows] + both[rows:]

    def outer(step, carry):
        one_row(jnp.where(step < 2, step - 3, step), (-3, -2, -1, 0, 1, 2, 3))
        return carry

    def inner(step, carry):
        one_row(step - 1, (-3, -2, 2, 3))
        return carry

    lax.fori_loop(0, 4, outer, 0)
    lax.fori_loop(0, 3, inner, 0)


def far_kernel(
    size_x,
    size_y,
    tops_x,
    tops_y,
    chunk,
    slot_ref,
    counts_ref,
    down_ref,
    tops_ref,
    near_ref,
    pack_ref,
    rows_ref,
    cols_ref,
    pattern_ref,
    inverse_ref,
    out_ref,
    base,
    windows,
    down,
    top_down,
    local,
):
    half_x = size_x // 2
    half_y = size_y // 2
    group = half_x * 4
    across = tops_x + half_x - 1
    along = tops_y + half_y - 1
    point = [rows_ref[j : j + 1, :] for j in range(3)]
    for axis in range(3):
        base[axis] = 1.8 * point[axis] - 1.8 * cols_ref[axis]

    windows[...] = jnp.zeros_like(windows)
    lanes_x = tops_x // half_x
    lanes_y = tops_y // half_y
    mine_x = lax.axis_index("gx")
    mine_y = lax.axis_index("gy")

    def place(device, carry):
        place_x = device // lanes_y
        place_y = device % lanes_y
        away_x = lax.rem(place_x - mine_x + lanes_x, lanes_x)
        away_y = lax.rem(place_y - mine_y + lanes_y, lanes_y)
        slot = slot_ref[away_x * lanes_y + away_y]
        i = place_x * half_x
        j = place_y * half_y
        for c in range(3):
            for p in range(half_x):
                for q in range(half_y):
                    row = tops_ref[slot, (c * half_x + p) * half_y + q, :][None]
                    for x in range(half_x):
                        windows[
                            i + p + half_x - 1 - x,
                            pl.ds((j + q + half_y - 1) * group + x * 4 + c, 1),
                            :,
                        ] = row
        return carry

    lax.fori_loop(0, lanes_x * lanes_y, place, 0)
    first_x = mine_x * half_x
    first_y = mine_y * half_y
    top_down[...] = jnp.zeros_like(top_down)
    parts = -(-along // chunk)

    def top_row(step, carry):
        wx = step // parts
        start = (step % parts) * chunk
        gap_x = first_x - (wx - (half_x - 1))
        dx = base[0] + 2.0 * gap_x.astype(F32)
        squares = dx * dx + base[2] * base[2] + SMOOTH2
        tables = []
        pieces = []
        for k in range(chunk):
            wy = start + k
            gap_y = first_y - (wy - (half_y - 1))
            distant = (jnp.abs(gap_x) >= 2) | (jnp.abs(gap_y) >= 2)
            dy = base[1] + 2.0 * gap_y.astype(F32)
            tables.append(lax.rsqrt(squares + dy * dy).astype(BF16))
            rows = windows[wx, pl.ds(wy * group, half_y * group), :]
            pieces.append(jnp.where(distant, rows, 0.0))
        high, low = split(jnp.concatenate(pieces, axis=1))
        top_down[...] += bdot(
            jnp.concatenate([high, low], axis=0), jnp.concatenate(tables, axis=0)
        )
        return carry

    lax.fori_loop(0, across * parts, top_row, 0)
    matrix = inverse_ref[...]
    rows = half_y * group
    top_local = dot_nt(top_down[:rows] + top_down[rows:], matrix)
    down[...] = down_ref[...]
    for a in range(2):
        for b in range(2):
            for e in range(2):
                offset = (a - 0.5, b - 0.5, e - 0.5)
                delta = [
                    offset[axis] + 0.9 * point[axis] - 3.0 * cols_ref[axis] for axis in range(3)
                ]
                table = lax.rsqrt(
                    delta[0] * delta[0] + delta[1] * delta[1] + delta[2] * delta[2] + SMOOTH2
                )
                inherited = jnp.dot(
                    top_local, table, precision=HIGHEST, preferred_element_type=F32
                )
                for y in range(half_y):
                    for x in range(half_x):
                        for c in range(3):
                            row = (c * size_x + 2 * x + a) * size_y + 2 * y + b
                            down[row : row + 1, e * LANES : (e + 1) * LANES] += inherited[
                                y * group + x * 4 + c : y * group + x * 4 + c + 1
                            ]
    for e in range(2):
        part = 0.5 * dot_nt(down[:, e * LANES : (e + 1) * LANES], matrix)
        local[e] = part.reshape(3, size_x, size_y, LANES)

    lane = lax.broadcasted_iota(jnp.int32, (1, LANES), 1)

    def one_column(index):
        i = index // size_y
        j = index % size_y
        row = [pack_ref[c, i, pl.ds(j, 1), :] for c in range(3)]
        results = []
        for half in range(2):
            lanes = slice(half * LANES, (half + 1) * LANES)
            place = [row[axis][:, lanes] for axis in range(3)]
            delta = [place[axis] - 1.5 * cols_ref[axis] for axis in range(3)]
            high, low = split(cubes(*delta))
            charge = jnp.concatenate(
                [local[half, c, i, pl.ds(j, 1), :] for c in range(3)], axis=0
            )
            weight = pattern_ref[half] * jnp.concatenate(
                [charge] * 5 + [jnp.zeros((1, LANES), F32)], axis=0
            )
            total = bdot(two_terms(*split(weight)), jnp.concatenate([high, low], axis=0))
            total = total[:16] + total[16:] + near_ref[index, :, lanes]
            place[2] = place[2] + (half - 0.5)
            living = jnp.where(lane < counts_ref[i, j, half], 1.0, 0.0)
            square = (
                place[0] * place[0] + place[1] * place[1] + place[2] * place[2] + SMOOTH2
            )
            potential = (
                square * total[0:3]
                - 2.0
                * (place[0] * total[3:6] + place[1] * total[6:9] + place[2] * total[9:12])
                + total[12:15]
            ) * living
            slopes = [
                (total[3 + 3 * axis : 6 + 3 * axis] - place[axis] * total[0:3]) * living
                for axis in range(3)
            ]
            results.append((potential, slopes))
        potential = jnp.concatenate([results[0][0], results[1][0]], axis=1)
        slopes = [
            jnp.concatenate([results[0][1][axis], results[1][1][axis]], axis=1)
            for axis in range(3)
        ]
        for c in range(3):
            out_ref[c, i, pl.ds(j, 1), :] = potential[c : c + 1]
            for axis in range(3):
                out_ref[3 + 3 * c + axis, i, pl.ds(j, 1), :] = slopes[axis][c : c + 1]

    def columns(index, carry):
        for k in range(4):
            one_column(index * 4 + k)
        return carry

    lax.fori_loop(0, size_x * size_y // 4, columns, 0)


def moved(array, axis, step):
    count = lax.axis_size(axis)
    return lax.ppermute(array, axis, [((i + step) % count, i) for i in range(count)])


def widened(blocks, away, axis, name):
    count = lax.axis_size(name)
    half = 1
    while 2 * half + 1 < count:
        missing = count - 2 * half - 1
        if missing <= 2 * half + 1:
            first = -((missing - 1) // 2)
            steps = (half + 1 - first,)
        else:
            first = -half
            missing = 2 * half + 1
            steps = (missing, -missing)
        sent = []
        known = []
        for array, places in zip(blocks, away):
            pick = [k for k, place in enumerate(places) if 0 <= place[axis] - first < missing]
            known += [places[k] for k in pick]
            if len(pick) == len(places):
                sent.append(array)
            else:
                size = array.shape[0] // len(places)
                sent += [array[k * size : (k + 1) * size] for k in pick]
        whole = sent[0] if len(sent) == 1 else jnp.concatenate(sent, axis=0)
        for step in steps:
            blocks = blocks + [moved(whole, name, step)]
            away = away + [
                [tuple(p + step * (k == axis) for k, p in enumerate(place)) for place in known]
            ]
        half = half + steps[0] if len(steps) == 2 else count
    return blocks, away


def body(offsets, strengths, counts, check_inverse):
    size_x, size_y, depth = counts.shape
    expansion = check_inverse.shape[0]
    half_x = size_x // 2
    half_y = size_y // 2
    lanes_x = lax.axis_size("gx")
    lanes_y = lax.axis_size("gy")
    tops_x = lanes_x * half_x
    tops_y = lanes_y * half_y
    points = sphere_points(expansion)
    rows = jnp.asarray(np.concatenate([points, np.zeros((5, LANES), np.float32)], axis=0))
    cols = jnp.asarray(np.repeat(points[:, :, None], LANES, axis=2))
    patterns = np.zeros((2, 16, LANES), np.float32)
    for half in range(2):
        lifted = (1.5 * points).astype(np.float32)
        lifted[2] += half - 0.5
        factors = [np.ones(LANES), *lifted, np.sum(lifted.astype(np.float64) ** 2, axis=0)]
        for k in range(5):
            patterns[half, 3 * k : 3 * k + 3, :] = factors[k]
    patterns = jnp.asarray(patterns)

    params = pltpu.CompilerParams(vmem_limit_bytes=58 * 2**20)
    smem = pl.BlockSpec(memory_space=pltpu.SMEM)
    vmem = pl.BlockSpec(memory_space=pltpu.VMEM)

    def cost(flops):
        return pl.CostEstimate(flops=flops, bytes_accessed=10**6, transcendentals=0)

    top_rows = 3 * half_x * half_y
    (_, _, end_x), (_, near_y, end_y) = parcel_rows(size_x, size_y)
    made = pl.pallas_call(
        functools.partial(up_kernel, size_x, size_y),
        out_shape=(
            jax.ShapeDtypeStruct((6, size_x, size_y, depth * LANES), F32),
            jax.ShapeDtypeStruct((2, 3, size_x, size_y, LANES), F32),
            jax.ShapeDtypeStruct((top_rows, LANES), F32),
            jax.ShapeDtypeStruct((LANES, LANES), F32),
            *[jax.ShapeDtypeStruct((end_x, LANES), F32)] * 2,
        ),
        in_specs=[smem] + [vmem] * 5,
        out_specs=(vmem,) * 6,
        scratch_shapes=[pltpu.VMEM((2, 3, size_x, size_y, LANES), F32)],
        compiler_params=params,
        cost_estimate=cost(6 * 10**9),
        name="up",
    )(counts, offsets, strengths, rows, cols, check_inverse)
    pack, leaf_charges, top_charges, matrix, to_below, to_above = made
    below = moved(to_above, "gx", -1)
    above = moved(to_below, "gx", 1)

    (own_table, own_tasks), *beside = near_tables(size_x, size_y)
    near_shape = jax.ShapeDtypeStruct((size_x * size_y, 16, 2 * LANES), F32)
    own = pl.pallas_call(
        functools.partial(own_kernel, size_x, size_y, own_tasks),
        out_shape=near_shape,
        in_specs=[smem, vmem],
        out_specs=vmem,
        scratch_shapes=[
            pltpu.VMEM((size_x * size_y, 4, 2 * LANES, LANES), F32),
            pltpu.VMEM((size_x * size_y, 4, 16, 2 * LANES), F32),
        ],
        compiler_params=params,
        cost_estimate=cost(3 * 10**10),
        name="own",
    )(jnp.asarray(own_table), pack)

    to_low, to_high, tops = pl.pallas_call(
        functools.partial(turn_kernel, size_x, size_y),
        out_shape=(
            jax.ShapeDtypeStruct((end_y, LANES), F32),
            jax.ShapeDtypeStruct((end_y, LANES), F32),
            jax.ShapeDtypeStruct((3 * top_rows, LANES), F32),
        ),
        in_specs=[vmem] * 5,
        out_specs=(vmem,) * 3,
        compiler_params=params,
        cost_estimate=cost(10**9),
        name="turn",
    )(leaf_charges, pack, top_charges, below, above)
    low = moved(to_high, "gy", -1)
    high = moved(to_low, "gy", 1)
    blocks, away = widened(
        [low[near_y:], tops, high[near_y:]],
        [[(x, y) for x in (-1, 0, 1)] for y in (-1, 0, 1)],
        1,
        "gy",
    )

    def beside_near(axis, before, parcels):
        table, tasks = beside[0 if axis == "gx" else 1]
        columns = 2 * (size_y if axis == "gx" else size_x + 2)
        return pl.pallas_call(
            functools.partial(halo_kernel, size_x, size_y, axis, tasks),
            out_shape=near_shape,
            in_specs=[smem] + [vmem] * 4,
            out_specs=vmem,
            scratch_shapes=[
                pltpu.VMEM((columns, 4, 2 * LANES, LANES), F32),
                pltpu.VMEM((columns, 4, 16, 2 * LANES), F32),
                pltpu.VMEM((6, columns, 2 * LANES), F32),
            ],
            compiler_params=params,
            cost_estimate=cost(10**10),
            name="beside_" + axis,
        )(jnp.asarray(table), before, pack, *parcels)

    near = beside_near("gx", own, (below, above))
    blocks, away = widened(blocks, away, 0, "gx")
    away = [place for places in away for place in places]
    blocks = jnp.concatenate(blocks, axis=0).reshape(len(away), top_rows, LANES)
    slots = np.zeros((lanes_x, lanes_y), np.int32)
    for slot, (x, y) in reversed(list(enumerate(away))):
        slots[x % lanes_x, y % lanes_y] = slot
    near = beside_near("gy", near, (low, high))

    down = pl.pallas_call(
        functools.partial(leaf_kernel, size_x, size_y),
        out_shape=jax.ShapeDtypeStruct((3 * size_x * size_y, 2 * LANES), F32),
        in_specs=[vmem] * 7,
        out_specs=vmem,
        scratch_shapes=[
            pltpu.VMEM((3, LANES, LANES), F32),
            pltpu.VMEM(
                (2, 3, size_x + 2 * WIDTH, size_y + 2 * WIDTH, LANES), F32
            ),
        ],
        compiler_params=params,
        cost_estimate=cost(6 * 10**9),
        name="leaf",
    )(leaf_charges, rows, cols, below, above, low, high)

    across = tops_x + half_x - 1
    along = tops_y + half_y - 1
    parts = -(-along // 20)
    chunk = -(-along // parts)
    return pl.pallas_call(
        functools.partial(far_kernel, size_x, size_y, tops_x, tops_y, chunk),
        out_shape=jax.ShapeDtypeStruct((12, size_x, size_y, depth * LANES), F32),
        in_specs=[smem] * 2 + [vmem] * 8,
        out_specs=vmem,
        scratch_shapes=[
            pltpu.VMEM((3, LANES, LANES), F32),
            pltpu.VMEM((across, (parts * chunk + half_y - 1) * half_x * 4, LANES), F32),
            pltpu.VMEM((3 * size_x * size_y, 2 * LANES), F32),
            pltpu.VMEM((2 * half_y * half_x * 4, LANES), F32),
            pltpu.VMEM((2, 3, size_x, size_y, LANES), F32),
        ],
        compiler_params=params,
        cost_estimate=cost(10**10),
        name="far",
    )(
        jnp.asarray(slots.reshape(-1)),
        counts,
        down,
        blocks,
        near,
        pack,
        rows,
        cols,
        patterns,
        matrix,
    )


def solution(mesh):
    return jax.shard_map(
        body,
        mesh=mesh,
        in_specs=(P(None, "gx", "gy", None), P(None, "gx", "gy", None), P("gx", "gy", None), P()),
        out_specs=P(None, "gx", "gy", None),
        check_vma=False,
    )
```

```python
import functools
import math

import jax
import jax.numpy as jnp
import numpy as np
from jax import lax
from jax.experimental import pallas as pl
from jax.experimental.pallas import tpu as pltpu
from jax.sharding import PartitionSpec as P

SMOOTH2 = 0.01
STRENGTH_SCALE = 0.03
LANES = 128
F32 = jnp.float32
BF16 = jnp.bfloat16
HIGHEST = lax.Precision.HIGHEST


def sphere_points(amount):
    counter = np.arange(amount, dtype=np.float32)
    height = (1.0 - (2.0 * counter + 1.0) / np.float32(amount)).astype(np.float32)
    radius = np.sqrt(np.maximum(1.0 - height * height, 0.0)).astype(np.float32)
    azimuth = counter * np.float32(math.pi * (3.0 - math.sqrt(5.0)))
    points = np.zeros((3, LANES), np.float32)
    points[:, :amount] = np.stack([radius * np.cos(azimuth), radius * np.sin(azimuth), height])
    return points


def split(value):
    high = value.astype(BF16)
    return high, (value - high.astype(F32)).astype(BF16)


def bdot(left, right):
    return jnp.dot(left, right, preferred_element_type=F32)


def dot_nt(left, right):
    return lax.dot_general(
        left, right, (((1,), (1,)), ((), ())), precision=HIGHEST, preferred_element_type=F32
    )


def two_terms(high, low):
    return jnp.concatenate(
        [
            jnp.concatenate([high, high], axis=1),
            jnp.concatenate([low, jnp.zeros_like(low)], axis=1),
        ],
        axis=0,
    )


def cubes(dx, dy, dz):
    inverse = lax.rsqrt(dx * dx + dy * dy + dz * dz + SMOOTH2)
    return inverse * inverse * inverse


SIDES = (-1, 1)
WIDTH = 3


def edge(side, size, width):
    return 0 if side < 0 else size - width


def landing(side, size, width):
    return 0 if side < 0 else size + width


def parcel_rows(size_x, size_y):
    tops = 3 * (size_x // 2) * (size_y // 2)
    leaves_x = 6 * WIDTH * size_y
    leaves_y = 6 * (size_x + 2 * WIDTH) * WIDTH
    near_x = leaves_x + 12 * size_y
    near_y = leaves_y + 12 * (size_x + 2)
    return (leaves_x, near_x, near_x + tops), (leaves_y, near_y, near_y + 3 * tops)


def lies_inside(axis, side):
    place = lax.axis_index(axis) + side
    return jnp.where((place >= 0) & (place < lax.axis_size(axis)), 1.0, 0.0)


def up_kernel(
    size_x,
    size_y,
    counts_ref,
    offsets_ref,
    strengths_ref,
    rows_ref,
    cols_ref,
    inverse_ref,
    pack_ref,
    leaf_ref,
    top_ref,
    matrix_ref,
    *rest,
):
    parcels = rest[:2]
    check = rest[2]
    point = [rows_ref[j : j + 1, :] for j in range(3)]
    lane = lax.broadcasted_iota(jnp.int32, (1, 2 * LANES), 1)
    expansion = inverse_ref.shape[0]
    matrix_ref[...] = jnp.zeros_like(matrix_ref)
    matrix_ref[:expansion, :expansion] = inverse_ref[...]
    pack_ref[0:3] = offsets_ref[...]

    def one_column(i, j):
        row = [offsets_ref[c, i, pl.ds(j, 1), :] for c in range(3)]
        at = (i * size_y + j) * 2
        last = jnp.where(lane < LANES, counts_ref[at], counts_ref[at + 1] + LANES)
        charges = []
        for c in range(3):
            value = jnp.where(
                lane < last, STRENGTH_SCALE * strengths_ref[c, i, pl.ds(j, 1), :], 0.0
            )
            pack_ref[3 + c, i, pl.ds(j, 1), :] = value
            charges.append(value)
        charge = jnp.concatenate(charges + [jnp.zeros((5, 2 * LANES), F32)], axis=0)
        for half in range(2):
            lanes = slice(half * LANES, (half + 1) * LANES)
            delta = [1.5 * cols_ref[axis] - row[axis][:, lanes] for axis in range(3)]
            kernel = lax.rsqrt(
                delta[0] * delta[0] + delta[1] * delta[1] + delta[2] * delta[2] + SMOOTH2
            )
            both = jnp.concatenate(split(charge[:, lanes]), axis=0)
            total = lax.dot_general(
                jnp.concatenate([both, both], axis=1),
                jnp.concatenate(split(kernel), axis=1),
                (((1,), (1,)), ((), ())),
                preferred_element_type=F32,
            )
            total = total[:8] + total[8:]
            for c in range(3):
                check[half, c, i, pl.ds(j, 1), :] = total[c : c + 1]

    def columns(index, carry):
        for k in range(4):
            step = index * 4 + k
            one_column(step // size_y, step % size_y)
        return carry

    lax.fori_loop(0, size_x * size_y // 4, columns, 0)
    matrix = matrix_ref[...]
    rows = 6 * size_x * size_y
    charges = 0.5 * dot_nt(check[...].reshape(rows, LANES), matrix)
    leaf_ref[...] = charges.reshape(2, 3, size_x, size_y, LANES)
    half_x = size_x // 2
    half_y = size_y // 2
    total = jnp.zeros((3 * half_x * half_y, LANES), F32)
    for a in range(2):
        for b in range(2):
            for e in range(2):
                shift = (a - 0.5, b - 0.5, e - 0.5)
                delta = [
                    3.0 * point[axis] - shift[axis] - 0.9 * cols_ref[axis] for axis in range(3)
                ]
                table = lax.rsqrt(
                    delta[0] * delta[0] + delta[1] * delta[1] + delta[2] * delta[2] + SMOOTH2
                )
                pieces = [
                    leaf_ref[e, c, 2 * x + a, pl.ds(b, half_y, stride=2), :]
                    for c in range(3)
                    for x in range(half_x)
                ]
                total = total + jnp.dot(
                    jnp.concatenate(pieces, axis=0),
                    table,
                    precision=HIGHEST,
                    preferred_element_type=F32,
                )
    tops = dot_nt(total, matrix)
    top_ref[...] = tops
    (_, second, end), _ = parcel_rows(size_x, size_y)
    for side, parcel in zip(SIDES, parcels):
        row = 0
        start = edge(side, size_x, WIDTH)
        for depth in range(2):
            for c in range(3):
                for x in range(start, start + WIDTH):
                    parcel[row : row + size_y] = leaf_ref[depth, c, x]
                    row += size_y
        for c in range(6):
            for half in range(2):
                lanes = slice(half * LANES, (half + 1) * LANES)
                parcel[row : row + size_y] = pack_ref[c, edge(side, size_x, 1), :, lanes]
                row += size_y
        parcel[second:end] = tops


def turn_kernel(
    size_x, size_y, leaf_ref, pack_ref, top_ref, below_ref, above_ref, low_ref, high_ref, tops_ref
):
    (_, near_x, end_x), (_, near_y, _) = parcel_rows(size_x, size_y)
    count = end_x - near_x
    for place, ref in ((0, below_ref), (2, above_ref)):
        tops_ref[place * count : (place + 1) * count] = ref[near_x:end_x]
    tops_ref[count : 2 * count] = top_ref[...]
    inside = [lies_inside("gx", side) for side in SIDES]
    for side, parcel in zip(SIDES, (low_ref, high_ref)):
        row = 0
        start = edge(side, size_y, WIDTH)
        for depth in range(2):
            for c in range(3):
                for x in range(-WIDTH, size_x + WIDTH):
                    if 0 <= x < size_x:
                        value = leaf_ref[depth, c, x, start : start + WIDTH]
                    else:
                        which = int(x >= size_x)
                        ref = (below_ref, above_ref)[which]
                        cell = x - size_x if which else x + WIDTH
                        at = ((depth * 3 + c) * WIDTH + cell) * size_y + start
                        value = ref[at : at + WIDTH] * inside[which]
                    parcel[row : row + WIDTH] = value
                    row += WIDTH
        start = edge(side, size_y, 1)
        first, _, _ = parcel_rows(size_x, size_y)[0]
        for c in range(6):
            for x in range(-1, size_x + 1):
                for half in range(2):
                    if 0 <= x < size_x:
                        lanes = slice(half * LANES, (half + 1) * LANES)
                        value = pack_ref[c, x, start : start + 1, lanes]
                    else:
                        which = int(x >= size_x)
                        ref = (below_ref, above_ref)[which]
                        at = first + (c * 2 + half) * size_y + start
                        value = ref[at : at + 1]
                        if c >= 3:
                            value = value * inside[which]
                    parcel[row : row + 1] = value
                    row += 1
        parcel[near_y : near_y + 3 * count] = tops_ref[...]


def near_masks():
    row = lax.broadcasted_iota(jnp.int32, (16, 2 * LANES), 0)
    lane = lax.broadcasted_iota(jnp.int32, (1, 2 * LANES), 1)
    return row // 3, row % 3, jnp.where(lane < LANES, -0.5, 0.5).astype(F32)


def prepare_column(row, slot, masks, spread, moments):
    level, kind, lift = masks
    x, y, z = row[0], row[1], row[2] + lift
    square = x * x + y * y + z * z
    values = jnp.concatenate(
        [-2.0 * x, -2.0 * y, -2.0 * z, square, jnp.zeros((4, 2 * LANES), F32)], axis=0
    )
    first = values.astype(BF16).astype(F32)
    second = (values - first).astype(BF16).astype(F32)
    terms = jnp.concatenate(
        [first, second, (values - first) - second, jnp.zeros_like(values)], axis=0
    ).T.astype(BF16)
    term = lax.broadcasted_iota(jnp.int32, (32, 4 * LANES), 0)
    place = lax.broadcasted_iota(jnp.int32, (32, 4 * LANES), 1) // LANES
    chosen = jnp.where((term % 8 == place) & (term < 24), 1.0, 0.0).astype(BF16)
    laid = bdot(terms, chosen)
    for axis in range(4):
        spread[slot, axis] = laid[:, axis * LANES : (axis + 1) * LANES]

    def wide(value):
        return jnp.broadcast_to(value, (16, 2 * LANES))

    charge = jnp.where(
        kind == 0, wide(row[3]), jnp.where(kind == 1, wide(row[4]), wide(row[5]))
    )
    charge = jnp.where(level < 5, charge, 0.0)
    factor = jnp.where(level == 3, wide(z), wide(square))
    factor = jnp.where(level == 2, wide(y), factor)
    factor = jnp.where(level == 1, wide(x), factor)
    moments[slot, 0] = charge * jnp.where(level == 0, 1.0, factor)
    last = jnp.where(level == 4, charge, 0.0)
    moments[slot, 1] = jnp.where(level == 1, charge, last * wide(2.0 * x))
    moments[slot, 2] = jnp.where(level == 2, charge, last * wide(2.0 * y))
    moments[slot, 3] = last


def shifted(moments, slot, shift_x, shift_y):
    return (
        moments[slot, 0]
        + shift_x * moments[slot, 1]
        + shift_y * moments[slot, 2]
        + (shift_x * shift_x + shift_y * shift_y) * moments[slot, 3]
    )


def pair_cubes(target, slot, shift_x, shift_y, spread):
    x = target[0] - shift_x
    y = target[1] - shift_y
    z = target[2]
    square = x * x + y * y + z * z + SMOOTH2
    result = []
    for half in range(2):
        part = slice(half * LANES, (half + 1) * LANES)
        highs = []
        lows = []
        for side in range(2):
            lanes = slice(side * LANES, (side + 1) * LANES)
            distance = (
                (square[:, lanes] + spread[slot, 3, part, :])
                + x[:, lanes] * spread[slot, 0, part, :]
                + y[:, lanes] * spread[slot, 1, part, :]
                + z[:, lanes] * spread[slot, 2, part, :]
            )
            inverse = lax.rsqrt(distance)
            high, low = split(inverse * inverse * inverse)
            highs.append(high)
            lows.append(low)
        result.append((jnp.concatenate(highs, axis=1), jnp.concatenate(lows, axis=1)))
    return result


def near_sums(target, blocks, spread, moments):
    total = jnp.zeros((32, 2 * LANES), F32)
    for slot, shift_x, shift_y in blocks:
        w_high, w_low = split(shifted(moments, slot, shift_x, shift_y))
        for half, terms in enumerate(pair_cubes(target, slot, shift_x, shift_y, spread)):
            part = slice(half * LANES, (half + 1) * LANES)
            total = total + bdot(
                two_terms(w_high[:, part], w_low[:, part]), jnp.concatenate(terms, axis=0)
            )
    return total[:16] + total[16:]


def run_tasks(size_y, tasks, table_ref, pack_ref, out_ref, lift, spread, moments, adds):
    for start, amount, sources in tasks:
        together = 1
        while together * sources < 12 and amount % (2 * together) == 0:
            together *= 2

        def one(index, start, sources):
            at = start + index * (2 + 3 * sources)
            i = table_ref[at]
            j = table_ref[at + 1]
            target = [pack_ref[c, i, pl.ds(j, 1), :] for c in range(3)]
            target[2] = target[2] + lift
            blocks = [
                (
                    table_ref[at + 2 + 3 * k],
                    table_ref[at + 3 + 3 * k].astype(F32),
                    table_ref[at + 4 + 3 * k].astype(F32),
                )
                for k in range(sources)
            ]
            return i * size_y + j, near_sums(target, blocks, spread, moments)

        def step(index, carry, start=start, sources=sources, together=together):
            found = [one(index * together + k, start, sources) for k in range(together)]
            for place, total in found:
                out_ref[place] = total + out_ref[place] if adds else total
            return carry

        lax.fori_loop(0, amount // together, step, 0)


def own_kernel(size_x, size_y, tasks, table_ref, pack_ref, out_ref, spread, moments):
    masks = near_masks()

    def prepare(index, carry):
        for k in range(4):
            slot = index * 4 + k
            row = [pack_ref[c, slot // size_y, pl.ds(slot % size_y, 1), :] for c in range(6)]
            prepare_column(row, slot, masks, spread, moments)
        return carry

    lax.fori_loop(0, size_x * size_y // 4, prepare, 0)
    out_ref[...] = jnp.zeros_like(out_ref)

    def places(i, j):
        row = [pack_ref[c, i, pl.ds(j, 1), :] for c in range(3)]
        return [row[0], row[1], row[2] + masks[2]]

    def one(at, others):
        i = table_ref[at]
        j = table_ref[at + 1]
        slot = i * size_y + j
        total = near_sums(places(i, j), [(slot, 0.0, 0.0)], spread, moments)
        found = []
        for k in range(others):
            i, j, away_x, away_y = [table_ref[at + 2 + 4 * k + m] for m in range(4)]
            away_x = away_x.astype(F32)
            away_y = away_y.astype(F32)
            other = i * size_y + j
            (h_first, l_first), (h_second, l_second) = pair_cubes(
                places(i, j), slot, -away_x, -away_y, spread
            )
            high = jnp.concatenate([h_first, h_second], axis=0)
            low = jnp.concatenate([l_first, l_second], axis=0)
            there = bdot(
                two_terms(*split(shifted(moments, slot, -away_x, -away_y))),
                jnp.concatenate([high, low], axis=0),
            )
            found.append((other, there[:16] + there[16:]))
            here = lax.dot_general(
                two_terms(*split(shifted(moments, other, away_x, away_y))),
                jnp.concatenate([high, low], axis=1),
                (((1,), (1,)), ((), ())),
                preferred_element_type=F32,
            )
            total = total + here[:16] + here[16:]
        found.append((slot, total))
        return found

    for start, amount, others in tasks:
        together = 3 if amount % 3 == 0 else 1

        def step(index, carry, start=start, others=others, together=together):
            found = []
            for k in range(together):
                found += one(start + (index * together + k) * (2 + 4 * others), others)
            for place, total in found:
                out_ref[place] += total
            return carry

        lax.fori_loop(0, amount // together, step, 0)


def halo_kernel(size_x, size_y, axis, tasks, table_ref, before_ref, pack_ref, *rest):
    parcels = rest[:2]
    out_ref, spread, moments, held = rest[2:]
    masks = near_masks()
    out_ref[...] = before_ref[...]
    ends = parcel_rows(size_x, size_y)[0 if axis == "gx" else 1]
    cells = size_y if axis == "gx" else size_x + 2
    for number, (side, parcel) in enumerate(zip(SIDES, parcels)):
        row = ends[0]
        inside = lies_inside(axis, side)
        for c in range(6):
            for half in range(2):
                lanes = slice(half * LANES, (half + 1) * LANES)
                if axis == "gx":
                    value = parcel[row : row + cells]
                    row += cells
                else:
                    value = parcel[pl.ds(ends[0] + c * 2 * cells + half, cells, stride=2), :]
                held[c, number * cells : (number + 1) * cells, lanes] = (
                    value if c < 3 else value * inside
                )

    def prepare(index, carry):
        for k in range(4):
            slot = index * 4 + k
            row = [held[c, pl.ds(slot, 1), :] for c in range(6)]
            prepare_column(row, slot, masks, spread, moments)
        return carry

    lax.fori_loop(0, 2 * cells // 4, prepare, 0)
    run_tasks(size_y, tasks, table_ref, pack_ref, out_ref, masks[2], spread, moments, True)


def near_tables(size_x, size_y):
    kinds = ({}, {}, {})
    for i in range(size_x):
        for j in range(size_y):
            pairs = []
            for x, y in ((0, 1), (1, -1), (1, 0), (1, 1)):
                if i + x < size_x and 0 <= j + y < size_y:
                    pairs += [i + x, j + y, x, y]
            kinds[0].setdefault(len(pairs) // 4, []).append([i, j] + pairs)
            found = ([], [], [])
            for x in (-1, 0, 1):
                for y in (-1, 0, 1):
                    if not 0 <= j + y < size_y:
                        found[2].extend([int(y > 0) * (size_x + 2) + i + x + 1, x, y])
                    elif not 0 <= i + x < size_x:
                        found[1].extend([int(x > 0) * size_y + j + y, x, y])
            for groups, sources in zip(kinds[1:], found[1:]):
                if sources:
                    groups.setdefault(len(sources) // 3, []).append([i, j] + sources)
    result = []
    for groups in kinds:
        flat = []
        tasks = []
        for sources in sorted(groups, reverse=True):
            tasks.append((len(flat), len(groups[sources]), sources))
            for entry in groups[sources]:
                flat += entry
        result.append((np.array(flat, np.int32), tasks))
    return result


def leaf_kernel(size_x, size_y, own_ref, rows_ref, cols_ref, *rest):
    parcels = rest[:4]
    down_ref, base, leaf_ref = rest[4:]
    for depth in range(2):
        for c in range(3):
            for x in range(size_x):
                leaf_ref[depth, c, WIDTH + x, WIDTH : WIDTH + size_y] = own_ref[depth, c, x]
    for side, parcel in zip(SIDES, parcels[:2]):
        inside = lies_inside("gx", side)
        start = landing(side, size_x, WIDTH)
        row = 0
        for depth in range(2):
            for c in range(3):
                for x in range(start, start + WIDTH):
                    leaf_ref[depth, c, x, WIDTH : WIDTH + size_y] = (
                        parcel[row : row + size_y] * inside
                    )
                    row += size_y
    for side, parcel in zip(SIDES, parcels[2:]):
        inside = lies_inside("gy", side)
        start = landing(side, size_y, WIDTH)
        row = 0
        for depth in range(2):
            for c in range(3):
                for x in range(size_x + 2 * WIDTH):
                    leaf_ref[depth, c, x, start : start + WIDTH] = (
                        parcel[row : row + WIDTH] * inside
                    )
                    row += WIDTH
    for axis in range(3):
        base[axis] = 0.9 * rows_ref[axis : axis + 1, :] - 0.9 * cols_ref[axis]
    down_ref[...] = jnp.zeros_like(down_ref)
    odd_y = lax.broadcasted_iota(jnp.int32, (size_y, LANES), 0) % 2
    near_y = {-3: jnp.where(odd_y == 1, 1.0, 0.0), 3: jnp.where(odd_y == 0, 1.0, 0.0)}

    def one_row(shift_x, shifts_y):
        dx = base[0] - shift_x.astype(F32)
        tables = []
        highs = []
        lows = []
        for shift_y in shifts_y:
            dy = base[1] - float(shift_y)
            flat = dx * dx + dy * dy + SMOOTH2
            table = []
            for shift_z in (-1, 0, 1):
                dz = base[2] - float(shift_z)
                table.append(lax.rsqrt(flat + dz * dz).astype(BF16))
            tables.append(jnp.concatenate([table[1], table[0]], axis=1))
            tables.append(jnp.concatenate([table[2], table[1]], axis=1))
            for depth in range(2):
                pieces = []
                for c in range(3):
                    for x in range(size_x):
                        near_x = (shift_x > -3) if x % 2 == 0 else (shift_x < 3)
                        piece = jnp.where(
                            near_x,
                            leaf_ref[depth, c, x + 3 + shift_x, 3 + shift_y : 3 + shift_y + size_y],
                            0.0,
                        )
                        if abs(shift_y) == 3:
                            piece = piece * near_y[shift_y]
                        pieces.append(piece)
                high, low = split(jnp.concatenate(pieces, axis=0))
                highs.append(high)
                lows.append(low)
        rows = 3 * size_x * size_y
        both = bdot(
            jnp.concatenate(
                [jnp.concatenate(highs, axis=1), jnp.concatenate(lows, axis=1)], axis=0
            ),
            jnp.concatenate(tables, axis=0),
        )
        down_ref[...] += both[:rows] + both[rows:]

    def outer(step, carry):
        one_row(jnp.where(step < 2, step - 3, step), (-3, -2, -1, 0, 1, 2, 3))
        return carry

    def inner(step, carry):
        one_row(step - 1, (-3, -2, 2, 3))
        return carry

    lax.fori_loop(0, 4, outer, 0)
    lax.fori_loop(0, 3, inner, 0)


def far_kernel(
    size_x,
    size_y,
    tops_x,
    tops_y,
    chunk,
    slot_ref,
    counts_ref,
    down_ref,
    tops_ref,
    near_ref,
    pack_ref,
    rows_ref,
    cols_ref,
    pattern_ref,
    inverse_ref,
    out_ref,
    base,
    windows,
    down,
    top_down,
    local,
):
    half_x = size_x // 2
    half_y = size_y // 2
    group = half_x * 4
    across = tops_x + half_x - 1
    along = tops_y + half_y - 1
    point = [rows_ref[j : j + 1, :] for j in range(3)]
    for axis in range(3):
        base[axis] = 1.8 * point[axis] - 1.8 * cols_ref[axis]

    windows[...] = jnp.zeros_like(windows)
    lanes_x = tops_x // half_x
    lanes_y = tops_y // half_y
    mine_x = lax.axis_index("gx")
    mine_y = lax.axis_index("gy")

    def place(device, carry):
        place_x = device // lanes_y
        place_y = device % lanes_y
        away_x = lax.rem(place_x - mine_x + lanes_x, lanes_x)
        away_y = lax.rem(place_y - mine_y + lanes_y, lanes_y)
        slot = slot_ref[away_x * lanes_y + away_y]
        i = place_x * half_x
        j = place_y * half_y
        for c in range(3):
            for p in range(half_x):
                for q in range(half_y):
                    row = tops_ref[slot, (c * half_x + p) * half_y + q, :][None]
                    for x in range(half_x):
                        windows[
                            i + p + half_x - 1 - x,
                            pl.ds((j + q + half_y - 1) * group + x * 4 + c, 1),
                            :,
                        ] = row
        return carry

    lax.fori_loop(0, lanes_x * lanes_y, place, 0)
    first_x = mine_x * half_x
    first_y = mine_y * half_y
    top_down[...] = jnp.zeros_like(top_down)
    parts = -(-along // chunk)

    def top_row(step, carry):
        wx = step // parts
        start = (step % parts) * chunk
        gap_x = first_x - (wx - (half_x - 1))
        dx = base[0] + 2.0 * gap_x.astype(F32)
        squares = dx * dx + base[2] * base[2] + SMOOTH2
        tables = []
        pieces = []
        for k in range(chunk):
            wy = start + k
            gap_y = first_y - (wy - (half_y - 1))
            distant = (jnp.abs(gap_x) >= 2) | (jnp.abs(gap_y) >= 2)
            dy = base[1] + 2.0 * gap_y.astype(F32)
            tables.append(lax.rsqrt(squares + dy * dy).astype(BF16))
            rows = windows[wx, pl.ds(wy * group, half_y * group), :]
            pieces.append(jnp.where(distant, rows, 0.0))
        high, low = split(jnp.concatenate(pieces, axis=1))
        top_down[...] += bdot(
            jnp.concatenate([high, low], axis=0), jnp.concatenate(tables, axis=0)
        )
        return carry

    lax.fori_loop(0, across * parts, top_row, 0)
    matrix = inverse_ref[...]
    rows = half_y * group
    top_local = dot_nt(top_down[:rows] + top_down[rows:], matrix)
    down[...] = down_ref[...]
    for a in range(2):
        for b in range(2):
            for e in range(2):
                offset = (a - 0.5, b - 0.5, e - 0.5)
                delta = [
                    offset[axis] + 0.9 * point[axis] - 3.0 * cols_ref[axis] for axis in range(3)
                ]
                table = lax.rsqrt(
                    delta[0] * delta[0] + delta[1] * delta[1] + delta[2] * delta[2] + SMOOTH2
                )
                inherited = jnp.dot(
                    top_local, table, precision=HIGHEST, preferred_element_type=F32
                )
                for y in range(half_y):
                    for x in range(half_x):
                        for c in range(3):
                            row = (c * size_x + 2 * x + a) * size_y + 2 * y + b
                            down[row : row + 1, e * LANES : (e + 1) * LANES] += inherited[
                                y * group + x * 4 + c : y * group + x * 4 + c + 1
                            ]
    for e in range(2):
        part = 0.5 * dot_nt(down[:, e * LANES : (e + 1) * LANES], matrix)
        local[e] = part.reshape(3, size_x, size_y, LANES)

    lane = lax.broadcasted_iota(jnp.int32, (1, LANES), 1)

    def one_column(index):
        i = index // size_y
        j = index % size_y
        row = [pack_ref[c, i, pl.ds(j, 1), :] for c in range(3)]
        results = []
        for half in range(2):
            lanes = slice(half * LANES, (half + 1) * LANES)
            place = [row[axis][:, lanes] for axis in range(3)]
            delta = [place[axis] - 1.5 * cols_ref[axis] for axis in range(3)]
            high, low = split(cubes(*delta))
            charge = jnp.concatenate(
                [local[half, c, i, pl.ds(j, 1), :] for c in range(3)], axis=0
            )
            weight = pattern_ref[half] * jnp.concatenate(
                [charge] * 5 + [jnp.zeros((1, LANES), F32)], axis=0
            )
            total = bdot(two_terms(*split(weight)), jnp.concatenate([high, low], axis=0))
            total = total[:16] + total[16:] + near_ref[index, :, lanes]
            place[2] = place[2] + (half - 0.5)
            living = jnp.where(lane < counts_ref[2 * index + half], 1.0, 0.0)
            square = (
                place[0] * place[0] + place[1] * place[1] + place[2] * place[2] + SMOOTH2
            )
            potential = (
                square * total[0:3]
                - 2.0
                * (place[0] * total[3:6] + place[1] * total[6:9] + place[2] * total[9:12])
                + total[12:15]
            ) * living
            slopes = [
                (total[3 + 3 * axis : 6 + 3 * axis] - place[axis] * total[0:3]) * living
                for axis in range(3)
            ]
            results.append((potential, slopes))
        potential = jnp.concatenate([results[0][0], results[1][0]], axis=1)
        slopes = [
            jnp.concatenate([results[0][1][axis], results[1][1][axis]], axis=1)
            for axis in range(3)
        ]
        for c in range(3):
            out_ref[c, i, pl.ds(j, 1), :] = potential[c : c + 1]
            for axis in range(3):
                out_ref[3 + 3 * c + axis, i, pl.ds(j, 1), :] = slopes[axis][c : c + 1]

    def columns(index, carry):
        for k in range(4):
            one_column(index * 4 + k)
        return carry

    lax.fori_loop(0, size_x * size_y // 4, columns, 0)


def moved(array, axis, step):
    count = lax.axis_size(axis)
    return lax.ppermute(array, axis, [((i + step) % count, i) for i in range(count)])


def widened(blocks, away, axis, name):
    count = lax.axis_size(name)
    half = 1
    while 2 * half + 1 < count:
        missing = count - 2 * half - 1
        if missing <= 2 * half + 1:
            first = -((missing - 1) // 2)
            steps = (half + 1 - first,)
        else:
            first = -half
            missing = 2 * half + 1
            steps = (missing, -missing)
        sent = []
        known = []
        for array, places in zip(blocks, away):
            pick = [k for k, place in enumerate(places) if 0 <= place[axis] - first < missing]
            known += [places[k] for k in pick]
            if len(pick) == len(places):
                sent.append(array)
            else:
                size = array.shape[0] // len(places)
                sent += [array[k * size : (k + 1) * size] for k in pick]
        whole = sent[0] if len(sent) == 1 else jnp.concatenate(sent, axis=0)
        for step in steps:
            blocks = blocks + [moved(whole, name, step)]
            away = away + [
                [tuple(p + step * (k == axis) for k, p in enumerate(place)) for place in known]
            ]
        half = half + steps[0] if len(steps) == 2 else count
    return blocks, away


def body(offsets, strengths, counts, check_inverse):
    size_x, size_y, depth = counts.shape
    expansion = check_inverse.shape[0]
    half_x = size_x // 2
    half_y = size_y // 2
    lanes_x = lax.axis_size("gx")
    lanes_y = lax.axis_size("gy")
    tops_x = lanes_x * half_x
    tops_y = lanes_y * half_y
    points = sphere_points(expansion)
    rows = jnp.asarray(np.concatenate([points, np.zeros((5, LANES), np.float32)], axis=0))
    cols = jnp.asarray(np.repeat(points[:, :, None], LANES, axis=2))
    patterns = np.zeros((2, 16, LANES), np.float32)
    for half in range(2):
        lifted = (1.5 * points).astype(np.float32)
        lifted[2] += half - 0.5
        factors = [np.ones(LANES), *lifted, np.sum(lifted.astype(np.float64) ** 2, axis=0)]
        for k in range(5):
            patterns[half, 3 * k : 3 * k + 3, :] = factors[k]
    patterns = jnp.asarray(patterns)

    params = pltpu.CompilerParams(vmem_limit_bytes=58 * 2**20)
    smem = pl.BlockSpec(memory_space=pltpu.SMEM)
    vmem = pl.BlockSpec(memory_space=pltpu.VMEM)

    def cost(flops):
        return pl.CostEstimate(flops=flops, bytes_accessed=10**6, transcendentals=0)

    top_rows = 3 * half_x * half_y
    (_, _, end_x), (_, near_y, end_y) = parcel_rows(size_x, size_y)
    made = pl.pallas_call(
        functools.partial(up_kernel, size_x, size_y),
        out_shape=(
            jax.ShapeDtypeStruct((6, size_x, size_y, depth * LANES), F32),
            jax.ShapeDtypeStruct((2, 3, size_x, size_y, LANES), F32),
            jax.ShapeDtypeStruct((top_rows, LANES), F32),
            jax.ShapeDtypeStruct((LANES, LANES), F32),
            *[jax.ShapeDtypeStruct((end_x, LANES), F32)] * 2,
        ),
        in_specs=[smem] + [vmem] * 5,
        out_specs=(vmem,) * 6,
        scratch_shapes=[pltpu.VMEM((2, 3, size_x, size_y, LANES), F32)],
        compiler_params=params,
        cost_estimate=cost(6 * 10**9),
        name="up",
    )(counts.reshape(-1), offsets, strengths, rows, cols, check_inverse)
    pack, leaf_charges, top_charges, matrix, to_below, to_above = made
    below = moved(to_above, "gx", -1)
    above = moved(to_below, "gx", 1)

    (own_table, own_tasks), *beside = near_tables(size_x, size_y)
    near_shape = jax.ShapeDtypeStruct((size_x * size_y, 16, 2 * LANES), F32)
    own = pl.pallas_call(
        functools.partial(own_kernel, size_x, size_y, own_tasks),
        out_shape=near_shape,
        in_specs=[smem, vmem],
        out_specs=vmem,
        scratch_shapes=[
            pltpu.VMEM((size_x * size_y, 4, 2 * LANES, LANES), F32),
            pltpu.VMEM((size_x * size_y, 4, 16, 2 * LANES), F32),
        ],
        compiler_params=params,
        cost_estimate=cost(3 * 10**10),
        name="own",
    )(jnp.asarray(own_table), pack)

    to_low, to_high, tops = pl.pallas_call(
        functools.partial(turn_kernel, size_x, size_y),
        out_shape=(
            jax.ShapeDtypeStruct((end_y, LANES), F32),
            jax.ShapeDtypeStruct((end_y, LANES), F32),
            jax.ShapeDtypeStruct((3 * top_rows, LANES), F32),
        ),
        in_specs=[vmem] * 5,
        out_specs=(vmem,) * 3,
        compiler_params=params,
        cost_estimate=cost(10**9),
        name="turn",
    )(leaf_charges, pack, top_charges, below, above)
    low = moved(to_high, "gy", -1)
    high = moved(to_low, "gy", 1)
    blocks, away = widened(
        [low[near_y:], tops, high[near_y:]],
        [[(x, y) for x in (-1, 0, 1)] for y in (-1, 0, 1)],
        1,
        "gy",
    )

    def beside_near(axis, before, parcels):
        table, tasks = beside[0 if axis == "gx" else 1]
        columns = 2 * (size_y if axis == "gx" else size_x + 2)
        return pl.pallas_call(
            functools.partial(halo_kernel, size_x, size_y, axis, tasks),
            out_shape=near_shape,
            in_specs=[smem] + [vmem] * 4,
            out_specs=vmem,
            scratch_shapes=[
                pltpu.VMEM((columns, 4, 2 * LANES, LANES), F32),
                pltpu.VMEM((columns, 4, 16, 2 * LANES), F32),
                pltpu.VMEM((6, columns, 2 * LANES), F32),
            ],
            compiler_params=params,
            cost_estimate=cost(10**10),
            name="beside_" + axis,
        )(jnp.asarray(table), before, pack, *parcels)

    near = beside_near("gx", own, (below, above))
    blocks, away = widened(blocks, away, 0, "gx")
    away = [place for places in away for place in places]
    blocks = jnp.concatenate(blocks, axis=0).reshape(len(away), top_rows, LANES)
    slots = np.zeros((lanes_x, lanes_y), np.int32)
    for slot, (x, y) in reversed(list(enumerate(away))):
        slots[x % lanes_x, y % lanes_y] = slot
    near = beside_near("gy", near, (low, high))

    down = pl.pallas_call(
        functools.partial(leaf_kernel, size_x, size_y),
        out_shape=jax.ShapeDtypeStruct((3 * size_x * size_y, 2 * LANES), F32),
        in_specs=[vmem] * 7,
        out_specs=vmem,
        scratch_shapes=[
            pltpu.VMEM((3, LANES, LANES), F32),
            pltpu.VMEM(
                (2, 3, size_x + 2 * WIDTH, size_y + 2 * WIDTH, LANES), F32
            ),
        ],
        compiler_params=params,
        cost_estimate=cost(6 * 10**9),
        name="leaf",
    )(leaf_charges, rows, cols, below, above, low, high)

    across = tops_x + half_x - 1
    along = tops_y + half_y - 1
    parts = -(-along // 20)
    chunk = -(-along // parts)
    return pl.pallas_call(
        functools.partial(far_kernel, size_x, size_y, tops_x, tops_y, chunk),
        out_shape=jax.ShapeDtypeStruct((12, size_x, size_y, depth * LANES), F32),
        in_specs=[smem] * 2 + [vmem] * 8,
        out_specs=vmem,
        scratch_shapes=[
            pltpu.VMEM((3, LANES, LANES), F32),
            pltpu.VMEM((across, (parts * chunk + half_y - 1) * half_x * 4, LANES), F32),
            pltpu.VMEM((3 * size_x * size_y, 2 * LANES), F32),
            pltpu.VMEM((2 * half_y * half_x * 4, LANES), F32),
            pltpu.VMEM((2, 3, size_x, size_y, LANES), F32),
        ],
        compiler_params=params,
        cost_estimate=cost(10**10),
        name="far",
    )(
        jnp.asarray(slots.reshape(-1)),
        counts.reshape(-1),
        down,
        blocks,
        near,
        pack,
        rows,
        cols,
        patterns,
        matrix,
    )


def solution(mesh):
    return jax.shard_map(
        body,
        mesh=mesh,
        in_specs=(P(None, "gx", "gy", None), P(None, "gx", "gy", None), P("gx", "gy", None), P()),
        out_specs=P(None, "gx", "gy", None),
        check_vma=False,
    )
```

```python
import functools
import math

import jax
import jax.numpy as jnp
import numpy as np
from jax import lax
from jax.experimental import pallas as pl
from jax.experimental.pallas import tpu as pltpu
from jax.sharding import PartitionSpec as P

SMOOTH2 = 0.01
STRENGTH_SCALE = 0.03
LANES = 128
F32 = jnp.float32
BF16 = jnp.bfloat16


def sphere_points(amount):
    counter = np.arange(amount, dtype=np.float32)
    height = (1.0 - (2.0 * counter + 1.0) / np.float32(amount)).astype(np.float32)
    radius = np.sqrt(np.maximum(1.0 - height * height, 0.0)).astype(np.float32)
    azimuth = counter * np.float32(math.pi * (3.0 - math.sqrt(5.0)))
    points = np.zeros((3, LANES), np.float32)
    points[:, :amount] = np.stack([radius * np.cos(azimuth), radius * np.sin(azimuth), height])
    return points


def split(value):
    high = value.astype(BF16)
    return high, (value - high.astype(F32)).astype(BF16)


def bdot(left, right):
    return jnp.dot(left, right, preferred_element_type=F32)


def two_terms(high, low):
    return jnp.concatenate(
        [
            jnp.concatenate([high, high], axis=1),
            jnp.concatenate([low, jnp.zeros_like(low)], axis=1),
        ],
        axis=0,
    )


def dot_split(left, right):
    rows = left.shape[0]
    both = bdot(two_terms(*split(left)), jnp.concatenate(split(right), axis=0))
    return both[:rows] + both[rows:]


def dot_split_nt(left, right):
    rows = left.shape[0]
    both = lax.dot_general(
        two_terms(*split(left)),
        jnp.concatenate(split(right), axis=1),
        (((1,), (1,)), ((), ())),
        preferred_element_type=F32,
    )
    return both[:rows] + both[rows:]


def lay_points(cols_ref, rows_ref):
    for axis in range(3):
        row = rows_ref[axis : axis + 1, :]
        cols_ref[axis] = jnp.broadcast_to(row, (LANES, LANES)).T


def lay_surface(surface, cols_ref):
    total = jnp.zeros((LANES, LANES), F32)
    for axis in range(3):
        surface[axis] = -3.0 * cols_ref[axis]
        total = total + 2.25 * cols_ref[axis] * cols_ref[axis]
    surface[3] = total


def surface_distance(surface, place):
    square = place[0] * place[0] + place[1] * place[1] + place[2] * place[2] + SMOOTH2
    return (
        (square + surface[3])
        + place[0] * surface[0]
        + place[1] * surface[1]
        + place[2] * surface[2]
    )


SIDES = (-1, 1)
WIDTH = 3


def edge(side, size, width):
    return 0 if side < 0 else size - width


def landing(side, size, width):
    return 0 if side < 0 else size + width


def parcel_rows(size_x, size_y):
    tops = 3 * (size_x // 2) * (size_y // 2)
    leaves_x = 6 * WIDTH * size_y
    leaves_y = 6 * (size_x + 2 * WIDTH) * WIDTH
    near_x = leaves_x + 12 * size_y
    near_y = leaves_y + 12 * (size_x + 2)
    return (leaves_x, near_x, near_x + tops), (leaves_y, near_y, near_y + 3 * tops)


def lies_inside(axis, side):
    place = lax.axis_index(axis) + side
    return jnp.where((place >= 0) & (place < lax.axis_size(axis)), 1.0, 0.0)


def up_kernel(
    size_x,
    size_y,
    counts_ref,
    offsets_ref,
    strengths_ref,
    rows_ref,
    inverse_ref,
    pack_ref,
    leaf_ref,
    top_ref,
    matrix_ref,
    living_ref,
    *rest,
):
    parcels = rest[:2]
    check, surface, cols_ref, strong, inverse, arrived = rest[2:]
    copies = [
        pltpu.make_async_copy(source, target, arrived.at[k])
        for k, (source, target) in enumerate(
            (
                (offsets_ref, pack_ref.at[0:3]),
                (strengths_ref, strong),
                (inverse_ref, inverse),
            )
        )
    ]
    for copy in copies:
        copy.start()
    lay_points(cols_ref, rows_ref)
    lay_surface(surface, cols_ref)
    for copy in copies:
        copy.wait()
    point = [rows_ref[j : j + 1, :] for j in range(3)]
    lane = lax.broadcasted_iota(jnp.int32, (1, LANES), 1)
    expansion = inverse_ref.shape[0]
    matrix_ref[...] = jnp.zeros_like(matrix_ref)
    matrix_ref[:expansion, :expansion] = inverse[...]

    def one_column(i, j):
        row = [pack_ref[c, i, pl.ds(j, 1), :] for c in range(3)]
        count = counts_ref[i, pl.ds(j, 1), :]
        living = jnp.concatenate(
            [
                jnp.where(lane < jnp.broadcast_to(count[:, k : k + 1], (1, LANES)), 1.0, 0.0)
                for k in range(2)
            ],
            axis=1,
        )
        living_ref[i, pl.ds(j, 1), :] = living
        charges = []
        for c in range(3):
            value = STRENGTH_SCALE * strong[c, i, pl.ds(j, 1), :] * living
            pack_ref[3 + c, i, pl.ds(j, 1), :] = value
            charges.append(value)
        charge = jnp.concatenate(charges + [jnp.zeros((5, 2 * LANES), F32)], axis=0)
        for half in range(2):
            lanes = slice(half * LANES, (half + 1) * LANES)
            place = [row[axis][:, lanes] for axis in range(3)]
            kernel = lax.rsqrt(surface_distance(surface, place))
            both = jnp.concatenate(split(charge[:, lanes]), axis=0)
            total = lax.dot_general(
                jnp.concatenate([both, both], axis=1),
                jnp.concatenate(split(kernel), axis=1),
                (((1,), (1,)), ((), ())),
                preferred_element_type=F32,
            )
            total = total[:8] + total[8:]
            for c in range(3):
                check[half, c, i, pl.ds(j, 1), :] = total[c : c + 1]

    def columns(index, carry):
        for k in range(4):
            step = index * 4 + k
            one_column(step // size_y, step % size_y)
        return carry

    lax.fori_loop(0, size_x * size_y // 4, columns, 0)
    matrix = matrix_ref[...]
    rows = 6 * size_x * size_y
    charges = 0.5 * dot_split_nt(check[...].reshape(rows, LANES), matrix)
    leaf_ref[...] = charges.reshape(2, 3, size_x, size_y, LANES)
    half_x = size_x // 2
    half_y = size_y // 2
    count = 3 * half_x * half_y
    padding = -count % 16
    filler = [jnp.zeros((padding, LANES), F32)] if padding else []
    total = jnp.zeros((count + padding, LANES), F32)
    for a in range(2):
        for b in range(2):
            for e in range(2):
                shift = (a - 0.5, b - 0.5, e - 0.5)
                delta = [
                    3.0 * point[axis] - shift[axis] - 0.9 * cols_ref[axis] for axis in range(3)
                ]
                table = lax.rsqrt(
                    delta[0] * delta[0] + delta[1] * delta[1] + delta[2] * delta[2] + SMOOTH2
                )
                pieces = [
                    leaf_ref[e, c, 2 * x + a, pl.ds(b, half_y, stride=2), :]
                    for c in range(3)
                    for x in range(half_x)
                ]
                total = total + dot_split(jnp.concatenate(pieces + filler, axis=0), table)
    tops = dot_split_nt(total, matrix)[:count]
    top_ref[...] = tops
    (_, second, end), _ = parcel_rows(size_x, size_y)
    for side, parcel in zip(SIDES, parcels):
        row = 0
        start = edge(side, size_x, WIDTH)
        for depth in range(2):
            for c in range(3):
                for x in range(start, start + WIDTH):
                    parcel[row : row + size_y] = leaf_ref[depth, c, x]
                    row += size_y
        for c in range(6):
            for half in range(2):
                lanes = slice(half * LANES, (half + 1) * LANES)
                parcel[row : row + size_y] = pack_ref[c, edge(side, size_x, 1), :, lanes]
                row += size_y
        parcel[second:end] = tops


def turn_kernel(
    size_x, size_y, leaf_ref, pack_ref, top_ref, below_ref, above_ref, low_ref, high_ref, tops_ref
):
    (_, near_x, end_x), (_, near_y, _) = parcel_rows(size_x, size_y)
    count = end_x - near_x
    for place, ref in ((0, below_ref), (2, above_ref)):
        tops_ref[place * count : (place + 1) * count] = ref[near_x:end_x]
    tops_ref[count : 2 * count] = top_ref[...]
    inside = [lies_inside("gx", side) for side in SIDES]
    for side, parcel in zip(SIDES, (low_ref, high_ref)):
        row = 0
        start = edge(side, size_y, WIDTH)
        for depth in range(2):
            for c in range(3):
                for x in range(-WIDTH, size_x + WIDTH):
                    if 0 <= x < size_x:
                        value = leaf_ref[depth, c, x, start : start + WIDTH]
                    else:
                        which = int(x >= size_x)
                        ref = (below_ref, above_ref)[which]
                        cell = x - size_x if which else x + WIDTH
                        at = ((depth * 3 + c) * WIDTH + cell) * size_y + start
                        value = ref[at : at + WIDTH] * inside[which]
                    parcel[row : row + WIDTH] = value
                    row += WIDTH
        start = edge(side, size_y, 1)
        first, _, _ = parcel_rows(size_x, size_y)[0]
        for c in range(6):
            for x in range(-1, size_x + 1):
                for half in range(2):
                    if 0 <= x < size_x:
                        lanes = slice(half * LANES, (half + 1) * LANES)
                        value = pack_ref[c, x, start : start + 1, lanes]
                    else:
                        which = int(x >= size_x)
                        ref = (below_ref, above_ref)[which]
                        at = first + (c * 2 + half) * size_y + start
                        value = ref[at : at + 1]
                        if c >= 3:
                            value = value * inside[which]
                    parcel[row : row + 1] = value
                    row += 1
        parcel[near_y : near_y + 3 * count] = tops_ref[...]


def near_masks():
    row = lax.broadcasted_iota(jnp.int32, (16, 2 * LANES), 0)
    lane = lax.broadcasted_iota(jnp.int32, (1, 2 * LANES), 1)
    return row // 3, row % 3, jnp.where(lane < LANES, -0.5, 0.5).astype(F32)


def prepare_column(row, slot, masks, spread, moments):
    level, kind, lift = masks
    x, y, z = row[0], row[1], row[2] + lift
    square = x * x + y * y + z * z
    values = jnp.concatenate(
        [-2.0 * x, -2.0 * y, -2.0 * z, square, jnp.zeros((4, 2 * LANES), F32)], axis=0
    )
    first = values.astype(BF16).astype(F32)
    second = (values - first).astype(BF16).astype(F32)
    terms = jnp.concatenate(
        [first, second, (values - first) - second, jnp.zeros_like(values)], axis=0
    ).T.astype(BF16)
    term = lax.broadcasted_iota(jnp.int32, (32, 4 * LANES), 0)
    place = lax.broadcasted_iota(jnp.int32, (32, 4 * LANES), 1) // LANES
    chosen = jnp.where((term % 8 == place) & (term < 24), 1.0, 0.0).astype(BF16)
    laid = bdot(terms, chosen)
    for axis in range(4):
        spread[slot, axis] = laid[:, axis * LANES : (axis + 1) * LANES]

    def wide(value):
        return jnp.broadcast_to(value, (16, 2 * LANES))

    charge = jnp.where(
        kind == 0, wide(row[3]), jnp.where(kind == 1, wide(row[4]), wide(row[5]))
    )
    charge = jnp.where(level < 5, charge, 0.0)
    factor = jnp.where(level == 3, wide(z), wide(square))
    factor = jnp.where(level == 2, wide(y), factor)
    factor = jnp.where(level == 1, wide(x), factor)
    moments[slot, 0] = charge * jnp.where(level == 0, 1.0, factor)
    last = jnp.where(level == 4, charge, 0.0)
    moments[slot, 1] = jnp.where(level == 1, charge, last * wide(2.0 * x))
    moments[slot, 2] = jnp.where(level == 2, charge, last * wide(2.0 * y))
    moments[slot, 3] = last


def shifted(moments, slot, shift_x, shift_y):
    return (
        moments[slot, 0]
        + shift_x * moments[slot, 1]
        + shift_y * moments[slot, 2]
        + (shift_x * shift_x + shift_y * shift_y) * moments[slot, 3]
    )


def pair_cubes(target, slot, shift_x, shift_y, spread):
    x = target[0] - shift_x
    y = target[1] - shift_y
    z = target[2]
    square = x * x + y * y + z * z + SMOOTH2
    result = []
    for half in range(2):
        part = slice(half * LANES, (half + 1) * LANES)
        highs = []
        lows = []
        for side in range(2):
            lanes = slice(side * LANES, (side + 1) * LANES)
            distance = (
                (square[:, lanes] + spread[slot, 3, part, :])
                + x[:, lanes] * spread[slot, 0, part, :]
                + y[:, lanes] * spread[slot, 1, part, :]
                + z[:, lanes] * spread[slot, 2, part, :]
            )
            inverse = lax.rsqrt(distance)
            high, low = split(inverse * inverse * inverse)
            highs.append(high)
            lows.append(low)
        result.append((jnp.concatenate(highs, axis=1), jnp.concatenate(lows, axis=1)))
    return result


def near_sums(target, blocks, spread, moments):
    total = jnp.zeros((32, 2 * LANES), F32)
    for slot, shift_x, shift_y in blocks:
        w_high, w_low = split(shifted(moments, slot, shift_x, shift_y))
        for half, terms in enumerate(pair_cubes(target, slot, shift_x, shift_y, spread)):
            part = slice(half * LANES, (half + 1) * LANES)
            total = total + bdot(
                two_terms(w_high[:, part], w_low[:, part]), jnp.concatenate(terms, axis=0)
            )
    return total[:16] + total[16:]


def run_tasks(size_y, tasks, table_ref, pack_ref, out_ref, lift, spread, moments, adds):
    for start, amount, sources in tasks:
        together = 1
        while together * sources < 12 and amount % (2 * together) == 0:
            together *= 2

        def one(index, start, sources):
            at = start + index * (2 + 3 * sources)
            i = table_ref[at]
            j = table_ref[at + 1]
            target = [pack_ref[c, i, pl.ds(j, 1), :] for c in range(3)]
            target[2] = target[2] + lift
            blocks = [
                (
                    table_ref[at + 2 + 3 * k],
                    table_ref[at + 3 + 3 * k].astype(F32),
                    table_ref[at + 4 + 3 * k].astype(F32),
                )
                for k in range(sources)
            ]
            return i * size_y + j, near_sums(target, blocks, spread, moments)

        def step(index, carry, start=start, sources=sources, together=together):
            found = [one(index * together + k, start, sources) for k in range(together)]
            for place, total in found:
                out_ref[place] = total + out_ref[place] if adds else total
            return carry

        lax.fori_loop(0, amount // together, step, 0)


def own_kernel(size_x, size_y, tasks, table_ref, pack_ref, out_ref, spread, moments):
    masks = near_masks()

    def prepare(index, carry):
        for k in range(4):
            slot = index * 4 + k
            row = [pack_ref[c, slot // size_y, pl.ds(slot % size_y, 1), :] for c in range(6)]
            prepare_column(row, slot, masks, spread, moments)
        return carry

    lax.fori_loop(0, size_x * size_y // 4, prepare, 0)
    out_ref[...] = jnp.zeros_like(out_ref)

    def places(i, j):
        row = [pack_ref[c, i, pl.ds(j, 1), :] for c in range(3)]
        return [row[0], row[1], row[2] + masks[2]]

    def one(at, others):
        i = table_ref[at]
        j = table_ref[at + 1]
        slot = i * size_y + j
        total = near_sums(places(i, j), [(slot, 0.0, 0.0)], spread, moments)
        found = []
        for k in range(others):
            i, j, away_x, away_y = [table_ref[at + 2 + 4 * k + m] for m in range(4)]
            away_x = away_x.astype(F32)
            away_y = away_y.astype(F32)
            other = i * size_y + j
            (h_first, l_first), (h_second, l_second) = pair_cubes(
                places(i, j), slot, -away_x, -away_y, spread
            )
            high = jnp.concatenate([h_first, h_second], axis=0)
            low = jnp.concatenate([l_first, l_second], axis=0)
            there = bdot(
                two_terms(*split(shifted(moments, slot, -away_x, -away_y))),
                jnp.concatenate([high, low], axis=0),
            )
            found.append((other, there[:16] + there[16:]))
            here = lax.dot_general(
                two_terms(*split(shifted(moments, other, away_x, away_y))),
                jnp.concatenate([high, low], axis=1),
                (((1,), (1,)), ((), ())),
                preferred_element_type=F32,
            )
            total = total + here[:16] + here[16:]
        found.append((slot, total))
        return found

    for start, amount, others in tasks:
        together = 3 if amount % 3 == 0 else 1

        def step(index, carry, start=start, others=others, together=together):
            found = []
            for k in range(together):
                found += one(start + (index * together + k) * (2 + 4 * others), others)
            for place, total in found:
                out_ref[place] += total
            return carry

        lax.fori_loop(0, amount // together, step, 0)


def halo_kernel(size_x, size_y, axis, tasks, table_ref, before_ref, pack_ref, *rest):
    parcels = rest[:2]
    out_ref, spread, moments, held = rest[2:]
    masks = near_masks()
    out_ref[...] = before_ref[...]
    ends = parcel_rows(size_x, size_y)[0 if axis == "gx" else 1]
    cells = size_y if axis == "gx" else size_x + 2
    for number, (side, parcel) in enumerate(zip(SIDES, parcels)):
        row = ends[0]
        inside = lies_inside(axis, side)
        for c in range(6):
            for half in range(2):
                lanes = slice(half * LANES, (half + 1) * LANES)
                if axis == "gx":
                    value = parcel[row : row + cells]
                    row += cells
                else:
                    value = parcel[pl.ds(ends[0] + c * 2 * cells + half, cells, stride=2), :]
                held[c, number * cells : (number + 1) * cells, lanes] = (
                    value if c < 3 else value * inside
                )

    def prepare(index, carry):
        for k in range(4):
            slot = index * 4 + k
            row = [held[c, pl.ds(slot, 1), :] for c in range(6)]
            prepare_column(row, slot, masks, spread, moments)
        return carry

    lax.fori_loop(0, 2 * cells // 4, prepare, 0)
    run_tasks(size_y, tasks, table_ref, pack_ref, out_ref, masks[2], spread, moments, True)


def near_tables(size_x, size_y):
    kinds = ({}, {}, {})
    for i in range(size_x):
        for j in range(size_y):
            pairs = []
            for x, y in ((0, 1), (1, -1), (1, 0), (1, 1)):
                if i + x < size_x and 0 <= j + y < size_y:
                    pairs += [i + x, j + y, x, y]
            kinds[0].setdefault(len(pairs) // 4, []).append([i, j] + pairs)
            found = ([], [], [])
            for x in (-1, 0, 1):
                for y in (-1, 0, 1):
                    if not 0 <= j + y < size_y:
                        found[2].extend([int(y > 0) * (size_x + 2) + i + x + 1, x, y])
                    elif not 0 <= i + x < size_x:
                        found[1].extend([int(x > 0) * size_y + j + y, x, y])
            for groups, sources in zip(kinds[1:], found[1:]):
                if sources:
                    groups.setdefault(len(sources) // 3, []).append([i, j] + sources)
    result = []
    for groups in kinds:
        flat = []
        tasks = []
        for sources in sorted(groups, reverse=True):
            tasks.append((len(flat), len(groups[sources]), sources))
            for entry in groups[sources]:
                flat += entry
        result.append((np.array(flat, np.int32), tasks))
    return result


def leaf_kernel(size_x, size_y, own_ref, rows_ref, *rest):
    parcels = rest[:4]
    down_ref, base, leaf_ref, cols_ref = rest[4:]
    lay_points(cols_ref, rows_ref)
    for depth in range(2):
        for c in range(3):
            for x in range(size_x):
                leaf_ref[depth, c, WIDTH + x, WIDTH : WIDTH + size_y] = own_ref[depth, c, x]
    for side, parcel in zip(SIDES, parcels[:2]):
        inside = lies_inside("gx", side)
        start = landing(side, size_x, WIDTH)
        row = 0
        for depth in range(2):
            for c in range(3):
                for x in range(start, start + WIDTH):
                    leaf_ref[depth, c, x, WIDTH : WIDTH + size_y] = (
                        parcel[row : row + size_y] * inside
                    )
                    row += size_y
    for side, parcel in zip(SIDES, parcels[2:]):
        inside = lies_inside("gy", side)
        start = landing(side, size_y, WIDTH)
        row = 0
        for depth in range(2):
            for c in range(3):
                for x in range(size_x + 2 * WIDTH):
                    leaf_ref[depth, c, x, start : start + WIDTH] = (
                        parcel[row : row + WIDTH] * inside
                    )
                    row += WIDTH
    for axis in range(3):
        base[axis] = 0.9 * rows_ref[axis : axis + 1, :] - 0.9 * cols_ref[axis]
    down_ref[...] = jnp.zeros_like(down_ref)
    odd_y = lax.broadcasted_iota(jnp.int32, (size_y, LANES), 0) % 2
    near_y = {-3: jnp.where(odd_y == 1, 1.0, 0.0), 3: jnp.where(odd_y == 0, 1.0, 0.0)}

    def one_row(shift_x, shifts_y):
        dx = base[0] - shift_x.astype(F32)
        tables = []
        highs = []
        lows = []
        for shift_y in shifts_y:
            dy = base[1] - float(shift_y)
            flat = dx * dx + dy * dy + SMOOTH2
            table = []
            for shift_z in (-1, 0, 1):
                dz = base[2] - float(shift_z)
                table.append(lax.rsqrt(flat + dz * dz).astype(BF16))
            tables.append(jnp.concatenate([table[1], table[0]], axis=1))
            tables.append(jnp.concatenate([table[2], table[1]], axis=1))
            for depth in range(2):
                pieces = []
                for c in range(3):
                    for x in range(size_x):
                        near_x = (shift_x > -3) if x % 2 == 0 else (shift_x < 3)
                        piece = jnp.where(
                            near_x,
                            leaf_ref[depth, c, x + 3 + shift_x, 3 + shift_y : 3 + shift_y + size_y],
                            0.0,
                        )
                        if abs(shift_y) == 3:
                            piece = piece * near_y[shift_y]
                        pieces.append(piece)
                high, low = split(jnp.concatenate(pieces, axis=0))
                highs.append(high)
                lows.append(low)
        rows = 3 * size_x * size_y
        both = bdot(
            jnp.concatenate(
                [jnp.concatenate(highs, axis=1), jnp.concatenate(lows, axis=1)], axis=0
            ),
            jnp.concatenate(tables, axis=0),
        )
        down_ref[...] += both[:rows] + both[rows:]

    def outer(step, carry):
        one_row(jnp.where(step < 2, step - 3, step), (-3, -2, -1, 0, 1, 2, 3))
        return carry

    def inner(step, carry):
        one_row(step - 1, (-3, -2, 2, 3))
        return carry

    lax.fori_loop(0, 4, outer, 0)
    lax.fori_loop(0, 3, inner, 0)


def far_kernel(
    size_x,
    size_y,
    tops_x,
    tops_y,
    chunk,
    slot_ref,
    living_ref,
    down_ref,
    tops_ref,
    near_ref,
    pack_ref,
    rows_ref,
    pattern_ref,
    inverse_ref,
    out_ref,
    base,
    windows,
    down,
    top_down,
    local,
    surface,
    squares_y,
    cols_ref,
):
    half_x = size_x // 2
    half_y = size_y // 2
    group = half_x * 4
    across = tops_x + half_x - 1
    along = tops_y + half_y - 1
    point = [rows_ref[j : j + 1, :] for j in range(3)]
    lay_points(cols_ref, rows_ref)
    for axis in range(3):
        base[axis] = 1.8 * point[axis] - 1.8 * cols_ref[axis]

    windows[...] = jnp.zeros_like(windows)
    lanes_x = tops_x // half_x
    lanes_y = tops_y // half_y
    mine_x = lax.axis_index("gx")
    mine_y = lax.axis_index("gy")

    def place(device, carry):
        place_x = device // lanes_y
        place_y = device % lanes_y
        away_x = lax.rem(place_x - mine_x + lanes_x, lanes_x)
        away_y = lax.rem(place_y - mine_y + lanes_y, lanes_y)
        slot = slot_ref[away_x * lanes_y + away_y]
        i = place_x * half_x
        j = place_y * half_y
        for c in range(3):
            for p in range(half_x):
                for q in range(half_y):
                    row = tops_ref[slot, (c * half_x + p) * half_y + q, :][None]
                    for x in range(half_x):
                        windows[
                            i + p + half_x - 1 - x,
                            pl.ds((j + q + half_y - 1) * group + x * 4 + c, 1),
                            :,
                        ] = row
        return carry

    lax.fori_loop(0, lanes_x * lanes_y, place, 0)
    first_x = mine_x * half_x
    first_y = mine_y * half_y
    top_down[...] = jnp.zeros_like(top_down)
    parts = -(-along // chunk)

    def square_y(wy, carry):
        dy = base[1] + 2.0 * (first_y - (wy - (half_y - 1))).astype(F32)
        squares_y[wy] = dy * dy
        return carry

    lax.fori_loop(0, parts * chunk, square_y, 0)

    def top_row(step):
        wx = step // parts
        start = (step % parts) * chunk
        gap_x = first_x - (wx - (half_x - 1))
        dx = base[0] + 2.0 * gap_x.astype(F32)
        squares = dx * dx + base[2] * base[2] + SMOOTH2
        tables = []
        pieces = []
        for k in range(chunk):
            wy = start + k
            gap_y = first_y - (wy - (half_y - 1))
            distant = (jnp.abs(gap_x) >= 2) | (jnp.abs(gap_y) >= 2)
            tables.append(lax.rsqrt(squares + squares_y[wy]).astype(BF16))
            rows = windows[wx, pl.ds(wy * group, half_y * group), :]
            pieces.append(jnp.where(distant, rows, 0.0))
        high, low = split(jnp.concatenate(pieces, axis=1))
        return bdot(jnp.concatenate([high, low], axis=0), jnp.concatenate(tables, axis=0))

    together = 3
    steps = across * parts

    def top_rows(index, carry):
        found = [top_row(index * together + k) for k in range(together)]
        top_down[...] += sum(found[1:], found[0])
        return carry

    lax.fori_loop(0, steps // together, top_rows, 0)
    for step in range(steps - steps % together, steps):
        top_down[...] += top_row(jnp.int32(step))
    matrix = inverse_ref[...]
    rows = half_y * group
    top_local = dot_split_nt(top_down[:rows] + top_down[rows:], matrix)
    lay_surface(surface, cols_ref)
    down[...] = down_ref[...]
    for a in range(2):
        for b in range(2):
            for e in range(2):
                offset = (a - 0.5, b - 0.5, e - 0.5)
                delta = [
                    offset[axis] + 0.9 * point[axis] - 3.0 * cols_ref[axis] for axis in range(3)
                ]
                table = lax.rsqrt(
                    delta[0] * delta[0] + delta[1] * delta[1] + delta[2] * delta[2] + SMOOTH2
                )
                inherited = dot_split(top_local, table)
                for y in range(half_y):
                    for x in range(half_x):
                        for c in range(3):
                            row = (c * size_x + 2 * x + a) * size_y + 2 * y + b
                            down[row : row + 1, e * LANES : (e + 1) * LANES] += inherited[
                                y * group + x * 4 + c : y * group + x * 4 + c + 1
                            ]
    for e in range(2):
        part = 0.5 * dot_split_nt(down[:, e * LANES : (e + 1) * LANES], matrix)
        local[e] = part.reshape(3, size_x, size_y, LANES)

    def one_column(index):
        i = index // size_y
        j = index % size_y
        row = [pack_ref[c, i, pl.ds(j, 1), :] for c in range(3)]
        alive = living_ref[i, pl.ds(j, 1), :]
        results = []
        for half in range(2):
            lanes = slice(half * LANES, (half + 1) * LANES)
            place = [row[axis][:, lanes] for axis in range(3)]
            inverse = lax.rsqrt(surface_distance(surface, place))
            high, low = split(inverse * inverse * inverse)
            charge = jnp.concatenate(
                [local[half, c, i, pl.ds(j, 1), :] for c in range(3)], axis=0
            )
            weight = pattern_ref[half] * jnp.concatenate(
                [charge] * 5 + [jnp.zeros((1, LANES), F32)], axis=0
            )
            total = bdot(two_terms(*split(weight)), jnp.concatenate([high, low], axis=0))
            total = total[:16] + total[16:] + near_ref[index, :, lanes]
            place[2] = place[2] + (half - 0.5)
            living = alive[:, lanes]
            square = (
                place[0] * place[0] + place[1] * place[1] + place[2] * place[2] + SMOOTH2
            )
            potential = (
                square * total[0:3]
                - 2.0
                * (place[0] * total[3:6] + place[1] * total[6:9] + place[2] * total[9:12])
                + total[12:15]
            ) * living
            slopes = [
                (total[3 + 3 * axis : 6 + 3 * axis] - place[axis] * total[0:3]) * living
                for axis in range(3)
            ]
            results.append((potential, slopes))
        potential = jnp.concatenate([results[0][0], results[1][0]], axis=1)
        slopes = [
            jnp.concatenate([results[0][1][axis], results[1][1][axis]], axis=1)
            for axis in range(3)
        ]
        for c in range(3):
            out_ref[c, i, pl.ds(j, 1), :] = potential[c : c + 1]
            for axis in range(3):
                out_ref[3 + 3 * c + axis, i, pl.ds(j, 1), :] = slopes[axis][c : c + 1]

    def columns(index, carry):
        for k in range(4):
            one_column(index * 4 + k)
        return carry

    lax.fori_loop(0, size_x * size_y // 4, columns, 0)


def moved(array, axis, step):
    count = lax.axis_size(axis)
    return lax.ppermute(array, axis, [((i + step) % count, i) for i in range(count)])


def widened(blocks, away, axis, name):
    count = lax.axis_size(name)
    half = 1
    while 2 * half + 1 < count:
        missing = count - 2 * half - 1
        if missing <= 2 * half + 1:
            first = -((missing - 1) // 2)
            steps = (half + 1 - first,)
        else:
            first = -half
            missing = 2 * half + 1
            steps = (missing, -missing)
        sent = []
        known = []
        for array, places in zip(blocks, away):
            pick = [k for k, place in enumerate(places) if 0 <= place[axis] - first < missing]
            known += [places[k] for k in pick]
            if len(pick) == len(places):
                sent.append(array)
            else:
                size = array.shape[0] // len(places)
                sent += [array[k * size : (k + 1) * size] for k in pick]
        whole = sent[0] if len(sent) == 1 else jnp.concatenate(sent, axis=0)
        for step in steps:
            blocks = blocks + [moved(whole, name, step)]
            away = away + [
                [tuple(p + step * (k == axis) for k, p in enumerate(place)) for place in known]
            ]
        half = half + steps[0] if len(steps) == 2 else count
    return blocks, away


def body(offsets, strengths, counts, check_inverse):
    size_x, size_y, depth = counts.shape
    expansion = check_inverse.shape[0]
    half_x = size_x // 2
    half_y = size_y // 2
    lanes_x = lax.axis_size("gx")
    lanes_y = lax.axis_size("gy")
    tops_x = lanes_x * half_x
    tops_y = lanes_y * half_y
    points = sphere_points(expansion)
    rows = jnp.asarray(np.concatenate([points, np.zeros((5, LANES), np.float32)], axis=0))
    patterns = np.zeros((2, 16, LANES), np.float32)
    for half in range(2):
        lifted = (1.5 * points).astype(np.float32)
        lifted[2] += half - 0.5
        factors = [np.ones(LANES), *lifted, np.sum(lifted.astype(np.float64) ** 2, axis=0)]
        for k in range(5):
            patterns[half, 3 * k : 3 * k + 3, :] = factors[k]
    patterns = jnp.asarray(patterns)

    def params(mebibytes):
        return pltpu.CompilerParams(vmem_limit_bytes=mebibytes * 2**20)

    smem = pl.BlockSpec(memory_space=pltpu.SMEM)
    vmem = pl.BlockSpec(memory_space=pltpu.VMEM)
    hbm = pl.BlockSpec(memory_space=pltpu.HBM)

    def cost(flops):
        return pl.CostEstimate(flops=flops, bytes_accessed=10**6, transcendentals=0)

    top_rows = 3 * half_x * half_y
    (_, _, end_x), (_, near_y, end_y) = parcel_rows(size_x, size_y)
    made = pl.pallas_call(
        functools.partial(up_kernel, size_x, size_y),
        out_shape=(
            jax.ShapeDtypeStruct((6, size_x, size_y, depth * LANES), F32),
            jax.ShapeDtypeStruct((2, 3, size_x, size_y, LANES), F32),
            jax.ShapeDtypeStruct((top_rows, LANES), F32),
            jax.ShapeDtypeStruct((LANES, LANES), F32),
            jax.ShapeDtypeStruct((size_x, size_y, depth * LANES), F32),
            *[jax.ShapeDtypeStruct((end_x, LANES), F32)] * 2,
        ),
        in_specs=[vmem, hbm, hbm, vmem, hbm],
        out_specs=(vmem,) * 7,
        scratch_shapes=[
            pltpu.VMEM((2, 3, size_x, size_y, LANES), F32),
            pltpu.VMEM((4, LANES, LANES), F32),
            pltpu.VMEM((3, LANES, LANES), F32),
            pltpu.VMEM(strengths.shape, F32),
            pltpu.VMEM(check_inverse.shape, F32),
            pltpu.SemaphoreType.DMA((3,)),
        ],
        compiler_params=params(12),
        cost_estimate=cost(6 * 10**9),
        name="up",
    )(counts, offsets, strengths, rows, check_inverse)
    pack, leaf_charges, top_charges, matrix, living, to_below, to_above = made
    below = moved(to_above, "gx", -1)
    above = moved(to_below, "gx", 1)

    (own_table, own_tasks), *beside = near_tables(size_x, size_y)
    near_shape = jax.ShapeDtypeStruct((size_x * size_y, 16, 2 * LANES), F32)
    own = pl.pallas_call(
        functools.partial(own_kernel, size_x, size_y, own_tasks),
        out_shape=near_shape,
        in_specs=[smem, vmem],
        out_specs=vmem,
        scratch_shapes=[
            pltpu.VMEM((size_x * size_y, 4, 2 * LANES, LANES), F32),
            pltpu.VMEM((size_x * size_y, 4, 16, 2 * LANES), F32),
        ],
        compiler_params=params(28),
        cost_estimate=cost(3 * 10**10),
        name="own",
    )(jnp.asarray(own_table), pack)

    to_low, to_high, tops = pl.pallas_call(
        functools.partial(turn_kernel, size_x, size_y),
        out_shape=(
            jax.ShapeDtypeStruct((end_y, LANES), F32),
            jax.ShapeDtypeStruct((end_y, LANES), F32),
            jax.ShapeDtypeStruct((3 * top_rows, LANES), F32),
        ),
        in_specs=[vmem] * 5,
        out_specs=(vmem,) * 3,
        compiler_params=params(12),
        cost_estimate=cost(10**9),
        name="turn",
    )(leaf_charges, pack, top_charges, below, above)
    low = moved(to_high, "gy", -1)
    high = moved(to_low, "gy", 1)
    blocks, away = widened(
        [low[near_y:], tops, high[near_y:]],
        [[(x, y) for x in (-1, 0, 1)] for y in (-1, 0, 1)],
        1,
        "gy",
    )

    def beside_near(axis, before, parcels):
        table, tasks = beside[0 if axis == "gx" else 1]
        columns = 2 * (size_y if axis == "gx" else size_x + 2)
        return pl.pallas_call(
            functools.partial(halo_kernel, size_x, size_y, axis, tasks),
            out_shape=near_shape,
            in_specs=[smem] + [vmem] * 4,
            out_specs=vmem,
            scratch_shapes=[
                pltpu.VMEM((columns, 4, 2 * LANES, LANES), F32),
                pltpu.VMEM((columns, 4, 16, 2 * LANES), F32),
                pltpu.VMEM((6, columns, 2 * LANES), F32),
            ],
            compiler_params=params(20),
            cost_estimate=cost(10**10),
            name="beside_" + axis,
        )(jnp.asarray(table), before, pack, *parcels)

    near = beside_near("gx", own, (below, above))
    blocks, away = widened(blocks, away, 0, "gx")
    away = [place for places in away for place in places]
    blocks = jnp.concatenate(blocks, axis=0).reshape(len(away), top_rows, LANES)
    slots = np.zeros((lanes_x, lanes_y), np.int32)
    for slot, (x, y) in reversed(list(enumerate(away))):
        slots[x % lanes_x, y % lanes_y] = slot
    near = beside_near("gy", near, (low, high))

    down = pl.pallas_call(
        functools.partial(leaf_kernel, size_x, size_y),
        out_shape=jax.ShapeDtypeStruct((3 * size_x * size_y, 2 * LANES), F32),
        in_specs=[vmem] * 6,
        out_specs=vmem,
        scratch_shapes=[
            pltpu.VMEM((3, LANES, LANES), F32),
            pltpu.VMEM(
                (2, 3, size_x + 2 * WIDTH, size_y + 2 * WIDTH, LANES), F32
            ),
            pltpu.VMEM((3, LANES, LANES), F32),
        ],
        compiler_params=params(12),
        cost_estimate=cost(6 * 10**9),
        name="leaf",
    )(leaf_charges, rows, below, above, low, high)

    across = tops_x + half_x - 1
    along = tops_y + half_y - 1
    parts = -(-along // 20)
    chunk = -(-along // parts)
    return pl.pallas_call(
        functools.partial(far_kernel, size_x, size_y, tops_x, tops_y, chunk),
        out_shape=jax.ShapeDtypeStruct((12, size_x, size_y, depth * LANES), F32),
        in_specs=[smem] + [vmem] * 8,
        out_specs=vmem,
        scratch_shapes=[
            pltpu.VMEM((3, LANES, LANES), F32),
            pltpu.VMEM((across, (parts * chunk + half_y - 1) * half_x * 4, LANES), F32),
            pltpu.VMEM((3 * size_x * size_y, 2 * LANES), F32),
            pltpu.VMEM((2 * half_y * half_x * 4, LANES), F32),
            pltpu.VMEM((2, 3, size_x, size_y, LANES), F32),
            pltpu.VMEM((4, LANES, LANES), F32),
            pltpu.VMEM((parts * chunk, LANES, LANES), F32),
            pltpu.VMEM((3, LANES, LANES), F32),
        ],
        compiler_params=params(40),
        cost_estimate=cost(10**10),
        name="far",
    )(
        jnp.asarray(slots.reshape(-1)),
        living,
        down,
        blocks,
        near,
        pack,
        rows,
        patterns,
        matrix,
    )


def solution(mesh):
    return jax.shard_map(
        body,
        mesh=mesh,
        in_specs=(P(None, "gx", "gy", None), P(None, "gx", "gy", None), P("gx", "gy", None), P()),
        out_specs=P(None, "gx", "gy", None),
        check_vma=False,
    )
```

```python
import functools
import math

import jax
import jax.numpy as jnp
import numpy as np
from jax import lax
from jax.experimental import pallas as pl
from jax.experimental.pallas import tpu as pltpu
from jax.sharding import PartitionSpec as P

SMOOTH2 = 0.01
STRENGTH_SCALE = 0.03
LANES = 128
F32 = jnp.float32
BF16 = jnp.bfloat16


def sphere_points(amount):
    counter = np.arange(amount, dtype=np.float32)
    height = (1.0 - (2.0 * counter + 1.0) / np.float32(amount)).astype(np.float32)
    radius = np.sqrt(np.maximum(1.0 - height * height, 0.0)).astype(np.float32)
    azimuth = counter * np.float32(math.pi * (3.0 - math.sqrt(5.0)))
    points = np.zeros((3, LANES), np.float32)
    points[:, :amount] = np.stack([radius * np.cos(azimuth), radius * np.sin(azimuth), height])
    return points


def split(value):
    high = value.astype(BF16)
    return high, (value - high.astype(F32)).astype(BF16)


def bdot(left, right):
    return jnp.dot(left, right, preferred_element_type=F32)


def two_terms(high, low):
    return jnp.concatenate(
        [
            jnp.concatenate([high, high], axis=1),
            jnp.concatenate([low, jnp.zeros_like(low)], axis=1),
        ],
        axis=0,
    )


def three_terms(value):
    first = value.astype(BF16)
    rest = value - first.astype(F32)
    second = rest.astype(BF16)
    third = (rest - second.astype(F32)).astype(BF16)
    return jnp.concatenate(
        [
            jnp.concatenate([first, first], axis=1),
            jnp.concatenate([second, second], axis=1),
            jnp.concatenate([third, jnp.zeros_like(third)], axis=1),
        ],
        axis=0,
    )


def dot_split(left, right):
    rows = left.shape[0]
    both = bdot(two_terms(*split(left)), jnp.concatenate(split(right), axis=0))
    return both[:rows] + both[rows:]


def dot_split_nt(left, right):
    rows = left.shape[0]
    both = lax.dot_general(
        two_terms(*split(left)),
        jnp.concatenate(split(right), axis=1),
        (((1,), (1,)), ((), ())),
        preferred_element_type=F32,
    )
    return both[:rows] + both[rows:]


def lay_points(cols_ref, rows_ref):
    for axis in range(3):
        row = rows_ref[axis : axis + 1, :]
        cols_ref[axis] = jnp.broadcast_to(row, (LANES, LANES)).T


def lay_surface(surface, cols_ref):
    total = jnp.zeros((LANES, LANES), F32)
    for axis in range(3):
        surface[axis] = -3.0 * cols_ref[axis]
        total = total + 2.25 * cols_ref[axis] * cols_ref[axis]
    surface[3] = total


def surface_distance(surface, place):
    square = place[0] * place[0] + place[1] * place[1] + place[2] * place[2] + SMOOTH2
    return (
        (square + surface[3])
        + place[0] * surface[0]
        + place[1] * surface[1]
        + place[2] * surface[2]
    )


SIDES = (-1, 1)
WIDTH = 3


def edge(side, size, width):
    return 0 if side < 0 else size - width


def landing(side, size, width):
    return 0 if side < 0 else size + width


def parcel_rows(size_x, size_y):
    tops = 3 * (size_x // 2) * (size_y // 2)
    leaves_x = 6 * WIDTH * size_y
    leaves_y = 6 * (size_x + 2 * WIDTH) * WIDTH
    near_x = leaves_x + 12 * size_y
    near_y = leaves_y + 12 * (size_x + 2)
    return (leaves_x, near_x, near_x + tops), (leaves_y, near_y, near_y + 3 * tops)


def lies_inside(axis, side):
    place = lax.axis_index(axis) + side
    return jnp.where((place >= 0) & (place < lax.axis_size(axis)), 1.0, 0.0)


def up_kernel(
    size_x,
    size_y,
    counts_ref,
    offsets_ref,
    strengths_ref,
    rows_ref,
    inverse_ref,
    pack_ref,
    leaf_ref,
    top_ref,
    matrix_ref,
    living_ref,
    *rest,
):
    parcels = rest[:2]
    check, surface, cols_ref, strong, inverse, arrived = rest[2:]
    copies = [
        pltpu.make_async_copy(source, target, arrived.at[k])
        for k, (source, target) in enumerate(
            (
                (offsets_ref, pack_ref.at[0:3]),
                (strengths_ref, strong),
                (inverse_ref, inverse),
            )
        )
    ]
    for copy in copies:
        copy.start()
    lay_points(cols_ref, rows_ref)
    lay_surface(surface, cols_ref)
    for copy in copies:
        copy.wait()
    point = [rows_ref[j : j + 1, :] for j in range(3)]
    lane = lax.broadcasted_iota(jnp.int32, (1, LANES), 1)
    expansion = inverse_ref.shape[0]
    matrix_ref[...] = jnp.zeros_like(matrix_ref)
    matrix_ref[:expansion, :expansion] = inverse[...]

    def one_column(i, j):
        row = [pack_ref[c, i, pl.ds(j, 1), :] for c in range(3)]
        count = counts_ref[i, pl.ds(j, 1), :]
        living = jnp.concatenate(
            [
                jnp.where(lane < jnp.broadcast_to(count[:, k : k + 1], (1, LANES)), 1.0, 0.0)
                for k in range(2)
            ],
            axis=1,
        )
        living_ref[i, pl.ds(j, 1), :] = living
        charges = []
        for c in range(3):
            value = STRENGTH_SCALE * strong[c, i, pl.ds(j, 1), :] * living
            pack_ref[3 + c, i, pl.ds(j, 1), :] = value
            charges.append(value)
        charge = jnp.concatenate(charges + [jnp.zeros((5, 2 * LANES), F32)], axis=0)
        for half in range(2):
            lanes = slice(half * LANES, (half + 1) * LANES)
            place = [row[axis][:, lanes] for axis in range(3)]
            kernel = lax.rsqrt(surface_distance(surface, place))
            both = jnp.concatenate(split(charge[:, lanes]), axis=0)
            total = lax.dot_general(
                jnp.concatenate([both, both], axis=1),
                jnp.concatenate(split(kernel), axis=1),
                (((1,), (1,)), ((), ())),
                preferred_element_type=F32,
            )
            total = total[:8] + total[8:]
            for c in range(3):
                check[half, c, i, pl.ds(j, 1), :] = total[c : c + 1]

    def columns(index, carry):
        for k in range(4):
            step = index * 4 + k
            one_column(step // size_y, step % size_y)
        return carry

    lax.fori_loop(0, size_x * size_y // 4, columns, 0)
    matrix = matrix_ref[...]
    rows = 6 * size_x * size_y
    charges = 0.5 * dot_split_nt(check[...].reshape(rows, LANES), matrix)
    leaf_ref[...] = charges.reshape(2, 3, size_x, size_y, LANES)
    half_x = size_x // 2
    half_y = size_y // 2
    count = 3 * half_x * half_y
    padding = -count % 16
    filler = [jnp.zeros((padding, LANES), F32)] if padding else []
    total = jnp.zeros((count + padding, LANES), F32)
    for a in range(2):
        for b in range(2):
            for e in range(2):
                shift = (a - 0.5, b - 0.5, e - 0.5)
                delta = [
                    3.0 * point[axis] - shift[axis] - 0.9 * cols_ref[axis] for axis in range(3)
                ]
                table = lax.rsqrt(
                    delta[0] * delta[0] + delta[1] * delta[1] + delta[2] * delta[2] + SMOOTH2
                )
                pieces = [
                    leaf_ref[e, c, 2 * x + a, pl.ds(b, half_y, stride=2), :]
                    for c in range(3)
                    for x in range(half_x)
                ]
                total = total + dot_split(jnp.concatenate(pieces + filler, axis=0), table)
    tops = dot_split_nt(total, matrix)[:count]
    top_ref[...] = tops
    (_, second, end), _ = parcel_rows(size_x, size_y)
    for side, parcel in zip(SIDES, parcels):
        row = 0
        start = edge(side, size_x, WIDTH)
        for depth in range(2):
            for c in range(3):
                for x in range(start, start + WIDTH):
                    parcel[row : row + size_y] = leaf_ref[depth, c, x]
                    row += size_y
        for c in range(6):
            for half in range(2):
                lanes = slice(half * LANES, (half + 1) * LANES)
                parcel[row : row + size_y] = pack_ref[c, edge(side, size_x, 1), :, lanes]
                row += size_y
        parcel[second:end] = tops


def turn_kernel(
    size_x, size_y, leaf_ref, pack_ref, top_ref, below_ref, above_ref, low_ref, high_ref, tops_ref
):
    (_, near_x, end_x), (_, near_y, _) = parcel_rows(size_x, size_y)
    count = end_x - near_x
    for place, ref in ((0, below_ref), (2, above_ref)):
        tops_ref[place * count : (place + 1) * count] = ref[near_x:end_x]
    tops_ref[count : 2 * count] = top_ref[...]
    inside = [lies_inside("gx", side) for side in SIDES]
    for side, parcel in zip(SIDES, (low_ref, high_ref)):
        row = 0
        start = edge(side, size_y, WIDTH)
        for depth in range(2):
            for c in range(3):
                for x in range(-WIDTH, size_x + WIDTH):
                    if 0 <= x < size_x:
                        value = leaf_ref[depth, c, x, start : start + WIDTH]
                    else:
                        which = int(x >= size_x)
                        ref = (below_ref, above_ref)[which]
                        cell = x - size_x if which else x + WIDTH
                        at = ((depth * 3 + c) * WIDTH + cell) * size_y + start
                        value = ref[at : at + WIDTH] * inside[which]
                    parcel[row : row + WIDTH] = value
                    row += WIDTH
        start = edge(side, size_y, 1)
        first, _, _ = parcel_rows(size_x, size_y)[0]
        for c in range(6):
            for x in range(-1, size_x + 1):
                for half in range(2):
                    if 0 <= x < size_x:
                        lanes = slice(half * LANES, (half + 1) * LANES)
                        value = pack_ref[c, x, start : start + 1, lanes]
                    else:
                        which = int(x >= size_x)
                        ref = (below_ref, above_ref)[which]
                        at = first + (c * 2 + half) * size_y + start
                        value = ref[at : at + 1]
                        if c >= 3:
                            value = value * inside[which]
                    parcel[row : row + 1] = value
                    row += 1
        parcel[near_y : near_y + 3 * count] = tops_ref[...]


def near_masks():
    row = lax.broadcasted_iota(jnp.int32, (16, 2 * LANES), 0)
    lane = lax.broadcasted_iota(jnp.int32, (1, 2 * LANES), 1)
    return row // 3, row % 3, jnp.where(lane < LANES, -0.5, 0.5).astype(F32)


def prepare_column(row, slot, masks, spread, moments):
    level, kind, lift = masks
    x, y, z = row[0], row[1], row[2] + lift
    square = x * x + y * y + z * z
    values = jnp.concatenate(
        [-2.0 * x, -2.0 * y, -2.0 * z, square, jnp.zeros((4, 2 * LANES), F32)], axis=0
    )
    first = values.astype(BF16).astype(F32)
    second = (values - first).astype(BF16).astype(F32)
    terms = jnp.concatenate(
        [first, second, (values - first) - second, jnp.zeros_like(values)], axis=0
    ).T.astype(BF16)
    term = lax.broadcasted_iota(jnp.int32, (32, 4 * LANES), 0)
    place = lax.broadcasted_iota(jnp.int32, (32, 4 * LANES), 1) // LANES
    chosen = jnp.where((term % 8 == place) & (term < 24), 1.0, 0.0).astype(BF16)
    laid = bdot(terms, chosen)
    for axis in range(4):
        spread[slot, axis] = laid[:, axis * LANES : (axis + 1) * LANES]

    def wide(value):
        return jnp.broadcast_to(value, (16, 2 * LANES))

    charge = jnp.where(
        kind == 0, wide(row[3]), jnp.where(kind == 1, wide(row[4]), wide(row[5]))
    )
    charge = jnp.where(level < 5, charge, 0.0)
    factor = jnp.where(level == 3, wide(z), wide(square))
    factor = jnp.where(level == 2, wide(y), factor)
    factor = jnp.where(level == 1, wide(x), factor)
    moments[slot, 0] = charge * jnp.where(level == 0, 1.0, factor)
    last = jnp.where(level == 4, charge, 0.0)
    moments[slot, 1] = jnp.where(level == 1, charge, last * wide(2.0 * x))
    moments[slot, 2] = jnp.where(level == 2, charge, last * wide(2.0 * y))
    moments[slot, 3] = last


def shifted(moments, slot, shift_x, shift_y):
    return (
        moments[slot, 0]
        + shift_x * moments[slot, 1]
        + shift_y * moments[slot, 2]
        + (shift_x * shift_x + shift_y * shift_y) * moments[slot, 3]
    )


def pair_cubes(target, slot, shift_x, shift_y, spread):
    x = target[0] - shift_x
    y = target[1] - shift_y
    z = target[2]
    square = x * x + y * y + z * z + SMOOTH2
    result = []
    for half in range(2):
        part = slice(half * LANES, (half + 1) * LANES)
        highs = []
        lows = []
        for side in range(2):
            lanes = slice(side * LANES, (side + 1) * LANES)
            distance = (
                (square[:, lanes] + spread[slot, 3, part, :])
                + x[:, lanes] * spread[slot, 0, part, :]
                + y[:, lanes] * spread[slot, 1, part, :]
                + z[:, lanes] * spread[slot, 2, part, :]
            )
            inverse = lax.rsqrt(distance)
            high, low = split(inverse * inverse * inverse)
            highs.append(high)
            lows.append(low)
        result.append((jnp.concatenate(highs, axis=1), jnp.concatenate(lows, axis=1)))
    return result


def near_sums(target, blocks, spread, moments):
    total = jnp.zeros((48, 2 * LANES), F32)
    for slot, shift_x, shift_y in blocks:
        weight = shifted(moments, slot, shift_x, shift_y)
        for half, terms in enumerate(pair_cubes(target, slot, shift_x, shift_y, spread)):
            part = slice(half * LANES, (half + 1) * LANES)
            total = total + bdot(
                three_terms(weight[:, part]), jnp.concatenate(terms, axis=0)
            )
    return total[:16] + total[16:32] + total[32:]


def run_tasks(size_y, tasks, table_ref, pack_ref, out_ref, lift, spread, moments, adds):
    for start, amount, sources in tasks:
        together = 1
        while together * sources < 12 and amount % (2 * together) == 0:
            together *= 2

        def one(index, start, sources):
            at = start + index * (2 + 3 * sources)
            i = table_ref[at]
            j = table_ref[at + 1]
            target = [pack_ref[c, i, pl.ds(j, 1), :] for c in range(3)]
            target[2] = target[2] + lift
            blocks = [
                (
                    table_ref[at + 2 + 3 * k],
                    table_ref[at + 3 + 3 * k].astype(F32),
                    table_ref[at + 4 + 3 * k].astype(F32),
                )
                for k in range(sources)
            ]
            return i * size_y + j, near_sums(target, blocks, spread, moments)

        def step(index, carry, start=start, sources=sources, together=together):
            found = [one(index * together + k, start, sources) for k in range(together)]
            for place, total in found:
                out_ref[place] = total + out_ref[place] if adds else total
            return carry

        lax.fori_loop(0, amount // together, step, 0)


def own_kernel(size_x, size_y, tasks, table_ref, pack_ref, out_ref, spread, moments):
    masks = near_masks()

    def prepare(index, carry):
        for k in range(4):
            slot = index * 4 + k
            row = [pack_ref[c, slot // size_y, pl.ds(slot % size_y, 1), :] for c in range(6)]
            prepare_column(row, slot, masks, spread, moments)
        return carry

    lax.fori_loop(0, size_x * size_y // 4, prepare, 0)
    out_ref[...] = jnp.zeros_like(out_ref)

    def places(i, j):
        row = [pack_ref[c, i, pl.ds(j, 1), :] for c in range(3)]
        return [row[0], row[1], row[2] + masks[2]]

    def one(at, others):
        i = table_ref[at]
        j = table_ref[at + 1]
        slot = i * size_y + j
        total = near_sums(places(i, j), [(slot, 0.0, 0.0)], spread, moments)
        found = []
        for k in range(others):
            i, j, away_x, away_y = [table_ref[at + 2 + 4 * k + m] for m in range(4)]
            away_x = away_x.astype(F32)
            away_y = away_y.astype(F32)
            other = i * size_y + j
            (h_first, l_first), (h_second, l_second) = pair_cubes(
                places(i, j), slot, -away_x, -away_y, spread
            )
            high = jnp.concatenate([h_first, h_second], axis=0)
            low = jnp.concatenate([l_first, l_second], axis=0)
            there = bdot(
                three_terms(shifted(moments, slot, -away_x, -away_y)),
                jnp.concatenate([high, low], axis=0),
            )
            found.append((other, there[:16] + there[16:32] + there[32:]))
            here = lax.dot_general(
                three_terms(shifted(moments, other, away_x, away_y)),
                jnp.concatenate([high, low], axis=1),
                (((1,), (1,)), ((), ())),
                preferred_element_type=F32,
            )
            total = total + here[:16] + here[16:32] + here[32:]
        found.append((slot, total))
        return found

    for start, amount, others in tasks:
        together = 3 if amount % 3 == 0 else 1

        def step(index, carry, start=start, others=others, together=together):
            found = []
            for k in range(together):
                found += one(start + (index * together + k) * (2 + 4 * others), others)
            for place, total in found:
                out_ref[place] += total
            return carry

        lax.fori_loop(0, amount // together, step, 0)


def halo_kernel(size_x, size_y, axis, tasks, table_ref, before_ref, pack_ref, *rest):
    parcels = rest[:2]
    out_ref, spread, moments, held = rest[2:]
    masks = near_masks()
    out_ref[...] = before_ref[...]
    ends = parcel_rows(size_x, size_y)[0 if axis == "gx" else 1]
    cells = size_y if axis == "gx" else size_x + 2
    for number, (side, parcel) in enumerate(zip(SIDES, parcels)):
        row = ends[0]
        inside = lies_inside(axis, side)
        for c in range(6):
            for half in range(2):
                lanes = slice(half * LANES, (half + 1) * LANES)
                if axis == "gx":
                    value = parcel[row : row + cells]
                    row += cells
                else:
                    value = parcel[pl.ds(ends[0] + c * 2 * cells + half, cells, stride=2), :]
                held[c, number * cells : (number + 1) * cells, lanes] = (
                    value if c < 3 else value * inside
                )

    def prepare(index, carry):
        for k in range(4):
            slot = index * 4 + k
            row = [held[c, pl.ds(slot, 1), :] for c in range(6)]
            prepare_column(row, slot, masks, spread, moments)
        return carry

    lax.fori_loop(0, 2 * cells // 4, prepare, 0)
    run_tasks(size_y, tasks, table_ref, pack_ref, out_ref, masks[2], spread, moments, True)


def near_tables(size_x, size_y):
    kinds = ({}, {}, {})
    for i in range(size_x):
        for j in range(size_y):
            pairs = []
            for x, y in ((0, 1), (1, -1), (1, 0), (1, 1)):
                if i + x < size_x and 0 <= j + y < size_y:
                    pairs += [i + x, j + y, x, y]
            kinds[0].setdefault(len(pairs) // 4, []).append([i, j] + pairs)
            found = ([], [], [])
            for x in (-1, 0, 1):
                for y in (-1, 0, 1):
                    if not 0 <= j + y < size_y:
                        found[2].extend([int(y > 0) * (size_x + 2) + i + x + 1, x, y])
                    elif not 0 <= i + x < size_x:
                        found[1].extend([int(x > 0) * size_y + j + y, x, y])
            for groups, sources in zip(kinds[1:], found[1:]):
                if sources:
                    groups.setdefault(len(sources) // 3, []).append([i, j] + sources)
    result = []
    flat = []
    for groups in kinds:
        tasks = []
        for sources in sorted(groups, reverse=True):
            tasks.append((len(flat), len(groups[sources]), sources))
            for entry in groups[sources]:
                flat += entry
        result.append(tasks)
    return np.array(flat, np.int32), result


def leaf_kernel(size_x, size_y, own_ref, rows_ref, *rest):
    parcels = rest[:4]
    down_ref, base, leaf_ref, cols_ref = rest[4:]
    lay_points(cols_ref, rows_ref)
    for depth in range(2):
        for c in range(3):
            for x in range(size_x):
                leaf_ref[depth, c, WIDTH + x, WIDTH : WIDTH + size_y] = own_ref[depth, c, x]
    for side, parcel in zip(SIDES, parcels[:2]):
        inside = lies_inside("gx", side)
        start = landing(side, size_x, WIDTH)
        row = 0
        for depth in range(2):
            for c in range(3):
                for x in range(start, start + WIDTH):
                    leaf_ref[depth, c, x, WIDTH : WIDTH + size_y] = (
                        parcel[row : row + size_y] * inside
                    )
                    row += size_y
    for side, parcel in zip(SIDES, parcels[2:]):
        inside = lies_inside("gy", side)
        start = landing(side, size_y, WIDTH)
        row = 0
        for depth in range(2):
            for c in range(3):
                for x in range(size_x + 2 * WIDTH):
                    leaf_ref[depth, c, x, start : start + WIDTH] = (
                        parcel[row : row + WIDTH] * inside
                    )
                    row += WIDTH
    for axis in range(3):
        base[axis] = 0.9 * rows_ref[axis : axis + 1, :] - 0.9 * cols_ref[axis]
    down_ref[...] = jnp.zeros_like(down_ref)
    odd_y = lax.broadcasted_iota(jnp.int32, (size_y, LANES), 0) % 2
    near_y = {-3: jnp.where(odd_y == 1, 1.0, 0.0), 3: jnp.where(odd_y == 0, 1.0, 0.0)}

    def one_row(shift_x, shifts_y):
        dx = base[0] - shift_x.astype(F32)
        tables = []
        charges = []
        for shift_y in shifts_y:
            dy = base[1] - float(shift_y)
            flat = dx * dx + dy * dy + SMOOTH2
            table = []
            for shift_z in (-1, 0, 1):
                dz = base[2] - float(shift_z)
                table.append(lax.rsqrt(flat + dz * dz).astype(BF16))
            tables.append(jnp.concatenate([table[1], table[0]], axis=1))
            tables.append(jnp.concatenate([table[2], table[1]], axis=1))
            for depth in range(2):
                pieces = []
                for c in range(3):
                    for x in range(size_x):
                        near_x = (shift_x > -3) if x % 2 == 0 else (shift_x < 3)
                        piece = jnp.where(
                            near_x,
                            leaf_ref[depth, c, x + 3 + shift_x, 3 + shift_y : 3 + shift_y + size_y],
                            0.0,
                        )
                        if abs(shift_y) == 3:
                            piece = piece * near_y[shift_y]
                        pieces.append(piece)
                charges.append(jnp.concatenate(pieces, axis=0).astype(BF16))
        down_ref[...] += bdot(
            jnp.concatenate(charges, axis=1), jnp.concatenate(tables, axis=0)
        )

    def outer(step, carry):
        one_row(jnp.where(step < 2, step - 3, step), (-3, -2, -1, 0, 1, 2, 3))
        return carry

    def inner(step, carry):
        one_row(step - 1, (-3, -2, 2, 3))
        return carry

    lax.fori_loop(0, 4, outer, 0)
    lax.fori_loop(0, 3, inner, 0)


def far_kernel(
    size_x,
    size_y,
    tops_x,
    tops_y,
    chunk,
    slots_at,
    slot_ref,
    living_ref,
    down_ref,
    tops_ref,
    near_ref,
    pack_ref,
    rows_ref,
    inverse_ref,
    out_ref,
    base,
    windows,
    down,
    top_down,
    local,
    surface,
    squares_y,
    cols_ref,
):
    half_x = size_x // 2
    half_y = size_y // 2
    group = half_x * 4
    across = tops_x + half_x - 1
    along = tops_y + half_y - 1
    point = [rows_ref[j : j + 1, :] for j in range(3)]
    lay_points(cols_ref, rows_ref)
    for axis in range(3):
        base[axis] = 1.8 * point[axis] - 1.8 * cols_ref[axis]

    windows[...] = jnp.zeros_like(windows)
    lanes_x = tops_x // half_x
    lanes_y = tops_y // half_y
    mine_x = lax.axis_index("gx")
    mine_y = lax.axis_index("gy")

    def place(device, carry):
        place_x = device // lanes_y
        place_y = device % lanes_y
        away_x = lax.rem(place_x - mine_x + lanes_x, lanes_x)
        away_y = lax.rem(place_y - mine_y + lanes_y, lanes_y)
        slot = slot_ref[slots_at + away_x * lanes_y + away_y]
        i = place_x * half_x
        j = place_y * half_y
        for c in range(3):
            for p in range(half_x):
                for q in range(half_y):
                    row = tops_ref[slot, (c * half_x + p) * half_y + q, :][None]
                    for x in range(half_x):
                        windows[
                            i + p + half_x - 1 - x,
                            pl.ds((j + q + half_y - 1) * group + x * 4 + c, 1),
                            :,
                        ] = row
        return carry

    lax.fori_loop(0, lanes_x * lanes_y, place, 0)
    first_x = mine_x * half_x
    first_y = mine_y * half_y
    top_down[...] = jnp.zeros_like(top_down)
    parts = -(-along // chunk)

    def square_y(wy, carry):
        dy = base[1] + 2.0 * (first_y - (wy - (half_y - 1))).astype(F32)
        squares_y[wy] = dy * dy
        return carry

    lax.fori_loop(0, parts * chunk, square_y, 0)

    def top_row(step):
        wx = step // parts
        start = (step % parts) * chunk
        gap_x = first_x - (wx - (half_x - 1))
        dx = base[0] + 2.0 * gap_x.astype(F32)
        squares = dx * dx + base[2] * base[2] + SMOOTH2
        tables = []
        pieces = []
        for k in range(chunk):
            wy = start + k
            gap_y = first_y - (wy - (half_y - 1))
            distant = (jnp.abs(gap_x) >= 2) | (jnp.abs(gap_y) >= 2)
            tables.append(lax.rsqrt(squares + squares_y[wy]).astype(BF16))
            rows = windows[wx, pl.ds(wy * group, half_y * group), :]
            pieces.append(jnp.where(distant, rows, 0.0))
        return bdot(
            jnp.concatenate(pieces, axis=1).astype(BF16), jnp.concatenate(tables, axis=0)
        )

    together = 3
    steps = across * parts

    def top_rows(index, carry):
        found = [top_row(index * together + k) for k in range(together)]
        top_down[...] += sum(found[1:], found[0])
        return carry

    lax.fori_loop(0, steps // together, top_rows, 0)
    for step in range(steps - steps % together, steps):
        top_down[...] += top_row(jnp.int32(step))
    matrix = inverse_ref[...]
    top_local = dot_split_nt(top_down[...], matrix)
    lay_surface(surface, cols_ref)
    down[...] = down_ref[...]
    for a in range(2):
        for b in range(2):
            for e in range(2):
                offset = (a - 0.5, b - 0.5, e - 0.5)
                delta = [
                    offset[axis] + 0.9 * point[axis] - 3.0 * cols_ref[axis] for axis in range(3)
                ]
                table = lax.rsqrt(
                    delta[0] * delta[0] + delta[1] * delta[1] + delta[2] * delta[2] + SMOOTH2
                )
                inherited = dot_split(top_local, table)
                for y in range(half_y):
                    for x in range(half_x):
                        for c in range(3):
                            row = (c * size_x + 2 * x + a) * size_y + 2 * y + b
                            down[row : row + 1, e * LANES : (e + 1) * LANES] += inherited[
                                y * group + x * 4 + c : y * group + x * 4 + c + 1
                            ]
    for e in range(2):
        part = 0.5 * dot_split_nt(down[:, e * LANES : (e + 1) * LANES], matrix)
        local[e] = part.reshape(3, size_x, size_y, LANES)

    level = lax.broadcasted_iota(jnp.int32, (16, LANES), 0) // 3
    kind = lax.broadcasted_iota(jnp.int32, (16, LANES), 0) % 3
    patterns = []
    for half in range(2):
        x = 1.5 * point[0]
        y = 1.5 * point[1]
        z = 1.5 * point[2] + (half - 0.5)
        pattern = jnp.where(level == 0, 1.0, 0.0)
        for power, value in enumerate((x, y, z, x * x + y * y + z * z)):
            value = jnp.broadcast_to(value, (16, LANES))
            pattern = jnp.where(level == power + 1, value, pattern)
        patterns.append(pattern)

    def one_column(index):
        i = index // size_y
        j = index % size_y
        row = [pack_ref[c, i, pl.ds(j, 1), :] for c in range(3)]
        alive = living_ref[i, pl.ds(j, 1), :]
        results = []
        for half in range(2):
            lanes = slice(half * LANES, (half + 1) * LANES)
            place = [row[axis][:, lanes] for axis in range(3)]
            inverse = lax.rsqrt(surface_distance(surface, place))
            high, low = split(inverse * inverse * inverse)
            charge = [
                jnp.broadcast_to(local[half, c, i, pl.ds(j, 1), :], (16, LANES)) for c in range(3)
            ]
            weight = patterns[half] * jnp.where(
                kind == 0, charge[0], jnp.where(kind == 1, charge[1], charge[2])
            )
            total = bdot(two_terms(*split(weight)), jnp.concatenate([high, low], axis=0))
            total = total[:16] + total[16:] + near_ref[index, :, lanes]
            place[2] = place[2] + (half - 0.5)
            living = alive[:, lanes]
            square = (
                place[0] * place[0] + place[1] * place[1] + place[2] * place[2] + SMOOTH2
            )
            potential = (
                square * total[0:3]
                - 2.0
                * (place[0] * total[3:6] + place[1] * total[6:9] + place[2] * total[9:12])
                + total[12:15]
            ) * living
            slopes = [
                (total[3 + 3 * axis : 6 + 3 * axis] - place[axis] * total[0:3]) * living
                for axis in range(3)
            ]
            results.append((potential, slopes))
        potential = jnp.concatenate([results[0][0], results[1][0]], axis=1)
        slopes = [
            jnp.concatenate([results[0][1][axis], results[1][1][axis]], axis=1)
            for axis in range(3)
        ]
        for c in range(3):
            out_ref[c, i, pl.ds(j, 1), :] = potential[c : c + 1]
            for axis in range(3):
                out_ref[3 + 3 * c + axis, i, pl.ds(j, 1), :] = slopes[axis][c : c + 1]

    def columns(index, carry):
        for k in range(4):
            one_column(index * 4 + k)
        return carry

    lax.fori_loop(0, size_x * size_y // 4, columns, 0)


def moved(array, axis, step):
    count = lax.axis_size(axis)
    return lax.ppermute(array, axis, [((i + step) % count, i) for i in range(count)])


def widening(away, axis, count):
    half = 1
    plan = []
    while 2 * half + 1 < count:
        missing = count - 2 * half - 1
        if missing <= 2 * half + 1:
            first = -((missing - 1) // 2)
            steps = (half + 1 - first,)
        else:
            first = -half
            missing = 2 * half + 1
            steps = (missing, -missing)
        picks = []
        known = []
        for places in away:
            pick = [k for k, place in enumerate(places) if 0 <= place[axis] - first < missing]
            picks.append(pick)
            known += [places[k] for k in pick]
        plan.append((steps, picks))
        for step in steps:
            away = away + [
                [tuple(p + step * (k == axis) for k, p in enumerate(place)) for place in known]
            ]
        half = half + steps[0] if len(steps) == 2 else count
    return plan, away


ROUND = [[(x, y) for x in (-1, 0, 1)] for y in (-1, 0, 1)]


def top_slots(lanes_x, lanes_y):
    _, away = widening(ROUND, 1, lanes_y)
    _, away = widening(away, 0, lanes_x)
    slots = np.zeros((lanes_x, lanes_y), np.int32)
    places = [place for held in away for place in held]
    for slot, (x, y) in reversed(list(enumerate(places))):
        slots[x % lanes_x, y % lanes_y] = slot
    return slots


def widened(blocks, away, axis, name):
    plan, final = widening(away, axis, lax.axis_size(name))
    for steps, picks in plan:
        sent = []
        for array, places, pick in zip(blocks, away, picks):
            if len(pick) == len(places):
                sent.append(array)
            else:
                size = array.shape[0] // len(places)
                sent += [array[k * size : (k + 1) * size] for k in pick]
        whole = sent[0] if len(sent) == 1 else jnp.concatenate(sent, axis=0)
        blocks = blocks + [moved(whole, name, step) for step in steps]
        away = final[: len(blocks)]
    return blocks, final


def body(offsets, strengths, counts, check_inverse):
    size_x, size_y, depth = counts.shape
    expansion = check_inverse.shape[0]
    half_x = size_x // 2
    half_y = size_y // 2
    lanes_x = lax.axis_size("gx")
    lanes_y = lax.axis_size("gy")
    tops_x = lanes_x * half_x
    tops_y = lanes_y * half_y
    points = sphere_points(expansion)
    rows = jnp.asarray(np.concatenate([points, np.zeros((5, LANES), np.float32)], axis=0))
    def params(mebibytes):
        return pltpu.CompilerParams(vmem_limit_bytes=mebibytes * 2**20)

    smem = pl.BlockSpec(memory_space=pltpu.SMEM)
    vmem = pl.BlockSpec(memory_space=pltpu.VMEM)
    hbm = pl.BlockSpec(memory_space=pltpu.HBM)

    def cost(flops):
        return pl.CostEstimate(flops=flops, bytes_accessed=10**6, transcendentals=0)

    top_rows = 3 * half_x * half_y
    (_, _, end_x), (_, near_y, end_y) = parcel_rows(size_x, size_y)
    made = pl.pallas_call(
        functools.partial(up_kernel, size_x, size_y),
        out_shape=(
            jax.ShapeDtypeStruct((6, size_x, size_y, depth * LANES), F32),
            jax.ShapeDtypeStruct((2, 3, size_x, size_y, LANES), F32),
            jax.ShapeDtypeStruct((top_rows, LANES), F32),
            jax.ShapeDtypeStruct((LANES, LANES), F32),
            jax.ShapeDtypeStruct((size_x, size_y, depth * LANES), F32),
            *[jax.ShapeDtypeStruct((end_x, LANES), F32)] * 2,
        ),
        in_specs=[vmem, hbm, hbm, vmem, hbm],
        out_specs=(vmem,) * 7,
        scratch_shapes=[
            pltpu.VMEM((2, 3, size_x, size_y, LANES), F32),
            pltpu.VMEM((4, LANES, LANES), F32),
            pltpu.VMEM((3, LANES, LANES), F32),
            pltpu.VMEM(strengths.shape, F32),
            pltpu.VMEM(check_inverse.shape, F32),
            pltpu.SemaphoreType.DMA((3,)),
        ],
        compiler_params=params(12),
        cost_estimate=cost(6 * 10**9),
        name="up",
    )(counts, offsets, strengths, rows, check_inverse)
    pack, leaf_charges, top_charges, matrix, living, to_below, to_above = made
    below = moved(to_above, "gx", -1)
    above = moved(to_below, "gx", 1)

    table, (own_tasks, *beside) = near_tables(size_x, size_y)
    slots_at = len(table)
    slots = top_slots(lanes_x, lanes_y)
    table = jnp.asarray(np.concatenate([table, slots.reshape(-1)]))
    near_shape = jax.ShapeDtypeStruct((size_x * size_y, 16, 2 * LANES), F32)
    own = pl.pallas_call(
        functools.partial(own_kernel, size_x, size_y, own_tasks),
        out_shape=near_shape,
        in_specs=[smem, vmem],
        out_specs=vmem,
        scratch_shapes=[
            pltpu.VMEM((size_x * size_y, 4, 2 * LANES, LANES), F32),
            pltpu.VMEM((size_x * size_y, 4, 16, 2 * LANES), F32),
        ],
        compiler_params=params(28),
        cost_estimate=cost(3 * 10**10),
        name="own",
    )(table, pack)

    to_low, to_high, tops = pl.pallas_call(
        functools.partial(turn_kernel, size_x, size_y),
        out_shape=(
            jax.ShapeDtypeStruct((end_y, LANES), F32),
            jax.ShapeDtypeStruct((end_y, LANES), F32),
            jax.ShapeDtypeStruct((3 * top_rows, LANES), F32),
        ),
        in_specs=[vmem] * 5,
        out_specs=(vmem,) * 3,
        compiler_params=params(12),
        cost_estimate=cost(10**9),
        name="turn",
    )(leaf_charges, pack, top_charges, below, above)
    low = moved(to_high, "gy", -1)
    high = moved(to_low, "gy", 1)
    blocks, away = widened(
        [low[near_y:], tops, high[near_y:]],
        ROUND,
        1,
        "gy",
    )

    def beside_near(axis, before, parcels):
        tasks = beside[0 if axis == "gx" else 1]
        columns = 2 * (size_y if axis == "gx" else size_x + 2)
        return pl.pallas_call(
            functools.partial(halo_kernel, size_x, size_y, axis, tasks),
            out_shape=near_shape,
            in_specs=[smem] + [vmem] * 4,
            out_specs=vmem,
            scratch_shapes=[
                pltpu.VMEM((columns, 4, 2 * LANES, LANES), F32),
                pltpu.VMEM((columns, 4, 16, 2 * LANES), F32),
                pltpu.VMEM((6, columns, 2 * LANES), F32),
            ],
            compiler_params=params(20),
            cost_estimate=cost(10**10),
            name="beside_" + axis,
        )(table, before, pack, *parcels)

    near = beside_near("gx", own, (below, above))
    blocks, away = widened(blocks, away, 0, "gx")
    blocks = jnp.concatenate(blocks, axis=0).reshape(-1, top_rows, LANES)
    near = beside_near("gy", near, (low, high))

    down = pl.pallas_call(
        functools.partial(leaf_kernel, size_x, size_y),
        out_shape=jax.ShapeDtypeStruct((3 * size_x * size_y, 2 * LANES), F32),
        in_specs=[vmem] * 6,
        out_specs=vmem,
        scratch_shapes=[
            pltpu.VMEM((3, LANES, LANES), F32),
            pltpu.VMEM(
                (2, 3, size_x + 2 * WIDTH, size_y + 2 * WIDTH, LANES), F32
            ),
            pltpu.VMEM((3, LANES, LANES), F32),
        ],
        compiler_params=params(12),
        cost_estimate=cost(6 * 10**9),
        name="leaf",
    )(leaf_charges, rows, below, above, low, high)

    across = tops_x + half_x - 1
    along = tops_y + half_y - 1
    parts = -(-along // 20)
    chunk = -(-along // parts)
    return pl.pallas_call(
        functools.partial(far_kernel, size_x, size_y, tops_x, tops_y, chunk, slots_at),
        out_shape=jax.ShapeDtypeStruct((12, size_x, size_y, depth * LANES), F32),
        in_specs=[smem] + [vmem] * 7,
        out_specs=vmem,
        scratch_shapes=[
            pltpu.VMEM((3, LANES, LANES), F32),
            pltpu.VMEM((across, (parts * chunk + half_y - 1) * half_x * 4, LANES), F32),
            pltpu.VMEM((3 * size_x * size_y, 2 * LANES), F32),
            pltpu.VMEM((half_y * half_x * 4, LANES), F32),
            pltpu.VMEM((2, 3, size_x, size_y, LANES), F32),
            pltpu.VMEM((4, LANES, LANES), F32),
            pltpu.VMEM((parts * chunk, LANES, LANES), F32),
            pltpu.VMEM((3, LANES, LANES), F32),
        ],
        compiler_params=params(40),
        cost_estimate=cost(10**10),
        name="far",
    )(
        table,
        living,
        down,
        blocks,
        near,
        pack,
        rows,
        matrix,
    )


def solution(mesh):
    return jax.shard_map(
        body,
        mesh=mesh,
        in_specs=(P(None, "gx", "gy", None), P(None, "gx", "gy", None), P("gx", "gy", None), P()),
        out_specs=P(None, "gx", "gy", None),
        check_vma=False,
    )
```

```python
import functools
import math

import jax
import jax.numpy as jnp
import numpy as np
from jax import lax
from jax.experimental import pallas as pl
from jax.experimental.pallas import tpu as pltpu
from jax.sharding import PartitionSpec as P

SMOOTH2 = 0.01
STRENGTH_SCALE = 0.03
LANES = 128
F32 = jnp.float32
BF16 = jnp.bfloat16


def sphere_points(amount):
    counter = np.arange(amount, dtype=np.float32)
    height = (1.0 - (2.0 * counter + 1.0) / np.float32(amount)).astype(np.float32)
    radius = np.sqrt(np.maximum(1.0 - height * height, 0.0)).astype(np.float32)
    azimuth = counter * np.float32(math.pi * (3.0 - math.sqrt(5.0)))
    points = np.zeros((3, LANES), np.float32)
    points[:, :amount] = np.stack([radius * np.cos(azimuth), radius * np.sin(azimuth), height])
    return points


def split(value):
    high = value.astype(BF16)
    return high, (value - high.astype(F32)).astype(BF16)


def bdot(left, right):
    return jnp.dot(left, right, preferred_element_type=F32)


def two_terms(high, low):
    return jnp.concatenate(
        [
            jnp.concatenate([high, high], axis=1),
            jnp.concatenate([low, jnp.zeros_like(low)], axis=1),
        ],
        axis=0,
    )


def three_terms(value):
    first = value.astype(BF16)
    rest = value - first.astype(F32)
    second = rest.astype(BF16)
    third = (rest - second.astype(F32)).astype(BF16)
    return jnp.concatenate(
        [
            jnp.concatenate([first, first], axis=1),
            jnp.concatenate([second, second], axis=1),
            jnp.concatenate([third, jnp.zeros_like(third)], axis=1),
        ],
        axis=0,
    )


def dot_split(left, right):
    rows = left.shape[0]
    both = bdot(two_terms(*split(left)), jnp.concatenate(split(right), axis=0))
    return both[:rows] + both[rows:]


def dot_split_nt(left, right):
    rows = left.shape[0]
    both = lax.dot_general(
        two_terms(*split(left)),
        jnp.concatenate(split(right), axis=1),
        (((1,), (1,)), ((), ())),
        preferred_element_type=F32,
    )
    return both[:rows] + both[rows:]


def lay_points(cols_ref, rows_ref):
    for axis in range(3):
        row = rows_ref[axis : axis + 1, :]
        cols_ref[axis] = jnp.broadcast_to(row, (LANES, LANES)).T


def lay_surface(surface, cols_ref):
    total = jnp.zeros((LANES, LANES), F32)
    for axis in range(3):
        surface[axis] = -3.0 * cols_ref[axis]
        total = total + 2.25 * cols_ref[axis] * cols_ref[axis]
    surface[3] = total


def surface_distance(surface, place):
    square = place[0] * place[0] + place[1] * place[1] + place[2] * place[2] + SMOOTH2
    return (
        (square + surface[3])
        + place[0] * surface[0]
        + place[1] * surface[1]
        + place[2] * surface[2]
    )


SIDES = (-1, 1)
WIDTH = 3


def edge(side, size, width):
    return 0 if side < 0 else size - width


def landing(side, size, width):
    return 0 if side < 0 else size + width


def parcel_rows(size_x, size_y):
    tops = 3 * (size_x // 2) * (size_y // 2)
    leaves_x = 6 * WIDTH * size_y
    leaves_y = 6 * (size_x + 2 * WIDTH) * WIDTH
    near_x = leaves_x + 12 * size_y
    near_y = leaves_y + 12 * (size_x + 2)
    return (leaves_x, near_x, near_x + tops), (leaves_y, near_y, near_y + 3 * tops)


def lies_inside(axis, side):
    place = lax.axis_index(axis) + side
    return jnp.where((place >= 0) & (place < lax.axis_size(axis)), 1.0, 0.0)


def up_kernel(
    size_x,
    size_y,
    living_ref,
    offsets_ref,
    strengths_ref,
    rows_ref,
    matrix_ref,
    pack_ref,
    leaf_ref,
    top_ref,
    *rest,
):
    parcels = rest[:2]
    check, surface, cols_ref = rest[2:]
    lay_points(cols_ref, rows_ref)
    lay_surface(surface, cols_ref)
    point = [rows_ref[j : j + 1, :] for j in range(3)]
    pack_ref[0:3] = offsets_ref[...]

    def one_column(i, j):
        row = [offsets_ref[c, i, pl.ds(j, 1), :] for c in range(3)]
        living = living_ref[i, pl.ds(j, 1), :]
        charges = []
        for c in range(3):
            value = STRENGTH_SCALE * strengths_ref[c, i, pl.ds(j, 1), :] * living
            pack_ref[3 + c, i, pl.ds(j, 1), :] = value
            charges.append(value)
        charge = jnp.concatenate(charges + [jnp.zeros((5, 2 * LANES), F32)], axis=0)
        for half in range(2):
            lanes = slice(half * LANES, (half + 1) * LANES)
            place = [row[axis][:, lanes] for axis in range(3)]
            kernel = lax.rsqrt(surface_distance(surface, place))
            both = jnp.concatenate(split(charge[:, lanes]), axis=0)
            total = lax.dot_general(
                jnp.concatenate([both, both], axis=1),
                jnp.concatenate(split(kernel), axis=1),
                (((1,), (1,)), ((), ())),
                preferred_element_type=F32,
            )
            total = total[:8] + total[8:]
            for c in range(3):
                check[half, c, i, pl.ds(j, 1), :] = total[c : c + 1]

    def columns(index, carry):
        for k in range(4):
            step = index * 4 + k
            one_column(step // size_y, step % size_y)
        return carry

    lax.fori_loop(0, size_x * size_y // 4, columns, 0)
    matrix = matrix_ref[...]
    rows = 6 * size_x * size_y
    charges = 0.5 * dot_split_nt(check[...].reshape(rows, LANES), matrix)
    leaf_ref[...] = charges.reshape(2, 3, size_x, size_y, LANES)
    half_x = size_x // 2
    half_y = size_y // 2
    count = 3 * half_x * half_y
    padding = -count % 16
    filler = [jnp.zeros((padding, LANES), F32)] if padding else []
    total = jnp.zeros((count + padding, LANES), F32)
    for a in range(2):
        for b in range(2):
            for e in range(2):
                shift = (a - 0.5, b - 0.5, e - 0.5)
                delta = [
                    3.0 * point[axis] - shift[axis] - 0.9 * cols_ref[axis] for axis in range(3)
                ]
                table = lax.rsqrt(
                    delta[0] * delta[0] + delta[1] * delta[1] + delta[2] * delta[2] + SMOOTH2
                )
                pieces = [
                    leaf_ref[e, c, 2 * x + a, pl.ds(b, half_y, stride=2), :]
                    for c in range(3)
                    for x in range(half_x)
                ]
                total = total + dot_split(jnp.concatenate(pieces + filler, axis=0), table)
    tops = dot_split_nt(total, matrix)[:count]
    top_ref[...] = tops
    (_, second, end), _ = parcel_rows(size_x, size_y)
    for side, parcel in zip(SIDES, parcels):
        row = 0
        start = edge(side, size_x, WIDTH)
        for depth in range(2):
            for c in range(3):
                for x in range(start, start + WIDTH):
                    parcel[row : row + size_y] = leaf_ref[depth, c, x]
                    row += size_y
        for c in range(6):
            for half in range(2):
                lanes = slice(half * LANES, (half + 1) * LANES)
                parcel[row : row + size_y] = pack_ref[c, edge(side, size_x, 1), :, lanes]
                row += size_y
        parcel[second:end] = tops


def turn_kernel(
    size_x, size_y, leaf_ref, pack_ref, top_ref, below_ref, above_ref, low_ref, high_ref, tops_ref
):
    (_, near_x, end_x), (_, near_y, _) = parcel_rows(size_x, size_y)
    count = end_x - near_x
    for place, ref in ((0, below_ref), (2, above_ref)):
        tops_ref[place * count : (place + 1) * count] = ref[near_x:end_x]
    tops_ref[count : 2 * count] = top_ref[...]
    inside = [lies_inside("gx", side) for side in SIDES]
    for side, parcel in zip(SIDES, (low_ref, high_ref)):
        row = 0
        start = edge(side, size_y, WIDTH)
        for depth in range(2):
            for c in range(3):
                for x in range(-WIDTH, size_x + WIDTH):
                    if 0 <= x < size_x:
                        value = leaf_ref[depth, c, x, start : start + WIDTH]
                    else:
                        which = int(x >= size_x)
                        ref = (below_ref, above_ref)[which]
                        cell = x - size_x if which else x + WIDTH
                        at = ((depth * 3 + c) * WIDTH + cell) * size_y + start
                        value = ref[at : at + WIDTH] * inside[which]
                    parcel[row : row + WIDTH] = value
                    row += WIDTH
        start = edge(side, size_y, 1)
        first, _, _ = parcel_rows(size_x, size_y)[0]
        for c in range(6):
            for x in range(-1, size_x + 1):
                for half in range(2):
                    if 0 <= x < size_x:
                        lanes = slice(half * LANES, (half + 1) * LANES)
                        value = pack_ref[c, x, start : start + 1, lanes]
                    else:
                        which = int(x >= size_x)
                        ref = (below_ref, above_ref)[which]
                        at = first + (c * 2 + half) * size_y + start
                        value = ref[at : at + 1]
                        if c >= 3:
                            value = value * inside[which]
                    parcel[row : row + 1] = value
                    row += 1
        parcel[near_y : near_y + 3 * count] = tops_ref[...]


def near_masks():
    row = lax.broadcasted_iota(jnp.int32, (16, 2 * LANES), 0)
    lane = lax.broadcasted_iota(jnp.int32, (1, 2 * LANES), 1)
    return row // 3, row % 3, jnp.where(lane < LANES, -0.5, 0.5).astype(F32)


def prepare_column(row, slot, masks, spread, moments):
    level, kind, lift = masks
    x, y, z = row[0], row[1], row[2] + lift
    square = x * x + y * y + z * z
    values = jnp.concatenate(
        [-2.0 * x, -2.0 * y, -2.0 * z, square, jnp.zeros((4, 2 * LANES), F32)], axis=0
    )
    first = values.astype(BF16).astype(F32)
    second = (values - first).astype(BF16).astype(F32)
    terms = jnp.concatenate(
        [first, second, (values - first) - second, jnp.zeros_like(values)], axis=0
    ).T.astype(BF16)
    term = lax.broadcasted_iota(jnp.int32, (32, 4 * LANES), 0)
    place = lax.broadcasted_iota(jnp.int32, (32, 4 * LANES), 1) // LANES
    chosen = jnp.where((term % 8 == place) & (term < 24), 1.0, 0.0).astype(BF16)
    laid = bdot(terms, chosen)
    for axis in range(4):
        spread[slot, axis] = laid[:, axis * LANES : (axis + 1) * LANES]

    def wide(value):
        return jnp.broadcast_to(value, (16, 2 * LANES))

    charge = jnp.where(
        kind == 0, wide(row[3]), jnp.where(kind == 1, wide(row[4]), wide(row[5]))
    )
    charge = jnp.where(level < 5, charge, 0.0)
    factor = jnp.where(level == 3, wide(z), wide(square))
    factor = jnp.where(level == 2, wide(y), factor)
    factor = jnp.where(level == 1, wide(x), factor)
    moments[slot, 0] = charge * jnp.where(level == 0, 1.0, factor)
    last = jnp.where(level == 4, charge, 0.0)
    moments[slot, 1] = jnp.where(level == 1, charge, last * wide(2.0 * x))
    moments[slot, 2] = jnp.where(level == 2, charge, last * wide(2.0 * y))
    moments[slot, 3] = last


def shifted(moments, slot, shift_x, shift_y):
    return (
        moments[slot, 0]
        + shift_x * moments[slot, 1]
        + shift_y * moments[slot, 2]
        + (shift_x * shift_x + shift_y * shift_y) * moments[slot, 3]
    )


def pair_cubes(target, slot, shift_x, shift_y, spread):
    x = target[0] - shift_x
    y = target[1] - shift_y
    z = target[2]
    square = x * x + y * y + z * z + SMOOTH2
    result = []
    for half in range(2):
        part = slice(half * LANES, (half + 1) * LANES)
        highs = []
        lows = []
        for side in range(2):
            lanes = slice(side * LANES, (side + 1) * LANES)
            distance = (
                (square[:, lanes] + spread[slot, 3, part, :])
                + x[:, lanes] * spread[slot, 0, part, :]
                + y[:, lanes] * spread[slot, 1, part, :]
                + z[:, lanes] * spread[slot, 2, part, :]
            )
            inverse = lax.rsqrt(distance)
            high, low = split(inverse * inverse * inverse)
            highs.append(high)
            lows.append(low)
        result.append((jnp.concatenate(highs, axis=1), jnp.concatenate(lows, axis=1)))
    return result


def near_sums(target, blocks, spread, moments):
    total = jnp.zeros((48, 2 * LANES), F32)
    for slot, shift_x, shift_y in blocks:
        weight = shifted(moments, slot, shift_x, shift_y)
        for half, terms in enumerate(pair_cubes(target, slot, shift_x, shift_y, spread)):
            part = slice(half * LANES, (half + 1) * LANES)
            total = total + bdot(
                three_terms(weight[:, part]), jnp.concatenate(terms, axis=0)
            )
    return total[:16] + total[16:32] + total[32:]


def run_tasks(size_y, tasks, table_ref, pack_ref, out_ref, lift, spread, moments, adds):
    for start, amount, sources in tasks:
        together = 1
        while together * sources < 24 and amount % (2 * together) == 0:
            together *= 2

        def one(index, start, sources):
            at = start + index * (2 + 3 * sources)
            i = table_ref[at]
            j = table_ref[at + 1]
            target = [pack_ref[c, i, pl.ds(j, 1), :] for c in range(3)]
            target[2] = target[2] + lift
            blocks = [
                (
                    table_ref[at + 2 + 3 * k],
                    table_ref[at + 3 + 3 * k].astype(F32),
                    table_ref[at + 4 + 3 * k].astype(F32),
                )
                for k in range(sources)
            ]
            return i * size_y + j, near_sums(target, blocks, spread, moments)

        def step(index, carry, start=start, sources=sources, together=together):
            found = [one(index * together + k, start, sources) for k in range(together)]
            for place, total in found:
                out_ref[place] = total + out_ref[place] if adds else total
            return carry

        lax.fori_loop(0, amount // together, step, 0)


def own_kernel(size_x, size_y, tasks, table_ref, pack_ref, out_ref, spread, moments):
    masks = near_masks()

    def prepare(index, carry):
        for k in range(4):
            slot = index * 4 + k
            row = [pack_ref[c, slot // size_y, pl.ds(slot % size_y, 1), :] for c in range(6)]
            prepare_column(row, slot, masks, spread, moments)
        return carry

    lax.fori_loop(0, size_x * size_y // 4, prepare, 0)
    out_ref[...] = jnp.zeros_like(out_ref)

    def places(i, j):
        row = [pack_ref[c, i, pl.ds(j, 1), :] for c in range(3)]
        return [row[0], row[1], row[2] + masks[2]]

    def one(at, others):
        i = table_ref[at]
        j = table_ref[at + 1]
        slot = i * size_y + j
        total = near_sums(places(i, j), [(slot, 0.0, 0.0)], spread, moments)
        found = []
        for k in range(others):
            i, j, away_x, away_y = [table_ref[at + 2 + 4 * k + m] for m in range(4)]
            away_x = away_x.astype(F32)
            away_y = away_y.astype(F32)
            other = i * size_y + j
            (h_first, l_first), (h_second, l_second) = pair_cubes(
                places(i, j), slot, -away_x, -away_y, spread
            )
            high = jnp.concatenate([h_first, h_second], axis=0)
            low = jnp.concatenate([l_first, l_second], axis=0)
            there = bdot(
                three_terms(shifted(moments, slot, -away_x, -away_y)),
                jnp.concatenate([high, low], axis=0),
            )
            found.append((other, there[:16] + there[16:32] + there[32:]))
            here = lax.dot_general(
                three_terms(shifted(moments, other, away_x, away_y)),
                jnp.concatenate([high, low], axis=1),
                (((1,), (1,)), ((), ())),
                preferred_element_type=F32,
            )
            total = total + here[:16] + here[16:32] + here[32:]
        found.append((slot, total))
        return found

    for start, amount, others in tasks:
        together = 3 if amount % 3 == 0 else 1

        def step(index, carry, start=start, others=others, together=together):
            found = []
            for k in range(together):
                found += one(start + (index * together + k) * (2 + 4 * others), others)
            for place, total in found:
                out_ref[place] += total
            return carry

        lax.fori_loop(0, amount // together, step, 0)


def halo_kernel(size_x, size_y, axis, tasks, table_ref, before_ref, pack_ref, *rest):
    parcels = rest[:2]
    out_ref, spread, moments, held = rest[2:]
    masks = near_masks()
    out_ref[...] = before_ref[...]
    ends = parcel_rows(size_x, size_y)[0 if axis == "gx" else 1]
    cells = size_y if axis == "gx" else size_x + 2
    for number, (side, parcel) in enumerate(zip(SIDES, parcels)):
        row = ends[0]
        inside = lies_inside(axis, side)
        for c in range(6):
            for half in range(2):
                lanes = slice(half * LANES, (half + 1) * LANES)
                if axis == "gx":
                    value = parcel[row : row + cells]
                    row += cells
                else:
                    value = parcel[pl.ds(ends[0] + c * 2 * cells + half, cells, stride=2), :]
                held[c, number * cells : (number + 1) * cells, lanes] = (
                    value if c < 3 else value * inside
                )

    def prepare(index, carry):
        for k in range(4):
            slot = index * 4 + k
            row = [held[c, pl.ds(slot, 1), :] for c in range(6)]
            prepare_column(row, slot, masks, spread, moments)
        return carry

    lax.fori_loop(0, 2 * cells // 4, prepare, 0)
    run_tasks(size_y, tasks, table_ref, pack_ref, out_ref, masks[2], spread, moments, True)


def near_tables(size_x, size_y):
    kinds = ({}, {}, {})
    for i in range(size_x):
        for j in range(size_y):
            pairs = []
            for x, y in ((0, 1), (1, -1), (1, 0), (1, 1)):
                if i + x < size_x and 0 <= j + y < size_y:
                    pairs += [i + x, j + y, x, y]
            kinds[0].setdefault(len(pairs) // 4, []).append([i, j] + pairs)
            found = ([], [], [])
            for x in (-1, 0, 1):
                for y in (-1, 0, 1):
                    if not 0 <= j + y < size_y:
                        found[2].extend([int(y > 0) * (size_x + 2) + i + x + 1, x, y])
                    elif not 0 <= i + x < size_x:
                        found[1].extend([int(x > 0) * size_y + j + y, x, y])
            for groups, sources in zip(kinds[1:], found[1:]):
                if sources:
                    groups.setdefault(len(sources) // 3, []).append([i, j] + sources)
    result = []
    flat = []
    for groups in kinds:
        tasks = []
        for sources in sorted(groups, reverse=True):
            tasks.append((len(flat), len(groups[sources]), sources))
            for entry in groups[sources]:
                flat += entry
        result.append(tasks)
    return np.array(flat, np.int32), result


def leaf_kernel(size_x, size_y, own_ref, rows_ref, *rest):
    parcels = rest[:4]
    down_ref, base, leaf_ref, cols_ref = rest[4:]
    lay_points(cols_ref, rows_ref)
    for depth in range(2):
        for c in range(3):
            for x in range(size_x):
                leaf_ref[depth, c, WIDTH + x, WIDTH : WIDTH + size_y] = own_ref[depth, c, x]
    for side, parcel in zip(SIDES, parcels[:2]):
        inside = lies_inside("gx", side)
        start = landing(side, size_x, WIDTH)
        row = 0
        for depth in range(2):
            for c in range(3):
                for x in range(start, start + WIDTH):
                    leaf_ref[depth, c, x, WIDTH : WIDTH + size_y] = (
                        parcel[row : row + size_y] * inside
                    )
                    row += size_y
    for side, parcel in zip(SIDES, parcels[2:]):
        inside = lies_inside("gy", side)
        start = landing(side, size_y, WIDTH)
        row = 0
        for depth in range(2):
            for c in range(3):
                for x in range(size_x + 2 * WIDTH):
                    leaf_ref[depth, c, x, start : start + WIDTH] = (
                        parcel[row : row + WIDTH] * inside
                    )
                    row += WIDTH
    for axis in range(3):
        base[axis] = 0.9 * rows_ref[axis : axis + 1, :] - 0.9 * cols_ref[axis]
    down_ref[...] = jnp.zeros_like(down_ref)
    odd_y = lax.broadcasted_iota(jnp.int32, (size_y, LANES), 0) % 2
    near_y = {-3: jnp.where(odd_y == 1, 1.0, 0.0), 3: jnp.where(odd_y == 0, 1.0, 0.0)}

    def one_row(shift_x, shifts_y):
        dx = base[0] - shift_x.astype(F32)
        tables = []
        charges = []
        for shift_y in shifts_y:
            dy = base[1] - float(shift_y)
            flat = dx * dx + dy * dy + SMOOTH2
            table = []
            for shift_z in (-1, 0, 1):
                dz = base[2] - float(shift_z)
                table.append(lax.rsqrt(flat + dz * dz).astype(BF16))
            tables.append(jnp.concatenate([table[1], table[0]], axis=1))
            tables.append(jnp.concatenate([table[2], table[1]], axis=1))
            for depth in range(2):
                pieces = []
                for c in range(3):
                    for x in range(size_x):
                        near_x = (shift_x > -3) if x % 2 == 0 else (shift_x < 3)
                        piece = jnp.where(
                            near_x,
                            leaf_ref[depth, c, x + 3 + shift_x, 3 + shift_y : 3 + shift_y + size_y],
                            0.0,
                        )
                        if abs(shift_y) == 3:
                            piece = piece * near_y[shift_y]
                        pieces.append(piece)
                charges.append(jnp.concatenate(pieces, axis=0).astype(BF16))
        down_ref[...] += bdot(
            jnp.concatenate(charges, axis=1), jnp.concatenate(tables, axis=0)
        )

    def outer(step, carry):
        one_row(jnp.where(step < 2, step - 3, step), (-3, -2, -1, 0, 1, 2, 3))
        return carry

    def inner(step, carry):
        one_row(step - 1, (-3, -2, 2, 3))
        return carry

    lax.fori_loop(0, 4, outer, 0)
    lax.fori_loop(0, 3, inner, 0)


def far_kernel(
    size_x,
    size_y,
    tops_x,
    tops_y,
    chunk,
    slots_at,
    slot_ref,
    living_ref,
    down_ref,
    tops_ref,
    near_ref,
    pack_ref,
    rows_ref,
    inverse_ref,
    out_ref,
    base,
    windows,
    down,
    top_down,
    local,
    surface,
    squares_y,
    cols_ref,
):
    half_x = size_x // 2
    half_y = size_y // 2
    group = half_x * 4
    across = tops_x + half_x - 1
    along = tops_y + half_y - 1
    point = [rows_ref[j : j + 1, :] for j in range(3)]
    lay_points(cols_ref, rows_ref)
    for axis in range(3):
        base[axis] = 1.8 * point[axis] - 1.8 * cols_ref[axis]

    windows[...] = jnp.zeros_like(windows)
    lanes_x = tops_x // half_x
    lanes_y = tops_y // half_y
    mine_x = lax.axis_index("gx")
    mine_y = lax.axis_index("gy")

    def place(device, carry):
        place_x = device // lanes_y
        place_y = device % lanes_y
        away_x = lax.rem(place_x - mine_x + lanes_x, lanes_x)
        away_y = lax.rem(place_y - mine_y + lanes_y, lanes_y)
        slot = slot_ref[slots_at + away_x * lanes_y + away_y]
        i = place_x * half_x
        j = place_y * half_y
        for c in range(3):
            for p in range(half_x):
                for q in range(half_y):
                    row = tops_ref[slot, (c * half_x + p) * half_y + q, :][None]
                    for x in range(half_x):
                        windows[
                            i + p + half_x - 1 - x,
                            pl.ds((j + q + half_y - 1) * group + x * 4 + c, 1),
                            :,
                        ] = row
        return carry

    lax.fori_loop(0, lanes_x * lanes_y, place, 0)
    first_x = mine_x * half_x
    first_y = mine_y * half_y
    top_down[...] = jnp.zeros_like(top_down)
    parts = -(-along // chunk)

    def square_y(wy, carry):
        dy = base[1] + 2.0 * (first_y - (wy - (half_y - 1))).astype(F32)
        squares_y[wy] = dy * dy
        return carry

    lax.fori_loop(0, parts * chunk, square_y, 0)

    def top_row(step):
        wx = step // parts
        start = (step % parts) * chunk
        gap_x = first_x - (wx - (half_x - 1))
        dx = base[0] + 2.0 * gap_x.astype(F32)
        squares = dx * dx + base[2] * base[2] + SMOOTH2
        tables = []
        pieces = []
        for k in range(chunk):
            wy = start + k
            gap_y = first_y - (wy - (half_y - 1))
            distant = (jnp.abs(gap_x) >= 2) | (jnp.abs(gap_y) >= 2)
            tables.append(lax.rsqrt(squares + squares_y[wy]).astype(BF16))
            rows = windows[wx, pl.ds(wy * group, half_y * group), :]
            pieces.append(jnp.where(distant, rows, 0.0))
        return bdot(
            jnp.concatenate(pieces, axis=1).astype(BF16), jnp.concatenate(tables, axis=0)
        )

    together = 3
    steps = across * parts

    def top_rows(index, carry):
        found = [top_row(index * together + k) for k in range(together)]
        top_down[...] += sum(found[1:], found[0])
        return carry

    lax.fori_loop(0, steps // together, top_rows, 0)
    for step in range(steps - steps % together, steps):
        top_down[...] += top_row(jnp.int32(step))
    matrix = inverse_ref[...]
    top_local = dot_split_nt(top_down[...], matrix)
    lay_surface(surface, cols_ref)
    down[...] = down_ref[...]
    for a in range(2):
        for b in range(2):
            for e in range(2):
                offset = (a - 0.5, b - 0.5, e - 0.5)
                delta = [
                    offset[axis] + 0.9 * point[axis] - 3.0 * cols_ref[axis] for axis in range(3)
                ]
                table = lax.rsqrt(
                    delta[0] * delta[0] + delta[1] * delta[1] + delta[2] * delta[2] + SMOOTH2
                )
                inherited = dot_split(top_local, table)
                for y in range(half_y):
                    for x in range(half_x):
                        for c in range(3):
                            row = (c * size_x + 2 * x + a) * size_y + 2 * y + b
                            down[row : row + 1, e * LANES : (e + 1) * LANES] += inherited[
                                y * group + x * 4 + c : y * group + x * 4 + c + 1
                            ]
    for e in range(2):
        part = 0.5 * dot_split_nt(down[:, e * LANES : (e + 1) * LANES], matrix)
        local[e] = part.reshape(3, size_x, size_y, LANES)

    level = lax.broadcasted_iota(jnp.int32, (16, LANES), 0) // 3
    kind = lax.broadcasted_iota(jnp.int32, (16, LANES), 0) % 3
    patterns = []
    for half in range(2):
        x = 1.5 * point[0]
        y = 1.5 * point[1]
        z = 1.5 * point[2] + (half - 0.5)
        pattern = jnp.where(level == 0, 1.0, 0.0)
        for power, value in enumerate((x, y, z, x * x + y * y + z * z)):
            value = jnp.broadcast_to(value, (16, LANES))
            pattern = jnp.where(level == power + 1, value, pattern)
        patterns.append(pattern)

    def one_column(index):
        i = index // size_y
        j = index % size_y
        row = [pack_ref[c, i, pl.ds(j, 1), :] for c in range(3)]
        alive = living_ref[i, pl.ds(j, 1), :]
        results = []
        for half in range(2):
            lanes = slice(half * LANES, (half + 1) * LANES)
            place = [row[axis][:, lanes] for axis in range(3)]
            inverse = lax.rsqrt(surface_distance(surface, place))
            high, low = split(inverse * inverse * inverse)
            charge = [
                jnp.broadcast_to(local[half, c, i, pl.ds(j, 1), :], (16, LANES)) for c in range(3)
            ]
            weight = patterns[half] * jnp.where(
                kind == 0, charge[0], jnp.where(kind == 1, charge[1], charge[2])
            )
            total = bdot(two_terms(*split(weight)), jnp.concatenate([high, low], axis=0))
            total = total[:16] + total[16:] + near_ref[index, :, lanes]
            place[2] = place[2] + (half - 0.5)
            living = alive[:, lanes]
            square = (
                place[0] * place[0] + place[1] * place[1] + place[2] * place[2] + SMOOTH2
            )
            potential = (
                square * total[0:3]
                - 2.0
                * (place[0] * total[3:6] + place[1] * total[6:9] + place[2] * total[9:12])
                + total[12:15]
            ) * living
            slopes = [
                (total[3 + 3 * axis : 6 + 3 * axis] - place[axis] * total[0:3]) * living
                for axis in range(3)
            ]
            results.append((potential, slopes))
        potential = jnp.concatenate([results[0][0], results[1][0]], axis=1)
        slopes = [
            jnp.concatenate([results[0][1][axis], results[1][1][axis]], axis=1)
            for axis in range(3)
        ]
        for c in range(3):
            out_ref[c, i, pl.ds(j, 1), :] = potential[c : c + 1]
            for axis in range(3):
                out_ref[3 + 3 * c + axis, i, pl.ds(j, 1), :] = slopes[axis][c : c + 1]

    def columns(index, carry):
        for k in range(4):
            one_column(index * 4 + k)
        return carry

    lax.fori_loop(0, size_x * size_y // 4, columns, 0)


def moved(array, axis, step):
    count = lax.axis_size(axis)
    return lax.ppermute(array, axis, [((i + step) % count, i) for i in range(count)])


def widening(away, axis, count):
    half = 1
    plan = []
    while 2 * half + 1 < count:
        missing = count - 2 * half - 1
        if missing <= 2 * half + 1:
            first = -((missing - 1) // 2)
            steps = (half + 1 - first,)
        else:
            first = -half
            missing = 2 * half + 1
            steps = (missing, -missing)
        picks = []
        known = []
        for places in away:
            pick = [k for k, place in enumerate(places) if 0 <= place[axis] - first < missing]
            picks.append(pick)
            known += [places[k] for k in pick]
        plan.append((steps, picks))
        for step in steps:
            away = away + [
                [tuple(p + step * (k == axis) for k, p in enumerate(place)) for place in known]
            ]
        half = half + steps[0] if len(steps) == 2 else count
    return plan, away


ROUND = [[(x, y) for x in (-1, 0, 1)] for y in (-1, 0, 1)]


def top_slots(lanes_x, lanes_y):
    _, away = widening(ROUND, 1, lanes_y)
    _, away = widening(away, 0, lanes_x)
    slots = np.zeros((lanes_x, lanes_y), np.int32)
    places = [place for held in away for place in held]
    for slot, (x, y) in reversed(list(enumerate(places))):
        slots[x % lanes_x, y % lanes_y] = slot
    return slots


def widened(blocks, away, axis, name):
    plan, final = widening(away, axis, lax.axis_size(name))
    for steps, picks in plan:
        sent = []
        for array, places, pick in zip(blocks, away, picks):
            if len(pick) == len(places):
                sent.append(array)
            else:
                size = array.shape[0] // len(places)
                sent += [array[k * size : (k + 1) * size] for k in pick]
        whole = sent[0] if len(sent) == 1 else jnp.concatenate(sent, axis=0)
        blocks = blocks + [moved(whole, name, step) for step in steps]
        away = final[: len(blocks)]
    return blocks, final


def body(offsets, strengths, counts, check_inverse):
    size_x, size_y, depth = counts.shape
    expansion = check_inverse.shape[0]
    half_x = size_x // 2
    half_y = size_y // 2
    lanes_x = lax.axis_size("gx")
    lanes_y = lax.axis_size("gy")
    tops_x = lanes_x * half_x
    tops_y = lanes_y * half_y
    points = sphere_points(expansion)
    rows = jnp.asarray(np.concatenate([points, np.zeros((5, LANES), np.float32)], axis=0))
    def params(mebibytes):
        return pltpu.CompilerParams(vmem_limit_bytes=mebibytes * 2**20)

    smem = pl.BlockSpec(memory_space=pltpu.SMEM)
    vmem = pl.BlockSpec(memory_space=pltpu.VMEM)

    def cost(flops):
        return pl.CostEstimate(flops=flops, bytes_accessed=10**6, transcendentals=0)

    top_rows = 3 * half_x * half_y
    slot = jnp.arange(LANES)
    living = (slot < counts[:, :, :, None]).astype(F32).reshape(size_x, size_y, depth * LANES)
    pad = LANES - expansion
    matrix = jnp.pad(check_inverse, ((0, pad), (0, pad)))
    (_, _, end_x), (_, near_y, end_y) = parcel_rows(size_x, size_y)
    made = pl.pallas_call(
        functools.partial(up_kernel, size_x, size_y),
        out_shape=(
            jax.ShapeDtypeStruct((6, size_x, size_y, depth * LANES), F32),
            jax.ShapeDtypeStruct((2, 3, size_x, size_y, LANES), F32),
            jax.ShapeDtypeStruct((top_rows, LANES), F32),
            *[jax.ShapeDtypeStruct((end_x, LANES), F32)] * 2,
        ),
        in_specs=[vmem] * 5,
        out_specs=(vmem,) * 5,
        scratch_shapes=[
            pltpu.VMEM((2, 3, size_x, size_y, LANES), F32),
            pltpu.VMEM((4, LANES, LANES), F32),
            pltpu.VMEM((3, LANES, LANES), F32),
        ],
        compiler_params=params(12),
        cost_estimate=cost(6 * 10**9),
        name="up",
    )(living, offsets, strengths, rows, matrix)
    pack, leaf_charges, top_charges, to_below, to_above = made
    below = moved(to_above, "gx", -1)
    above = moved(to_below, "gx", 1)

    table, (own_tasks, *beside) = near_tables(size_x, size_y)
    slots_at = len(table)
    slots = top_slots(lanes_x, lanes_y)
    table = jnp.asarray(np.concatenate([table, slots.reshape(-1)]))
    near_shape = jax.ShapeDtypeStruct((size_x * size_y, 16, 2 * LANES), F32)
    own = pl.pallas_call(
        functools.partial(own_kernel, size_x, size_y, own_tasks),
        out_shape=near_shape,
        in_specs=[smem, vmem],
        out_specs=vmem,
        scratch_shapes=[
            pltpu.VMEM((size_x * size_y, 4, 2 * LANES, LANES), F32),
            pltpu.VMEM((size_x * size_y, 4, 16, 2 * LANES), F32),
        ],
        compiler_params=params(28),
        cost_estimate=cost(3 * 10**10),
        name="own",
    )(table, pack)

    to_low, to_high, tops = pl.pallas_call(
        functools.partial(turn_kernel, size_x, size_y),
        out_shape=(
            jax.ShapeDtypeStruct((end_y, LANES), F32),
            jax.ShapeDtypeStruct((end_y, LANES), F32),
            jax.ShapeDtypeStruct((3 * top_rows, LANES), F32),
        ),
        in_specs=[vmem] * 5,
        out_specs=(vmem,) * 3,
        compiler_params=params(12),
        cost_estimate=cost(10**9),
        name="turn",
    )(leaf_charges, pack, top_charges, below, above)
    low = moved(to_high, "gy", -1)
    high = moved(to_low, "gy", 1)
    blocks, away = widened(
        [low[near_y:], tops, high[near_y:]],
        ROUND,
        1,
        "gy",
    )

    def beside_near(axis, before, parcels):
        tasks = beside[0 if axis == "gx" else 1]
        columns = 2 * (size_y if axis == "gx" else size_x + 2)
        return pl.pallas_call(
            functools.partial(halo_kernel, size_x, size_y, axis, tasks),
            out_shape=near_shape,
            in_specs=[smem] + [vmem] * 4,
            out_specs=vmem,
            scratch_shapes=[
                pltpu.VMEM((columns, 4, 2 * LANES, LANES), F32),
                pltpu.VMEM((columns, 4, 16, 2 * LANES), F32),
                pltpu.VMEM((6, columns, 2 * LANES), F32),
            ],
            compiler_params=params(20),
            cost_estimate=cost(10**10),
            name="beside_" + axis,
        )(table, before, pack, *parcels)

    near = beside_near("gx", own, (below, above))
    blocks, away = widened(blocks, away, 0, "gx")
    blocks = jnp.concatenate(blocks, axis=0).reshape(-1, top_rows, LANES)
    near = beside_near("gy", near, (low, high))

    down = pl.pallas_call(
        functools.partial(leaf_kernel, size_x, size_y),
        out_shape=jax.ShapeDtypeStruct((3 * size_x * size_y, 2 * LANES), F32),
        in_specs=[vmem] * 6,
        out_specs=vmem,
        scratch_shapes=[
            pltpu.VMEM((3, LANES, LANES), F32),
            pltpu.VMEM(
                (2, 3, size_x + 2 * WIDTH, size_y + 2 * WIDTH, LANES), F32
            ),
            pltpu.VMEM((3, LANES, LANES), F32),
        ],
        compiler_params=params(12),
        cost_estimate=cost(6 * 10**9),
        name="leaf",
    )(leaf_charges, rows, below, above, low, high)

    across = tops_x + half_x - 1
    along = tops_y + half_y - 1
    parts = -(-along // 20)
    chunk = -(-along // parts)
    return pl.pallas_call(
        functools.partial(far_kernel, size_x, size_y, tops_x, tops_y, chunk, slots_at),
        out_shape=jax.ShapeDtypeStruct((12, size_x, size_y, depth * LANES), F32),
        in_specs=[smem] + [vmem] * 7,
        out_specs=vmem,
        scratch_shapes=[
            pltpu.VMEM((3, LANES, LANES), F32),
            pltpu.VMEM((across, (parts * chunk + half_y - 1) * half_x * 4, LANES), F32),
            pltpu.VMEM((3 * size_x * size_y, 2 * LANES), F32),
            pltpu.VMEM((half_y * half_x * 4, LANES), F32),
            pltpu.VMEM((2, 3, size_x, size_y, LANES), F32),
            pltpu.VMEM((4, LANES, LANES), F32),
            pltpu.VMEM((parts * chunk, LANES, LANES), F32),
            pltpu.VMEM((3, LANES, LANES), F32),
        ],
        compiler_params=params(40),
        cost_estimate=cost(10**10),
        name="far",
    )(
        table,
        living,
        down,
        blocks,
        near,
        pack,
        rows,
        matrix,
    )


def solution(mesh):
    return jax.shard_map(
        body,
        mesh=mesh,
        in_specs=(P(None, "gx", "gy", None), P(None, "gx", "gy", None), P("gx", "gy", None), P()),
        out_specs=P(None, "gx", "gy", None),
        check_vma=False,
    )
```

```python
import functools
import math

import jax
import jax.numpy as jnp
import numpy as np
from jax import lax
from jax.experimental import pallas as pl
from jax.experimental.pallas import tpu as pltpu
from jax.sharding import PartitionSpec as P

SMOOTH2 = 0.01
STRENGTH_SCALE = 0.03
LANES = 128
F32 = jnp.float32
BF16 = jnp.bfloat16


def sphere_points(amount):
    counter = np.arange(amount, dtype=np.float32)
    height = (1.0 - (2.0 * counter + 1.0) / np.float32(amount)).astype(np.float32)
    radius = np.sqrt(np.maximum(1.0 - height * height, 0.0)).astype(np.float32)
    azimuth = counter * np.float32(math.pi * (3.0 - math.sqrt(5.0)))
    points = np.zeros((3, LANES), np.float32)
    points[:, :amount] = np.stack([radius * np.cos(azimuth), radius * np.sin(azimuth), height])
    return points


def split(value):
    high = value.astype(BF16)
    return high, (value - high.astype(F32)).astype(BF16)


def bdot(left, right):
    return jnp.dot(left, right, preferred_element_type=F32)


def two_terms(high, low):
    return jnp.concatenate(
        [
            jnp.concatenate([high, high], axis=1),
            jnp.concatenate([low, jnp.zeros_like(low)], axis=1),
        ],
        axis=0,
    )


def three_terms(value):
    first = value.astype(BF16)
    rest = value - first.astype(F32)
    second = rest.astype(BF16)
    third = (rest - second.astype(F32)).astype(BF16)
    return jnp.concatenate(
        [
            jnp.concatenate([first, first], axis=1),
            jnp.concatenate([second, second], axis=1),
            jnp.concatenate([third, jnp.zeros_like(third)], axis=1),
        ],
        axis=0,
    )


def dot_split(left, right):
    rows = left.shape[0]
    both = bdot(two_terms(*split(left)), jnp.concatenate(split(right), axis=0))
    return both[:rows] + both[rows:]


def dot_split_nt(left, right):
    rows = left.shape[0]
    both = lax.dot_general(
        two_terms(*split(left)),
        jnp.concatenate(split(right), axis=1),
        (((1,), (1,)), ((), ())),
        preferred_element_type=F32,
    )
    return both[:rows] + both[rows:]


def lay_points(cols_ref, rows_ref):
    for axis in range(3):
        row = rows_ref[axis : axis + 1, :]
        cols_ref[axis] = jnp.broadcast_to(row, (LANES, LANES)).T


def lay_surface(surface, cols_ref):
    total = jnp.zeros((LANES, LANES), F32)
    for axis in range(3):
        surface[axis] = -3.0 * cols_ref[axis]
        total = total + 2.25 * cols_ref[axis] * cols_ref[axis]
    surface[3] = total


def surface_distance(surface, place):
    square = place[0] * place[0] + place[1] * place[1] + place[2] * place[2] + SMOOTH2
    return (
        (square + surface[3])
        + place[0] * surface[0]
        + place[1] * surface[1]
        + place[2] * surface[2]
    )


SIDES = (-1, 1)
WIDTH = 3


def edge(side, size, width):
    return 0 if side < 0 else size - width


def landing(side, size, width):
    return 0 if side < 0 else size + width


def parcel_rows(size_x, size_y):
    tops = 3 * (size_x // 2) * (size_y // 2)
    leaves_x = 6 * WIDTH * size_y
    leaves_y = 6 * (size_x + 2 * WIDTH) * WIDTH
    near_x = leaves_x + 12 * size_y
    near_y = leaves_y + 12 * (size_x + 2)
    return (leaves_x, near_x, near_x + tops), (leaves_y, near_y, near_y + 3 * tops)


def lies_inside(axis, side):
    place = lax.axis_index(axis) + side
    return jnp.where((place >= 0) & (place < lax.axis_size(axis)), 1.0, 0.0)


def up_kernel(
    size_x,
    size_y,
    living_ref,
    offsets_ref,
    strengths_ref,
    rows_ref,
    matrix_ref,
    pack_ref,
    leaf_ref,
    top_ref,
    *rest,
):
    parcels = rest[:2]
    check, surface, cols_ref = rest[2:]
    lay_points(cols_ref, rows_ref)
    lay_surface(surface, cols_ref)
    point = [rows_ref[j : j + 1, :] for j in range(3)]
    pack_ref[0:3] = offsets_ref[...]

    def one_column(i, j):
        row = [offsets_ref[c, i, pl.ds(j, 1), :] for c in range(3)]
        living = living_ref[i, pl.ds(j, 1), :]
        charges = []
        for c in range(3):
            value = STRENGTH_SCALE * strengths_ref[c, i, pl.ds(j, 1), :] * living
            pack_ref[3 + c, i, pl.ds(j, 1), :] = value
            charges.append(value)
        charge = jnp.concatenate(charges + [jnp.zeros((5, 2 * LANES), F32)], axis=0)
        for half in range(2):
            lanes = slice(half * LANES, (half + 1) * LANES)
            place = [row[axis][:, lanes] for axis in range(3)]
            kernel = lax.rsqrt(surface_distance(surface, place))
            both = jnp.concatenate(split(charge[:, lanes]), axis=0)
            total = lax.dot_general(
                jnp.concatenate([both, both], axis=1),
                jnp.concatenate(split(kernel), axis=1),
                (((1,), (1,)), ((), ())),
                preferred_element_type=F32,
            )
            total = total[:8] + total[8:]
            for c in range(3):
                check[half, c, i, pl.ds(j, 1), :] = total[c : c + 1]

    def columns(index, carry):
        for k in range(8):
            step = index * 8 + k
            one_column(step // size_y, step % size_y)
        return carry

    lax.fori_loop(0, size_x * size_y // 8, columns, 0)
    matrix = matrix_ref[...]
    rows = 6 * size_x * size_y
    charges = 0.5 * dot_split_nt(check[...].reshape(rows, LANES), matrix)
    leaf_ref[...] = charges.reshape(2, 3, size_x, size_y, LANES)
    half_x = size_x // 2
    half_y = size_y // 2
    count = 3 * half_x * half_y
    padding = -count % 16
    filler = [jnp.zeros((padding, LANES), F32)] if padding else []
    total = jnp.zeros((count + padding, LANES), F32)
    for a in range(2):
        for b in range(2):
            for e in range(2):
                shift = (a - 0.5, b - 0.5, e - 0.5)
                delta = [
                    3.0 * point[axis] - shift[axis] - 0.9 * cols_ref[axis] for axis in range(3)
                ]
                table = lax.rsqrt(
                    delta[0] * delta[0] + delta[1] * delta[1] + delta[2] * delta[2] + SMOOTH2
                )
                pieces = [
                    leaf_ref[e, c, 2 * x + a, pl.ds(b, half_y, stride=2), :]
                    for c in range(3)
                    for x in range(half_x)
                ]
                total = total + dot_split(jnp.concatenate(pieces + filler, axis=0), table)
    tops = dot_split_nt(total, matrix)[:count]
    top_ref[...] = tops
    (_, second, end), _ = parcel_rows(size_x, size_y)
    for side, parcel in zip(SIDES, parcels):
        row = 0
        start = edge(side, size_x, WIDTH)
        for depth in range(2):
            for c in range(3):
                for x in range(start, start + WIDTH):
                    parcel[row : row + size_y] = leaf_ref[depth, c, x]
                    row += size_y
        for c in range(6):
            for half in range(2):
                lanes = slice(half * LANES, (half + 1) * LANES)
                parcel[row : row + size_y] = pack_ref[c, edge(side, size_x, 1), :, lanes]
                row += size_y
        parcel[second:end] = tops


def turn_kernel(
    size_x, size_y, leaf_ref, pack_ref, top_ref, below_ref, above_ref, low_ref, high_ref, tops_ref
):
    (_, near_x, end_x), (_, near_y, _) = parcel_rows(size_x, size_y)
    count = end_x - near_x
    for place, ref in ((0, below_ref), (2, above_ref)):
        tops_ref[place * count : (place + 1) * count] = ref[near_x:end_x]
    tops_ref[count : 2 * count] = top_ref[...]
    inside = [lies_inside("gx", side) for side in SIDES]
    for side, parcel in zip(SIDES, (low_ref, high_ref)):
        row = 0
        start = edge(side, size_y, WIDTH)
        for depth in range(2):
            for c in range(3):
                for x in range(-WIDTH, size_x + WIDTH):
                    if 0 <= x < size_x:
                        value = leaf_ref[depth, c, x, start : start + WIDTH]
                    else:
                        which = int(x >= size_x)
                        ref = (below_ref, above_ref)[which]
                        cell = x - size_x if which else x + WIDTH
                        at = ((depth * 3 + c) * WIDTH + cell) * size_y + start
                        value = ref[at : at + WIDTH] * inside[which]
                    parcel[row : row + WIDTH] = value
                    row += WIDTH
        start = edge(side, size_y, 1)
        first, _, _ = parcel_rows(size_x, size_y)[0]
        for c in range(6):
            for x in range(-1, size_x + 1):
                for half in range(2):
                    if 0 <= x < size_x:
                        lanes = slice(half * LANES, (half + 1) * LANES)
                        value = pack_ref[c, x, start : start + 1, lanes]
                    else:
                        which = int(x >= size_x)
                        ref = (below_ref, above_ref)[which]
                        at = first + (c * 2 + half) * size_y + start
                        value = ref[at : at + 1]
                        if c >= 3:
                            value = value * inside[which]
                    parcel[row : row + 1] = value
                    row += 1
        parcel[near_y : near_y + 3 * count] = tops_ref[...]


def near_masks():
    row = lax.broadcasted_iota(jnp.int32, (16, 2 * LANES), 0)
    lane = lax.broadcasted_iota(jnp.int32, (1, 2 * LANES), 1)
    return row // 3, row % 3, jnp.where(lane < LANES, -0.5, 0.5).astype(F32)


def prepare_column(row, slot, masks, spread, moments):
    level, kind, lift = masks
    x, y, z = row[0], row[1], row[2] + lift
    square = x * x + y * y + z * z
    values = jnp.concatenate(
        [-2.0 * x, -2.0 * y, -2.0 * z, square, jnp.zeros((4, 2 * LANES), F32)], axis=0
    )
    first = values.astype(BF16).astype(F32)
    second = (values - first).astype(BF16).astype(F32)
    terms = jnp.concatenate(
        [first, second, (values - first) - second, jnp.zeros_like(values)], axis=0
    ).T.astype(BF16)
    term = lax.broadcasted_iota(jnp.int32, (32, 4 * LANES), 0)
    place = lax.broadcasted_iota(jnp.int32, (32, 4 * LANES), 1) // LANES
    chosen = jnp.where((term % 8 == place) & (term < 24), 1.0, 0.0).astype(BF16)
    laid = bdot(terms, chosen)
    for axis in range(4):
        spread[slot, axis] = laid[:, axis * LANES : (axis + 1) * LANES]

    def wide(value):
        return jnp.broadcast_to(value, (16, 2 * LANES))

    charge = jnp.where(
        kind == 0, wide(row[3]), jnp.where(kind == 1, wide(row[4]), wide(row[5]))
    )
    charge = jnp.where(level < 5, charge, 0.0)
    factor = jnp.where(level == 3, wide(z), wide(square))
    factor = jnp.where(level == 2, wide(y), factor)
    factor = jnp.where(level == 1, wide(x), factor)
    moments[slot, 0] = charge * jnp.where(level == 0, 1.0, factor)
    last = jnp.where(level == 4, charge, 0.0)
    moments[slot, 1] = jnp.where(level == 1, charge, last * wide(2.0 * x))
    moments[slot, 2] = jnp.where(level == 2, charge, last * wide(2.0 * y))
    moments[slot, 3] = last


def shifted(moments, slot, shift_x, shift_y):
    return (
        moments[slot, 0]
        + shift_x * moments[slot, 1]
        + shift_y * moments[slot, 2]
        + (shift_x * shift_x + shift_y * shift_y) * moments[slot, 3]
    )


def pair_cubes(target, slot, shift_x, shift_y, spread):
    x = target[0] - shift_x
    y = target[1] - shift_y
    z = target[2]
    square = x * x + y * y + z * z + SMOOTH2
    result = []
    for half in range(2):
        part = slice(half * LANES, (half + 1) * LANES)
        highs = []
        lows = []
        for side in range(2):
            lanes = slice(side * LANES, (side + 1) * LANES)
            distance = (
                (square[:, lanes] + spread[slot, 3, part, :])
                + x[:, lanes] * spread[slot, 0, part, :]
                + y[:, lanes] * spread[slot, 1, part, :]
                + z[:, lanes] * spread[slot, 2, part, :]
            )
            inverse = lax.rsqrt(distance)
            high, low = split(inverse * inverse * inverse)
            highs.append(high)
            lows.append(low)
        result.append((jnp.concatenate(highs, axis=1), jnp.concatenate(lows, axis=1)))
    return result


def near_sums(target, blocks, spread, moments):
    total = jnp.zeros((48, 2 * LANES), F32)
    for slot, shift_x, shift_y in blocks:
        weight = shifted(moments, slot, shift_x, shift_y)
        for half, terms in enumerate(pair_cubes(target, slot, shift_x, shift_y, spread)):
            part = slice(half * LANES, (half + 1) * LANES)
            total = total + bdot(
                three_terms(weight[:, part]), jnp.concatenate(terms, axis=0)
            )
    return total[:16] + total[16:32] + total[32:]


def run_tasks(size_y, tasks, table_ref, pack_ref, out_ref, lift, spread, moments, adds):
    for start, amount, sources in tasks:
        together = 1
        while together * sources < 24 and amount % (2 * together) == 0:
            together *= 2

        def one(index, start, sources):
            at = start + index * (2 + 3 * sources)
            i = table_ref[at]
            j = table_ref[at + 1]
            target = [pack_ref[c, i, pl.ds(j, 1), :] for c in range(3)]
            target[2] = target[2] + lift
            blocks = [
                (
                    table_ref[at + 2 + 3 * k],
                    table_ref[at + 3 + 3 * k].astype(F32),
                    table_ref[at + 4 + 3 * k].astype(F32),
                )
                for k in range(sources)
            ]
            return i * size_y + j, near_sums(target, blocks, spread, moments)

        def step(index, carry, start=start, sources=sources, together=together):
            found = [one(index * together + k, start, sources) for k in range(together)]
            for place, total in found:
                out_ref[place] = total + out_ref[place] if adds else total
            return carry

        lax.fori_loop(0, amount // together, step, 0)


def own_kernel(size_x, size_y, tasks, table_ref, pack_ref, out_ref, spread, moments):
    masks = near_masks()

    def prepare(index, carry):
        for k in range(4):
            slot = index * 4 + k
            row = [pack_ref[c, slot // size_y, pl.ds(slot % size_y, 1), :] for c in range(6)]
            prepare_column(row, slot, masks, spread, moments)
        return carry

    lax.fori_loop(0, size_x * size_y // 4, prepare, 0)
    out_ref[...] = jnp.zeros_like(out_ref)

    def places(i, j):
        row = [pack_ref[c, i, pl.ds(j, 1), :] for c in range(3)]
        return [row[0], row[1], row[2] + masks[2]]

    def one(at, others):
        i = table_ref[at]
        j = table_ref[at + 1]
        slot = i * size_y + j
        total = near_sums(places(i, j), [(slot, 0.0, 0.0)], spread, moments)
        found = []
        for k in range(others):
            i, j, away_x, away_y = [table_ref[at + 2 + 4 * k + m] for m in range(4)]
            away_x = away_x.astype(F32)
            away_y = away_y.astype(F32)
            other = i * size_y + j
            (h_first, l_first), (h_second, l_second) = pair_cubes(
                places(i, j), slot, -away_x, -away_y, spread
            )
            high = jnp.concatenate([h_first, h_second], axis=0)
            low = jnp.concatenate([l_first, l_second], axis=0)
            there = bdot(
                three_terms(shifted(moments, slot, -away_x, -away_y)),
                jnp.concatenate([high, low], axis=0),
            )
            found.append((other, there[:16] + there[16:32] + there[32:]))
            here = lax.dot_general(
                three_terms(shifted(moments, other, away_x, away_y)),
                jnp.concatenate([high, low], axis=1),
                (((1,), (1,)), ((), ())),
                preferred_element_type=F32,
            )
            total = total + here[:16] + here[16:32] + here[32:]
        found.append((slot, total))
        return found

    for start, amount, others in tasks:
        together = 3 if amount % 3 == 0 else 1

        def step(index, carry, start=start, others=others, together=together):
            found = []
            for k in range(together):
                found += one(start + (index * together + k) * (2 + 4 * others), others)
            for place, total in found:
                out_ref[place] += total
            return carry

        lax.fori_loop(0, amount // together, step, 0)


def halo_kernel(size_x, size_y, axis, tasks, table_ref, before_ref, pack_ref, *rest):
    parcels = rest[:2]
    out_ref, spread, moments, held = rest[2:]
    masks = near_masks()
    out_ref[...] = before_ref[...]
    ends = parcel_rows(size_x, size_y)[0 if axis == "gx" else 1]
    cells = size_y if axis == "gx" else size_x + 2
    for number, (side, parcel) in enumerate(zip(SIDES, parcels)):
        row = ends[0]
        inside = lies_inside(axis, side)
        for c in range(6):
            for half in range(2):
                lanes = slice(half * LANES, (half + 1) * LANES)
                if axis == "gx":
                    value = parcel[row : row + cells]
                    row += cells
                else:
                    value = parcel[pl.ds(ends[0] + c * 2 * cells + half, cells, stride=2), :]
                held[c, number * cells : (number + 1) * cells, lanes] = (
                    value if c < 3 else value * inside
                )

    def prepare(index, carry):
        for k in range(4):
            slot = index * 4 + k
            row = [held[c, pl.ds(slot, 1), :] for c in range(6)]
            prepare_column(row, slot, masks, spread, moments)
        return carry

    lax.fori_loop(0, 2 * cells // 4, prepare, 0)
    run_tasks(size_y, tasks, table_ref, pack_ref, out_ref, masks[2], spread, moments, True)


def near_tables(size_x, size_y):
    kinds = ({}, {}, {})
    for i in range(size_x):
        for j in range(size_y):
            pairs = []
            for x, y in ((0, 1), (1, -1), (1, 0), (1, 1)):
                if i + x < size_x and 0 <= j + y < size_y:
                    pairs += [i + x, j + y, x, y]
            kinds[0].setdefault(len(pairs) // 4, []).append([i, j] + pairs)
            found = ([], [], [])
            for x in (-1, 0, 1):
                for y in (-1, 0, 1):
                    if not 0 <= j + y < size_y:
                        found[2].extend([int(y > 0) * (size_x + 2) + i + x + 1, x, y])
                    elif not 0 <= i + x < size_x:
                        found[1].extend([int(x > 0) * size_y + j + y, x, y])
            for groups, sources in zip(kinds[1:], found[1:]):
                if sources:
                    groups.setdefault(len(sources) // 3, []).append([i, j] + sources)
    result = []
    flat = []
    for groups in kinds:
        tasks = []
        for sources in sorted(groups, reverse=True):
            tasks.append((len(flat), len(groups[sources]), sources))
            for entry in groups[sources]:
                flat += entry
        result.append(tasks)
    return np.array(flat, np.int32), result


def leaf_kernel(size_x, size_y, own_ref, rows_ref, *rest):
    parcels = rest[:4]
    down_ref, base, leaf_ref, cols_ref = rest[4:]
    lay_points(cols_ref, rows_ref)
    for depth in range(2):
        for c in range(3):
            for x in range(size_x):
                leaf_ref[depth, c, WIDTH + x, WIDTH : WIDTH + size_y] = own_ref[depth, c, x]
    for side, parcel in zip(SIDES, parcels[:2]):
        inside = lies_inside("gx", side)
        start = landing(side, size_x, WIDTH)
        row = 0
        for depth in range(2):
            for c in range(3):
                for x in range(start, start + WIDTH):
                    leaf_ref[depth, c, x, WIDTH : WIDTH + size_y] = (
                        parcel[row : row + size_y] * inside
                    )
                    row += size_y
    for side, parcel in zip(SIDES, parcels[2:]):
        inside = lies_inside("gy", side)
        start = landing(side, size_y, WIDTH)
        row = 0
        for depth in range(2):
            for c in range(3):
                for x in range(size_x + 2 * WIDTH):
                    leaf_ref[depth, c, x, start : start + WIDTH] = (
                        parcel[row : row + WIDTH] * inside
                    )
                    row += WIDTH
    for axis in range(3):
        base[axis] = 0.9 * rows_ref[axis : axis + 1, :] - 0.9 * cols_ref[axis]
    down_ref[...] = jnp.zeros_like(down_ref)
    odd_y = lax.broadcasted_iota(jnp.int32, (size_y, LANES), 0) % 2
    near_y = {-3: jnp.where(odd_y == 1, 1.0, 0.0), 3: jnp.where(odd_y == 0, 1.0, 0.0)}

    def one_row(shift_x, shifts_y):
        dx = base[0] - shift_x.astype(F32)
        tables = []
        charges = []
        for shift_y in shifts_y:
            dy = base[1] - float(shift_y)
            flat = dx * dx + dy * dy + SMOOTH2
            table = []
            for shift_z in (-1, 0, 1):
                dz = base[2] - float(shift_z)
                table.append(lax.rsqrt(flat + dz * dz).astype(BF16))
            tables.append(jnp.concatenate([table[1], table[0]], axis=1))
            tables.append(jnp.concatenate([table[2], table[1]], axis=1))
            for depth in range(2):
                pieces = []
                for c in range(3):
                    for x in range(size_x):
                        near_x = (shift_x > -3) if x % 2 == 0 else (shift_x < 3)
                        piece = jnp.where(
                            near_x,
                            leaf_ref[depth, c, x + 3 + shift_x, 3 + shift_y : 3 + shift_y + size_y],
                            0.0,
                        )
                        if abs(shift_y) == 3:
                            piece = piece * near_y[shift_y]
                        pieces.append(piece)
                charges.append(jnp.concatenate(pieces, axis=0).astype(BF16))
        down_ref[...] += bdot(
            jnp.concatenate(charges, axis=1), jnp.concatenate(tables, axis=0)
        )

    def outer(step, carry):
        one_row(jnp.where(step < 2, step - 3, step), (-3, -2, -1, 0, 1, 2, 3))
        return carry

    def inner(step, carry):
        one_row(step - 1, (-3, -2, 2, 3))
        return carry

    lax.fori_loop(0, 4, outer, 0)
    lax.fori_loop(0, 3, inner, 0)


def far_kernel(
    size_x,
    size_y,
    tops_x,
    tops_y,
    chunk,
    slots_at,
    slot_ref,
    living_ref,
    down_ref,
    tops_ref,
    near_ref,
    pack_ref,
    rows_ref,
    inverse_ref,
    out_ref,
    base,
    windows,
    down,
    top_down,
    local,
    surface,
    squares_y,
    cols_ref,
):
    half_x = size_x // 2
    half_y = size_y // 2
    group = half_x * 4
    across = tops_x + half_x - 1
    along = tops_y + half_y - 1
    point = [rows_ref[j : j + 1, :] for j in range(3)]
    lay_points(cols_ref, rows_ref)
    for axis in range(3):
        base[axis] = 1.8 * point[axis] - 1.8 * cols_ref[axis]

    windows[...] = jnp.zeros_like(windows)
    lanes_x = tops_x // half_x
    lanes_y = tops_y // half_y
    mine_x = lax.axis_index("gx")
    mine_y = lax.axis_index("gy")

    def place(device, carry):
        place_x = device // lanes_y
        place_y = device % lanes_y
        away_x = lax.rem(place_x - mine_x + lanes_x, lanes_x)
        away_y = lax.rem(place_y - mine_y + lanes_y, lanes_y)
        slot = slot_ref[slots_at + away_x * lanes_y + away_y]
        i = place_x * half_x
        j = place_y * half_y
        for c in range(3):
            for p in range(half_x):
                for q in range(half_y):
                    row = tops_ref[slot, (c * half_x + p) * half_y + q, :][None]
                    for x in range(half_x):
                        windows[
                            i + p + half_x - 1 - x,
                            pl.ds((j + q + half_y - 1) * group + x * 4 + c, 1),
                            :,
                        ] = row
        return carry

    lax.fori_loop(0, lanes_x * lanes_y, place, 0, unroll=4)
    first_x = mine_x * half_x
    first_y = mine_y * half_y
    top_down[...] = jnp.zeros_like(top_down)
    parts = -(-along // chunk)

    def square_y(wy, carry):
        dy = base[1] + 2.0 * (first_y - (wy - (half_y - 1))).astype(F32)
        squares_y[wy] = dy * dy
        return carry

    lax.fori_loop(0, parts * chunk, square_y, 0)

    def top_row(step):
        wx = step // parts
        start = (step % parts) * chunk
        gap_x = first_x - (wx - (half_x - 1))
        dx = base[0] + 2.0 * gap_x.astype(F32)
        squares = dx * dx + base[2] * base[2] + SMOOTH2
        tables = []
        pieces = []
        for k in range(chunk):
            wy = start + k
            gap_y = first_y - (wy - (half_y - 1))
            distant = (jnp.abs(gap_x) >= 2) | (jnp.abs(gap_y) >= 2)
            tables.append(lax.rsqrt(squares + squares_y[wy]).astype(BF16))
            rows = windows[wx, pl.ds(wy * group, half_y * group), :]
            pieces.append(jnp.where(distant, rows, 0.0))
        return bdot(
            jnp.concatenate(pieces, axis=1).astype(BF16), jnp.concatenate(tables, axis=0)
        )

    together = 3
    steps = across * parts

    def top_rows(index, carry):
        found = [top_row(index * together + k) for k in range(together)]
        top_down[...] += sum(found[1:], found[0])
        return carry

    lax.fori_loop(0, steps // together, top_rows, 0)
    for step in range(steps - steps % together, steps):
        top_down[...] += top_row(jnp.int32(step))
    matrix = inverse_ref[...]
    top_local = dot_split_nt(top_down[...], matrix)
    lay_surface(surface, cols_ref)
    down[...] = down_ref[...]
    for a in range(2):
        for b in range(2):
            for e in range(2):
                offset = (a - 0.5, b - 0.5, e - 0.5)
                delta = [
                    offset[axis] + 0.9 * point[axis] - 3.0 * cols_ref[axis] for axis in range(3)
                ]
                table = lax.rsqrt(
                    delta[0] * delta[0] + delta[1] * delta[1] + delta[2] * delta[2] + SMOOTH2
                )
                inherited = dot_split(top_local, table)
                for y in range(half_y):
                    for x in range(half_x):
                        for c in range(3):
                            row = (c * size_x + 2 * x + a) * size_y + 2 * y + b
                            down[row : row + 1, e * LANES : (e + 1) * LANES] += inherited[
                                y * group + x * 4 + c : y * group + x * 4 + c + 1
                            ]
    for e in range(2):
        part = 0.5 * dot_split_nt(down[:, e * LANES : (e + 1) * LANES], matrix)
        local[e] = part.reshape(3, size_x, size_y, LANES)

    level = lax.broadcasted_iota(jnp.int32, (16, LANES), 0) // 3
    kind = lax.broadcasted_iota(jnp.int32, (16, LANES), 0) % 3
    patterns = []
    for half in range(2):
        x = 1.5 * point[0]
        y = 1.5 * point[1]
        z = 1.5 * point[2] + (half - 0.5)
        pattern = jnp.where(level == 0, 1.0, 0.0)
        for power, value in enumerate((x, y, z, x * x + y * y + z * z)):
            value = jnp.broadcast_to(value, (16, LANES))
            pattern = jnp.where(level == power + 1, value, pattern)
        patterns.append(pattern)

    def one_column(index):
        i = index // size_y
        j = index % size_y
        row = [pack_ref[c, i, pl.ds(j, 1), :] for c in range(3)]
        alive = living_ref[i, pl.ds(j, 1), :]
        results = []
        for half in range(2):
            lanes = slice(half * LANES, (half + 1) * LANES)
            place = [row[axis][:, lanes] for axis in range(3)]
            inverse = lax.rsqrt(surface_distance(surface, place))
            high, low = split(inverse * inverse * inverse)
            charge = [
                jnp.broadcast_to(local[half, c, i, pl.ds(j, 1), :], (16, LANES)) for c in range(3)
            ]
            weight = patterns[half] * jnp.where(
                kind == 0, charge[0], jnp.where(kind == 1, charge[1], charge[2])
            )
            total = bdot(two_terms(*split(weight)), jnp.concatenate([high, low], axis=0))
            total = total[:16] + total[16:] + near_ref[index, :, lanes]
            place[2] = place[2] + (half - 0.5)
            living = alive[:, lanes]
            square = (
                place[0] * place[0] + place[1] * place[1] + place[2] * place[2] + SMOOTH2
            )
            potential = (
                square * total[0:3]
                - 2.0
                * (place[0] * total[3:6] + place[1] * total[6:9] + place[2] * total[9:12])
                + total[12:15]
            ) * living
            slopes = [
                (total[3 + 3 * axis : 6 + 3 * axis] - place[axis] * total[0:3]) * living
                for axis in range(3)
            ]
            results.append((potential, slopes))
        potential = jnp.concatenate([results[0][0], results[1][0]], axis=1)
        slopes = [
            jnp.concatenate([results[0][1][axis], results[1][1][axis]], axis=1)
            for axis in range(3)
        ]
        for c in range(3):
            out_ref[c, i, pl.ds(j, 1), :] = potential[c : c + 1]
            for axis in range(3):
                out_ref[3 + 3 * c + axis, i, pl.ds(j, 1), :] = slopes[axis][c : c + 1]

    def columns(index, carry):
        for k in range(8):
            one_column(index * 8 + k)
        return carry

    lax.fori_loop(0, size_x * size_y // 8, columns, 0)


def moved(array, axis, step):
    count = lax.axis_size(axis)
    return lax.ppermute(array, axis, [((i + step) % count, i) for i in range(count)])


def widening(away, axis, count):
    half = 1
    plan = []
    while 2 * half + 1 < count:
        missing = count - 2 * half - 1
        if missing <= 2 * half + 1:
            first = -((missing - 1) // 2)
            steps = (half + 1 - first,)
        else:
            first = -half
            missing = 2 * half + 1
            steps = (missing, -missing)
        picks = []
        known = []
        for places in away:
            pick = [k for k, place in enumerate(places) if 0 <= place[axis] - first < missing]
            picks.append(pick)
            known += [places[k] for k in pick]
        plan.append((steps, picks))
        for step in steps:
            away = away + [
                [tuple(p + step * (k == axis) for k, p in enumerate(place)) for place in known]
            ]
        half = half + steps[0] if len(steps) == 2 else count
    return plan, away


ROUND = [[(x, y) for x in (-1, 0, 1)] for y in (-1, 0, 1)]


def top_slots(lanes_x, lanes_y):
    _, away = widening(ROUND, 1, lanes_y)
    _, away = widening(away, 0, lanes_x)
    slots = np.zeros((lanes_x, lanes_y), np.int32)
    places = [place for held in away for place in held]
    for slot, (x, y) in reversed(list(enumerate(places))):
        slots[x % lanes_x, y % lanes_y] = slot
    return slots


def widened(blocks, away, axis, name):
    plan, final = widening(away, axis, lax.axis_size(name))
    for steps, picks in plan:
        sent = []
        for array, places, pick in zip(blocks, away, picks):
            if len(pick) == len(places):
                sent.append(array)
            else:
                size = array.shape[0] // len(places)
                sent += [array[k * size : (k + 1) * size] for k in pick]
        whole = sent[0] if len(sent) == 1 else jnp.concatenate(sent, axis=0)
        blocks = blocks + [moved(whole, name, step) for step in steps]
        away = final[: len(blocks)]
    return blocks, final


def body(offsets, strengths, counts, check_inverse):
    size_x, size_y, depth = counts.shape
    expansion = check_inverse.shape[0]
    half_x = size_x // 2
    half_y = size_y // 2
    lanes_x = lax.axis_size("gx")
    lanes_y = lax.axis_size("gy")
    tops_x = lanes_x * half_x
    tops_y = lanes_y * half_y
    points = sphere_points(expansion)
    rows = jnp.asarray(np.concatenate([points, np.zeros((5, LANES), np.float32)], axis=0))
    def params(mebibytes):
        return pltpu.CompilerParams(vmem_limit_bytes=mebibytes * 2**20)

    smem = pl.BlockSpec(memory_space=pltpu.SMEM)
    vmem = pl.BlockSpec(memory_space=pltpu.VMEM)

    def cost(flops):
        return pl.CostEstimate(flops=flops, bytes_accessed=10**6, transcendentals=0)

    top_rows = 3 * half_x * half_y
    slot = jnp.arange(LANES)
    living = (slot < counts[:, :, :, None]).astype(F32).reshape(size_x, size_y, depth * LANES)
    pad = LANES - expansion
    matrix = jnp.pad(check_inverse, ((0, pad), (0, pad)))
    (_, _, end_x), (_, near_y, end_y) = parcel_rows(size_x, size_y)
    made = pl.pallas_call(
        functools.partial(up_kernel, size_x, size_y),
        out_shape=(
            jax.ShapeDtypeStruct((6, size_x, size_y, depth * LANES), F32),
            jax.ShapeDtypeStruct((2, 3, size_x, size_y, LANES), F32),
            jax.ShapeDtypeStruct((top_rows, LANES), F32),
            *[jax.ShapeDtypeStruct((end_x, LANES), F32)] * 2,
        ),
        in_specs=[vmem] * 5,
        out_specs=(vmem,) * 5,
        scratch_shapes=[
            pltpu.VMEM((2, 3, size_x, size_y, LANES), F32),
            pltpu.VMEM((4, LANES, LANES), F32),
            pltpu.VMEM((3, LANES, LANES), F32),
        ],
        compiler_params=params(12),
        cost_estimate=cost(6 * 10**9),
        name="up",
    )(living, offsets, strengths, rows, matrix)
    pack, leaf_charges, top_charges, to_below, to_above = made
    below = moved(to_above, "gx", -1)
    above = moved(to_below, "gx", 1)

    table, (own_tasks, *beside) = near_tables(size_x, size_y)
    slots_at = len(table)
    slots = top_slots(lanes_x, lanes_y)
    table = jnp.asarray(np.concatenate([table, slots.reshape(-1)]))
    near_shape = jax.ShapeDtypeStruct((size_x * size_y, 16, 2 * LANES), F32)
    own = pl.pallas_call(
        functools.partial(own_kernel, size_x, size_y, own_tasks),
        out_shape=near_shape,
        in_specs=[smem, vmem],
        out_specs=vmem,
        scratch_shapes=[
            pltpu.VMEM((size_x * size_y, 4, 2 * LANES, LANES), F32),
            pltpu.VMEM((size_x * size_y, 4, 16, 2 * LANES), F32),
        ],
        compiler_params=params(28),
        cost_estimate=cost(3 * 10**10),
        name="own",
    )(table, pack)

    to_low, to_high, tops = pl.pallas_call(
        functools.partial(turn_kernel, size_x, size_y),
        out_shape=(
            jax.ShapeDtypeStruct((end_y, LANES), F32),
            jax.ShapeDtypeStruct((end_y, LANES), F32),
            jax.ShapeDtypeStruct((3 * top_rows, LANES), F32),
        ),
        in_specs=[vmem] * 5,
        out_specs=(vmem,) * 3,
        compiler_params=params(12),
        cost_estimate=cost(10**9),
        name="turn",
    )(leaf_charges, pack, top_charges, below, above)
    low = moved(to_high, "gy", -1)
    high = moved(to_low, "gy", 1)
    blocks, away = widened(
        [low[near_y:], tops, high[near_y:]],
        ROUND,
        1,
        "gy",
    )

    def beside_near(axis, before, parcels):
        tasks = beside[0 if axis == "gx" else 1]
        columns = 2 * (size_y if axis == "gx" else size_x + 2)
        return pl.pallas_call(
            functools.partial(halo_kernel, size_x, size_y, axis, tasks),
            out_shape=near_shape,
            in_specs=[smem] + [vmem] * 4,
            out_specs=vmem,
            scratch_shapes=[
                pltpu.VMEM((columns, 4, 2 * LANES, LANES), F32),
                pltpu.VMEM((columns, 4, 16, 2 * LANES), F32),
                pltpu.VMEM((6, columns, 2 * LANES), F32),
            ],
            compiler_params=params(20),
            cost_estimate=cost(10**10),
            name="beside_" + axis,
        )(table, before, pack, *parcels)

    near = beside_near("gx", own, (below, above))
    blocks, away = widened(blocks, away, 0, "gx")
    blocks = jnp.concatenate(blocks, axis=0).reshape(-1, top_rows, LANES)
    near = beside_near("gy", near, (low, high))

    down = pl.pallas_call(
        functools.partial(leaf_kernel, size_x, size_y),
        out_shape=jax.ShapeDtypeStruct((3 * size_x * size_y, 2 * LANES), F32),
        in_specs=[vmem] * 6,
        out_specs=vmem,
        scratch_shapes=[
            pltpu.VMEM((3, LANES, LANES), F32),
            pltpu.VMEM(
                (2, 3, size_x + 2 * WIDTH, size_y + 2 * WIDTH, LANES), F32
            ),
            pltpu.VMEM((3, LANES, LANES), F32),
        ],
        compiler_params=params(12),
        cost_estimate=cost(6 * 10**9),
        name="leaf",
    )(leaf_charges, rows, below, above, low, high)

    across = tops_x + half_x - 1
    along = tops_y + half_y - 1
    parts = -(-along // 20)
    chunk = -(-along // parts)
    return pl.pallas_call(
        functools.partial(far_kernel, size_x, size_y, tops_x, tops_y, chunk, slots_at),
        out_shape=jax.ShapeDtypeStruct((12, size_x, size_y, depth * LANES), F32),
        in_specs=[smem] + [vmem] * 7,
        out_specs=vmem,
        scratch_shapes=[
            pltpu.VMEM((3, LANES, LANES), F32),
            pltpu.VMEM((across, (parts * chunk + half_y - 1) * half_x * 4, LANES), F32),
            pltpu.VMEM((3 * size_x * size_y, 2 * LANES), F32),
            pltpu.VMEM((half_y * half_x * 4, LANES), F32),
            pltpu.VMEM((2, 3, size_x, size_y, LANES), F32),
            pltpu.VMEM((4, LANES, LANES), F32),
            pltpu.VMEM((parts * chunk, LANES, LANES), F32),
            pltpu.VMEM((3, LANES, LANES), F32),
        ],
        compiler_params=params(40),
        cost_estimate=cost(10**10),
        name="far",
    )(
        table,
        living,
        down,
        blocks,
        near,
        pack,
        rows,
        matrix,
    )


def solution(mesh):
    return jax.shard_map(
        body,
        mesh=mesh,
        in_specs=(P(None, "gx", "gy", None), P(None, "gx", "gy", None), P("gx", "gy", None), P()),
        out_specs=P(None, "gx", "gy", None),
        check_vma=False,
    )
```
